128 devices in a mesh: lon: 8 (over x, y_lo), lat: 16 (over z, y_hi, core).
Axes of the slice: x: 4, y: 4 (y_hi: 2, y_lo: 2; y = y_hi * 2 + y_lo), z: 4, core: 2. Of those that a mesh axis runs over, the one named last changes fastest.
Arguments:
- tokens: bfloat16 [2, 384, 192, 512], P(None, 'lat', 'lon'), may hold values from -6 to 6
- cotangent: bfloat16 [2, 384, 192, 512], P(None, 'lat', 'lon'), may hold values from -6 to 6
- valid: int32 [384, 192], P('lat', 'lon'), may hold values 0 or 1
- w_qkv: bfloat16 [512, 1536], replicated, as said below
- w_out: bfloat16 [512, 512], replicated, may hold values from -0.25 to 0.25
- w_up: bfloat16 [512, 2048], replicated, may hold values from -0.25 to 0.25
- w_down: bfloat16 [2048, 512], replicated, may hold values from -0.125 to 0.125
- gains: float32 [2, 512], replicated, may hold values from 0.1 to 1.9
Outputs:
- outputs: bfloat16 [2, 384, 192, 512], P(None, 'lat', 'lon')
- grad_tokens: bfloat16 [2, 384, 192, 512], P(None, 'lat', 'lon')
- grad_qkv: float32 [512, 1536], replicated
- grad_out: float32 [512, 512], replicated
- grad_up: float32 [512, 2048], replicated
- grad_down: float32 [2048, 512], replicated
- grad_gains: float32 [2, 512], replicated
The draws below stay inside these ranges and needn't reach their ends.
Inputs may be any that keep to these rules, and one draw needn't show every extreme that they name: `w_qkv`: query, key and value columns in this order, heads of 64 side by side.
All inputs are finite; a program needn't handle non-finite values. No bound on the sum of `valid` on one device may be relied on, other than what follows from the above.
Results may differ from the reference program's by a relative error of at most 0.024.
The reference program's roundings to bfloat16 on the way count: a program that leaves them out, or rounds other values in their place, can miss the bound.
Values may be sent and summed in bfloat16 or wider, within the bound.
A program may use at most 192 MiB of HBM per device.

```python
import jax
import jax.numpy as jnp
from jax import lax

D = 512
FF = 2048
HEAD_SIZE = 64
DEPTH = 2
WLAT = 12
WLON = 6
LAT_DEV = 24
NLAT = 384
NLON = 192


def draw_w_qkv(key, part):
    key = jax.random.fold_in(key, 17)
    base = jax.random.normal(key, (D, 3 * D), jnp.float32) * D ** (-0.5)
    return base.astype(jnp.bfloat16)


def touch_ends(entries, stream_key, low, largest):
    longest = entries.shape.index(max(entries.shape))
    spots = []
    for shift in (0, 1):
        where = [jax.random.randint(jax.random.fold_in(stream_key, axis), (), 0, length) for axis, length in enumerate(entries.shape)]
        where[longest] = (where[longest] + shift) % entries.shape[longest]
        spots.append(tuple(where))
    return entries.at[spots[0]].set(low).at[spots[1]].set(largest)


def shard_levels(stream_key, extent, cuts, least, largest):
    def one(axis_at, parts):
        heights = jax.random.uniform(jax.random.fold_in(jax.random.fold_in(stream_key, 6), axis_at), (parts,), jnp.float32, least / len(cuts), largest / len(cuts))
        return jnp.repeat(jnp.exp(heights), extent[axis_at] // parts).reshape((-1,) + (1,) * (len(extent) - axis_at - 1))

    level = one(*cuts[0])
    for cut in cuts[1:]:
        level = level * one(*cut)
    return level


def normal_values(own_key, dims, deviation, limit, cuts=(), held_as=jnp.bfloat16):
    factor_of = shard_levels(own_key, dims, cuts, -0.22, 0.18) if cuts else 1.0
    entries = jax.random.normal(own_key, dims, jnp.float32) * deviation * factor_of
    return jnp.minimum(jnp.maximum(entries, -limit), limit).astype(held_as)


def setup_inputs(seed: int = 0) -> dict:
    key_list = jax.random.split(jax.random.key(seed), 9)
    tokens = normal_values(key_list[0], (DEPTH, NLAT, NLON, D), 1.0, 6.0, ((1, 16), (2, 8)))
    cotangent = normal_values(key_list[1], (DEPTH, NLAT, NLON, D), 1.0, 6.0, ((1, 16), (2, 8)))
    valid = touch_ends((jax.random.randint(key_list[2], (NLAT, NLON), 0, 8) < 7).astype(jnp.int32), jax.random.fold_in(key_list[2], 1), 0, 1)
    w_qkv = draw_w_qkv(jax.random.fold_in(key_list[8], 71), 0)
    w_out = normal_values(key_list[4], (D, D), D ** -0.5, 0.25)
    w_up = normal_values(key_list[5], (D, FF), D ** -0.5, 0.25)
    w_down = normal_values(key_list[6], (FF, D), FF ** -0.5, 0.125)
    gains = jnp.clip(1.0 + 0.18 * jax.random.normal(key_list[7], (2, D), jnp.float32), 0.1, 1.9)
    return {"tokens": tokens, "cotangent": cotangent, "valid": valid, "w_qkv": w_qkv, "w_out": w_out, "w_up": w_up, "w_down": w_down, "gains": gains}


epsilon = 1e-05

def normalize(values, gain_row):
    centre = lax.optimization_barrier(jnp.mean(values, -1, keepdims=True))
    centred = values - centre
    inv_std = lax.rsqrt(lax.optimization_barrier(jnp.mean(centred * centred, -1, keepdims=True)) + epsilon)
    normed = centred * inv_std
    return (normed, inv_std, normed * gain_row)

def norm_back(grad_value, normed, inv_std, gain_row):
    scaled = grad_value * gain_row
    return inv_std * (scaled - lax.optimization_barrier(jnp.mean(scaled, -1, keepdims=True)) - normed * lax.optimization_barrier(jnp.mean(scaled * normed, -1, keepdims=True)))

def to_windows(field):
    levels, lat_rows, lon_cols, channels = field.shape
    shaped = field.reshape(levels, lat_rows // WLAT, WLAT, lon_cols // WLON, WLON, channels)
    return shaped.transpose(1, 3, 0, 2, 4, 5).reshape(-1, levels * WLAT * WLON, channels)

def from_windows(windows, levels, lat_rows, lon_cols):
    channels = windows.shape[-1]
    shaped = windows.reshape(lat_rows // WLAT, lon_cols // WLON, levels, WLAT, WLON, channels)
    return shaped.transpose(2, 0, 3, 1, 4, 5).reshape(levels, lat_rows, lon_cols, channels)

def window_mask(valid_part, first_row, total_rows, levels):
    lat_rows, lon_cols = valid_part.shape
    row_ids = first_row + jnp.arange(lat_rows, dtype=jnp.int32)
    region = (row_ids >= total_rows - WLAT).astype(jnp.int32) + (row_ids >= total_rows - WLAT // 2).astype(jnp.int32)
    region = jnp.broadcast_to(region[None, :, None, None], (levels, lat_rows, lon_cols, 1))
    usable = jnp.broadcast_to(valid_part[None, :, :, None], (levels, lat_rows, lon_cols, 1))
    region = to_windows(region)[..., 0]
    usable = to_windows(usable)[..., 0]
    win_size = region.shape[1]
    itself = jnp.arange(win_size, dtype=jnp.int32)[:, None] == jnp.arange(win_size, dtype=jnp.int32)[None, :]
    return (region[:, :, None] == region[:, None, :]) & ((usable[:, None, :] == 1) | itself[None])

def attend(shifted, allowed, w_qkv, w_out):
    levels, lat_rows, lon_cols, channels = shifted.shape
    head_count = channels // HEAD_SIZE
    windows = to_windows(shifted)
    win_count, win_size = (windows.shape[0], windows.shape[1])
    flat_rows = windows.reshape(win_count * win_size, channels)
    packed = jnp.dot(flat_rows, w_qkv, preferred_element_type=jnp.float32).astype(jnp.bfloat16)
    packed = packed.reshape(win_count, win_size, 3, head_count, HEAD_SIZE)
    query_part = packed[:, :, 0]
    key_part = packed[:, :, 1]
    value_part = packed[:, :, 2]
    scores = jnp.einsum('wqhd,wkhd->whqk', query_part.astype(jnp.float32), key_part.astype(jnp.float32)) * HEAD_SIZE ** (-0.5)
    scores = jnp.where(allowed[:, None], scores, -1e+30)
    softmax_out = jax.nn.softmax(scores, axis=-1)
    weights = softmax_out.astype(jnp.bfloat16)
    context = jnp.einsum('whqk,wkhd->wqhd', weights.astype(jnp.float32), value_part.astype(jnp.float32))
    context = context.astype(jnp.bfloat16).reshape(win_count * win_size, channels)
    result = jnp.dot(context, w_out, preferred_element_type=jnp.float32).astype(jnp.bfloat16)
    saved = (flat_rows, query_part, key_part, value_part, softmax_out, weights, context)
    return (from_windows(result.reshape(win_count, win_size, channels), levels, lat_rows, lon_cols), saved)

def attend_back(grad_field, saved, w_qkv, w_out):
    flat_rows, query_part, key_part, value_part, softmax_out, weights, context = saved
    levels, lat_rows, lon_cols, channels = grad_field.shape
    win_count, win_size = (query_part.shape[0], query_part.shape[1])
    grad_flat = to_windows(grad_field).reshape(win_count * win_size, channels)
    grad_context = jnp.dot(grad_flat, w_out.T, preferred_element_type=jnp.float32).astype(jnp.bfloat16)
    grad_context = grad_context.reshape(query_part.shape).astype(jnp.float32)
    grad_weights = jnp.einsum('wqhd,wkhd->whqk', grad_context, value_part.astype(jnp.float32))
    grad_value = jnp.einsum('whqk,wqhd->wkhd', weights.astype(jnp.float32), grad_context).astype(jnp.bfloat16)
    inner = lax.optimization_barrier(jnp.sum(softmax_out * grad_weights, -1, keepdims=True))
    grad_scores = (softmax_out * (grad_weights - inner) * HEAD_SIZE ** (-0.5)).astype(jnp.bfloat16).astype(jnp.float32)
    grad_query = jnp.einsum('whqk,wkhd->wqhd', grad_scores, key_part.astype(jnp.float32)).astype(jnp.bfloat16)
    grad_key = jnp.einsum('whqk,wqhd->wkhd', grad_scores, query_part.astype(jnp.float32)).astype(jnp.bfloat16)
    grad_packed = jnp.stack([grad_query, grad_key, grad_value], axis=2).reshape(win_count * win_size, 3 * channels)
    grad_shift = jnp.dot(grad_packed, w_qkv.T, preferred_element_type=jnp.float32).astype(jnp.bfloat16)
    grad_shift = from_windows(grad_shift.reshape(win_count, win_size, channels), levels, lat_rows, lon_cols)
    return (grad_shift, (flat_rows, grad_packed), (context, grad_flat))

def feed_forward(mixed, cotangent, gain_row, w_up, w_down):
    channels = mixed.shape[-1]
    mixed_rows = mixed.reshape(-1, channels)
    normed, inv_std, scaled = normalize(mixed_rows, gain_row)
    hidden_in = scaled.astype(jnp.bfloat16)
    raised = jnp.dot(hidden_in, w_up, preferred_element_type=jnp.float32)
    activated = jax.nn.gelu(raised).astype(jnp.bfloat16)
    result = (mixed_rows + jnp.dot(activated, w_down, preferred_element_type=jnp.float32)).astype(jnp.bfloat16)
    grad_rows = cotangent.reshape(-1, channels)
    grad_act = jnp.dot(grad_rows, w_down.T, preferred_element_type=jnp.float32)
    grad_raised = jax.vjp(jax.nn.gelu, raised)[1](grad_act)[0].astype(jnp.bfloat16)
    grad_in = jnp.dot(grad_raised, w_up.T, preferred_element_type=jnp.float32)
    gain_grad = lax.optimization_barrier(jnp.sum(grad_in * normed, 0))
    grad_mixed = grad_rows.astype(jnp.float32) + norm_back(grad_in, normed, inv_std, gain_row)
    return (result.reshape(mixed.shape), grad_mixed.reshape(mixed.shape), gain_grad, (hidden_in, grad_raised), (activated, grad_rows))

def banded(field):
    levels, lat_rows, lon_cols, channels = field.shape
    return field.reshape(levels, lat_rows // LAT_DEV, LAT_DEV, lon_cols, channels).transpose(1, 0, 2, 3, 4)

def unbanded(bands):
    band_count, levels, lat_rows, lon_cols, channels = bands.shape
    return bands.transpose(1, 0, 2, 3, 4).reshape(levels, band_count * lat_rows, lon_cols, channels)

def outer_sum(left_part, right_part):
    return jnp.dot(left_part.T, right_part, preferred_element_type=jnp.float32)

def reference(tokens, cotangent, valid, w_qkv, w_out, w_up, w_down, gains):
    levels, lat_rows, lon_cols, channels = tokens.shape
    half_lat = WLAT // 2
    half_lon = WLON // 2
    tokens_wide = tokens.astype(jnp.float32)
    normed1, inv_std1, scaled1 = normalize(tokens_wide, gains[0])
    lowered = scaled1.astype(jnp.bfloat16)
    shifted = jnp.roll(lowered, (-half_lat, -half_lon), axis=(1, 2))
    band_count = lat_rows // LAT_DEV
    valid_bands = valid.reshape(band_count, LAT_DEV, lon_cols)
    band_starts = jnp.arange(band_count, dtype=jnp.int32) * LAT_DEV

    def forward_band(pieces):
        band_rows, usable, first_row = pieces
        allowed = window_mask(usable, first_row, lat_rows, levels)
        result, saved = attend(band_rows, allowed, w_qkv, w_out)
        return result
    attended = unbanded(lax.map(forward_band, (banded(shifted), valid_bands, band_starts)))
    mixed = tokens_wide + jnp.roll(attended, (half_lat, half_lon), axis=(1, 2)).astype(jnp.float32)

    def mlp_band(pieces):
        band_rows, band_cot = pieces
        result, grad_mixed, gain_grad, up_pair, down_pair = feed_forward(band_rows, band_cot, gains[1], w_up, w_down)
        return (result, grad_mixed, gain_grad, outer_sum(*up_pair), outer_sum(*down_pair))
    outputs, grad_mixed, gain_two, up_grads, down_grads = lax.map(mlp_band, (banded(mixed), banded(cotangent)))
    outputs = unbanded(outputs)
    grad_mixed = unbanded(grad_mixed)
    grad_attended = jnp.roll(grad_mixed.astype(jnp.bfloat16), (-half_lat, -half_lon), axis=(1, 2))

    def backward_band(pieces):
        band_rows, usable, first_row, band_grad = pieces
        allowed = window_mask(usable, first_row, lat_rows, levels)
        result, saved = attend(band_rows, allowed, w_qkv, w_out)
        grad_shift, qkv_pair, out_pair = attend_back(band_grad, saved, w_qkv, w_out)
        return (grad_shift, outer_sum(*qkv_pair), outer_sum(*out_pair))
    grad_shifted, qkv_grads, out_grads = lax.map(backward_band, (banded(shifted), valid_bands, band_starts, banded(grad_attended)))
    grad_lowered = jnp.roll(unbanded(grad_shifted), (half_lat, half_lon), axis=(1, 2)).astype(jnp.float32)
    gain_one = lax.optimization_barrier(jnp.sum(grad_lowered * normed1, axis=(0, 1, 2)))
    grad_tokens = (grad_mixed + norm_back(grad_lowered, normed1, inv_std1, gains[0])).astype(jnp.bfloat16)
    grad_scale = (levels * lat_rows * lon_cols) ** (-0.5)
    grad_gains = jnp.stack([gain_one, lax.optimization_barrier(jnp.sum(gain_two, 0))]) * grad_scale
    return (outputs, grad_tokens, lax.optimization_barrier(jnp.sum(qkv_grads, 0)) * grad_scale, lax.optimization_barrier(jnp.sum(out_grads, 0)) * grad_scale, lax.optimization_barrier(jnp.sum(up_grads, 0)) * grad_scale, lax.optimization_barrier(jnp.sum(down_grads, 0)) * grad_scale, grad_gains)
```

```python
import functools

import jax
import jax.numpy as jnp
import numpy as np
from jax import lax
from jax.experimental import pallas as pl
from jax.experimental.pallas import tpu as pltpu
from jax.sharding import PartitionSpec as P

F32 = jnp.float32
BF16 = jnp.bfloat16
MESH = pl.DeviceIdType.MESH
HEAD = 64
WIN = 144
TOK = 1152
HALF = 576
D = 512
FF = 2048
COLS = 24
BLOCK = 144
PIECE = 48
epsilon = 1e-05
LOW = -1e30
ONE_WAY = 8
VMEM_BYTES = 60 * 1024 * 1024


def gather_maps():
    into = np.zeros((HALF, HALF + 2 * PIECE), np.float32)
    back = np.zeros((HALF, HALF + 2 * PIECE), np.float32)
    rim_in = np.zeros((4 * PIECE, TOK), np.float32)
    rim_back = np.zeros((2 * PIECE, HALF), np.float32)
    for lev in range(2):
        for half in range(2):
            for r in range(6):
                for col in range(COLS):
                    window = (col // 6) * WIN + lev * 72 + half * 36 + r * 6 + col % 6
                    chunk = (lev * 2 + half) * BLOCK + r * COLS
                    if col + 3 < COLS:
                        into[window, chunk + col + 3] = 1
                        back[chunk + col + 3, window] = 1
                    else:
                        rim = half * PIECE + lev * 18 + r * 3 + col + 3 - COLS
                        into[window, HALF + rim] = 1
                        back[chunk + col + 3 - COLS, HALF + rim] = 1
                        rim_back[rim, window] = 1
    for lev in range(2):
        for block in range(4):
            for r in range(6):
                for col in range(3):
                    rim_in[block * PIECE + lev * 18 + r * 3 + col, lev * HALF + block * BLOCK + r * COLS + col] = 1
    return [jnp.asarray(m, BF16) for m in (into, back, rim_in, rim_back)]


def mm(a, b):
    return lax.dot_general(a, b, (((1,), (0,)), ((), ())), preferred_element_type=F32)


def mm_nt(a, b):
    return lax.dot_general(a, b, (((1,), (1,)), ((), ())), preferred_element_type=F32)


def mm_tn(a, b):
    return lax.dot_general(a, b, (((0,), (0,)), ((), ())), preferred_element_type=F32)


def norm_stats(values):
    centred = values - jnp.mean(values, -1, keepdims=True)
    inv_std = lax.rsqrt(jnp.mean(centred * centred, -1, keepdims=True) + epsilon)
    return centred * inv_std, inv_std


def norm_back(grad_value, normed, inv_std, gain_row):
    scaled = grad_value * gain_row
    return inv_std * (
        scaled
        - jnp.mean(scaled, -1, keepdims=True)
        - normed * jnp.mean(scaled * normed, -1, keepdims=True)
    )


def rows_loop(total, step, body):
    def run(i, carry):
        body(pl.ds(pl.multiple_of(i * step, step), step))
        return carry

    lax.fori_loop(0, total // step, run, 0)


def halo_kernel(tok, cot, rim_map, lat_t, lat_c, rim_t, rim_c, pack_t, pack_c, send, recv):
    lon, lat = lax.axis_index("lon"), lax.axis_index("lat")
    n_lon, n_lat = lax.axis_size("lon"), lax.axis_size("lat")
    lon_m, lon_p = lax.rem(lon + n_lon - 1, n_lon), lax.rem(lon + 1, n_lon)
    lat_m, lat_p = lax.rem(lat + n_lat - 1, n_lat), lax.rem(lat + 1, n_lat)
    barrier = pltpu.get_barrier_semaphore()
    for peer in ((lon, lat_m), (lon, lat_p), (lon_m, lat), (lon_p, lat), (lon_m, lat_m), (lon_p, lat_p)):
        pl.semaphore_signal(barrier, inc=1, device_id=peer, device_id_type=MESH)
    pack_t[...] = mm(rim_map[...], tok[...]).astype(BF16)
    pack_c[...] = mm(rim_map[...], cot[...]).astype(BF16)
    pl.semaphore_wait(barrier, 6)
    copies = []

    def push(src, dst, peer):
        k = len(copies)
        copy = pltpu.make_async_remote_copy(
            src_ref=src, dst_ref=dst, send_sem=send.at[k], recv_sem=recv.at[k], device_id=peer, device_id_type=MESH
        )
        copy.start()
        copies.append(copy)

    for pack, rim, lat_rim, src in ((pack_t, rim_t, lat_t, tok), (pack_c, rim_c, lat_c, cot)):
        rest = pl.ds(PIECE, 3 * PIECE)
        push(pack.at[rest], rim.at[rest], (lon_m, lat))
        push(pack.at[pl.ds(0, PIECE)], rim.at[pl.ds(0, PIECE)], (lon_m, lat_m))
        for lev in range(2):
            push(src.at[pl.ds(lev * HALF, BLOCK)], lat_rim.at[pl.ds(lev * BLOCK, BLOCK)], (lon, lat_m))
    for copy in copies:
        copy.wait()


def halo(tok, cot, rim_map):
    vm = pl.BlockSpec(memory_space=pltpu.VMEM)
    rim = jax.ShapeDtypeStruct((4 * PIECE, D), BF16)
    lat_rim = jax.ShapeDtypeStruct((2 * BLOCK, D), BF16)
    return pl.pallas_call(
        halo_kernel,
        out_shape=(lat_rim, lat_rim, rim, rim),
        in_specs=[vm] * 3,
        out_specs=(vm,) * 4,
        scratch_shapes=[
            pltpu.VMEM((4 * PIECE, D), BF16),
            pltpu.VMEM((4 * PIECE, D), BF16),
            pltpu.SemaphoreType.DMA((8,)),
            pltpu.SemaphoreType.DMA((8,)),
        ],
        compiler_params=pltpu.CompilerParams(collective_id=0, has_side_effects=True, vmem_limit_bytes=VMEM_BYTES),
        name="halo_in",
    )(tok, cot, rim_map)


def window_bias(key_bias, split):
    rows = lax.broadcasted_iota(jnp.int32, (WIN, WIN), 0)
    cols = lax.broadcasted_iota(jnp.int32, (WIN, WIN), 1)
    bias = jnp.where(rows == cols, 0.0, jnp.broadcast_to(key_bias, (WIN, WIN)))
    apart = ((rows // 36) % 2) != ((cols // 36) % 2)
    return bias + jnp.where(apart, split, 0.0)


def scores_t(key2, query_m, bias):
    s = mm_nt(key2, query_m) * HEAD ** (-0.5) + bias
    e = jnp.exp(s - jnp.max(s, 0, keepdims=True))
    return e * (1.0 / jnp.sum(e, 0, keepdims=True))


def head_masks():
    lane = lax.broadcasted_iota(jnp.int32, (WIN, 128), 1)
    return [lane < HEAD, lane >= HEAD]


def split_amount(window):
    last = (lax.axis_index("lat") == lax.axis_size("lat") - 1) & (window >= 4)
    return jnp.where(last, LOW, 0.0).astype(F32)


def forward_kernel(
    tok, cot, lat_t, lat_c, rim_t, rim_c, into, key_bias, w_qkv, w_out, w_up, w_down, gains,
    x_ref, packed, lowered, context, out_win, gmix, grads, gain2,
    src, c_ref, mixed, hid, hid_t, c_t, acc_out, acc_in,
):
    gain_a = gains[0:1, :]
    gain_b = gains[1:2, :]
    for full, lat_rim, rim, dst in ((tok, lat_t, rim_t, x_ref), (cot, lat_c, rim_c, c_ref)):
        for wr in range(2):
            for lev in range(2):
                if wr == 0:
                    src[lev * 288:(lev + 1) * 288, :] = full[lev * HALF + 144:lev * HALF + 432, :]
                else:
                    src[lev * 288:lev * 288 + 144, :] = full[lev * HALF + 432:lev * HALF + 576, :]
                    src[lev * 288 + 144:(lev + 1) * 288, :] = lat_rim[lev * BLOCK:(lev + 1) * BLOCK, :]
            if wr == 0:
                src[HALF:, :] = rim[PIECE:3 * PIECE, :]
            else:
                src[HALF:HALF + PIECE, :] = rim[3 * PIECE:, :]
                src[HALF + PIECE:, :] = rim[:PIECE, :]
            for n in range(2):
                cols = slice(n * 256, (n + 1) * 256)
                dst[wr * HALF:(wr + 1) * HALF, cols] = mm(into[...], src[:, cols]).astype(BF16)

    def first_norm(rows):
        normed, _ = norm_stats(x_ref[rows, :].astype(F32))
        lowered[rows, :] = (normed * gain_a).astype(BF16)

    rows_loop(TOK, WIN, first_norm)

    def project(n, carry):
        cols = pl.ds(pl.multiple_of(n * 256, 256), 256)
        packed[:, cols] = mm(lowered[...], w_qkv[:, cols]).astype(BF16)
        return carry

    lax.fori_loop(0, 6, project, 0)
    masks = head_masks()

    def attend(w, carry):
        rows = pl.ds(pl.multiple_of(w * WIN, WIN), WIN)
        bias = window_bias(key_bias[rows, :], split_amount(w))
        for pair in range(4):
            lanes = slice(pair * 128, (pair + 1) * 128)
            query = packed[rows, lanes]
            key = packed[rows, D + pair * 128:D + (pair + 1) * 128]
            value = packed[rows, 2 * D + pair * 128:2 * D + (pair + 1) * 128]
            total = None
            for mask in masks:
                probs = scores_t(key, jnp.where(mask, query, 0), bias)
                part = mm_tn(probs.astype(BF16), jnp.where(mask, value, 0))
                total = part if total is None else total + part
            context[rows, lanes] = total.astype(BF16)
        return carry

    lax.fori_loop(0, 8, attend, 0)

    def second_norm(rows):
        attended = mm(context[rows, :], w_out[...]).astype(BF16)
        m = x_ref[rows, :].astype(F32) + attended.astype(F32)
        mixed[rows, :] = m
        normed, _ = norm_stats(m)
        hid[rows, :] = (normed * gain_b).astype(BF16)

    rows_loop(TOK, 288, second_norm)
    hid_t[...] = hid[...].T
    c_t[...] = c_ref[...].T
    acc_out[...] = jnp.zeros_like(acc_out)
    acc_in[...] = jnp.zeros_like(acc_in)
    wide = 256

    def columns(n, carry):
        cols = pl.ds(pl.multiple_of(n * wide, wide), wide)
        raised = mm(hid[...], w_up[:, cols])
        slope = np.float32(np.sqrt(2 / np.pi))
        square = raised * raised
        t = jnp.tanh(slope * (raised + np.float32(0.044715) * (square * raised)))
        cdf = 0.5 * (1.0 + t)
        activated = (raised * cdf).astype(BF16)
        deriv = cdf + 0.5 * raised * (1.0 - t * t) * (slope * (1.0 + np.float32(3 * 0.044715) * square))
        grad_act = mm_nt(c_ref[...], w_down[cols, :])
        grad_raised = (grad_act * deriv).astype(BF16)
        acc_out[...] += mm(activated, w_down[cols, :])
        acc_in[...] += mm_nt(grad_raised, w_up[:, cols])
        half = pl.ds(pl.multiple_of(lax.rem(n, 2) * wide, wide), wide)
        up_rows = pl.ds(pl.multiple_of((n // 2) * 512, 512), 512)
        grads[up_rows, half] = mm(hid_t[...], grad_raised)
        down_rows = pl.ds(pl.multiple_of(FF + n * wide, wide), wide)
        grads[down_rows, :] = mm(c_t[...], activated).T
        return carry

    lax.fori_loop(0, FF // wide, columns, 0)
    gain2[...] = jnp.zeros_like(gain2)

    def finish(rows):
        m = mixed[rows, :]
        out_win[rows, :] = (m + acc_out[rows, :]).astype(BF16)
        normed, inv_std = norm_stats(m)
        grad_in = acc_in[rows, :]
        gain2[0:1, :] += jnp.sum(grad_in * normed, 0, keepdims=True)
        gmix[rows, :] = c_ref[rows, :].astype(F32) + norm_back(grad_in, normed, inv_std, gain_b)

    rows_loop(TOK, WIN, finish)


def forward(*args):
    vm = pl.BlockSpec(memory_space=pltpu.VMEM)
    shape = jax.ShapeDtypeStruct
    return pl.pallas_call(
        forward_kernel,
        out_shape=(
            shape((TOK, D), BF16),
            shape((TOK, 3 * D), BF16),
            shape((TOK, D), BF16),
            shape((TOK, D), BF16),
            shape((TOK, D), BF16),
            shape((TOK, D), F32),
            shape((2 * FF, D), F32),
            shape((8, D), F32),
        ),
        in_specs=[vm] * len(args),
        out_specs=(vm,) * 8,
        scratch_shapes=[
            pltpu.VMEM((HALF + 2 * PIECE, D), BF16),
            pltpu.VMEM((TOK, D), BF16),
            pltpu.VMEM((TOK, D), F32),
            pltpu.VMEM((TOK, D), BF16),
            pltpu.VMEM((D, TOK), BF16),
            pltpu.VMEM((D, TOK), BF16),
            pltpu.VMEM((TOK, D), F32),
            pltpu.VMEM((TOK, D), F32),
        ],
        compiler_params=pltpu.CompilerParams(vmem_limit_bytes=VMEM_BYTES),
        name="forward",
    )(*args)


def backward_kernel(
    x_ref, packed, lowered, context, out_win, gmix, key_bias, w_qkv, w_out, gains, rim_back,
    grads, gtok_win, gain1, rims,
    g_att, g_ctx, g_pack, low_t, ctx_t,
):
    gain_a = gains[0:1, :]

    def start(rows):
        g_att[rows, :] = gmix[rows, :].astype(BF16)
        g_ctx[rows, :] = mm_nt(g_att[rows, :], w_out[...]).astype(BF16)

    rows_loop(TOK, 288, start)
    masks = head_masks()

    def attend(w, carry):
        rows = pl.ds(pl.multiple_of(w * WIN, WIN), WIN)
        bias = window_bias(key_bias[rows, :], split_amount(w))
        for pair in range(4):
            lanes = slice(pair * 128, (pair + 1) * 128)
            key_lanes = slice(D + pair * 128, D + (pair + 1) * 128)
            value_lanes = slice(2 * D + pair * 128, 2 * D + (pair + 1) * 128)
            query = packed[rows, lanes]
            key = packed[rows, key_lanes]
            value = packed[rows, value_lanes]
            grad = g_ctx[rows, lanes]
            sums = [None, None, None]
            for mask in masks:
                query_m = jnp.where(mask, query, 0)
                grad_m = jnp.where(mask, grad, 0)
                probs = scores_t(key, query_m, bias)
                g_weights = mm_nt(value, grad_m)
                inner = jnp.sum(probs * g_weights, 0, keepdims=True)
                g_scores = (probs * (g_weights - inner) * HEAD ** (-0.5)).astype(BF16)
                parts = (
                    mm_tn(g_scores, jnp.where(mask, key, 0)),
                    mm(g_scores, query_m),
                    mm(probs.astype(BF16), grad_m),
                )
                sums = [b if a is None else a + b for a, b in zip(sums, parts)]
            g_pack[rows, lanes] = sums[0].astype(BF16)
            g_pack[rows, key_lanes] = sums[1].astype(BF16)
            g_pack[rows, value_lanes] = sums[2].astype(BF16)
        return carry

    lax.fori_loop(0, 8, attend, 0)
    low_t[...] = lowered[...].T
    ctx_t[...] = context[...].T

    def weight(n, carry):
        cols = pl.ds(pl.multiple_of(n * 256, 256), 256)
        half = pl.ds(pl.multiple_of(lax.rem(n, 2) * 256, 256), 256)
        grads[pl.ds(pl.multiple_of((n // 2) * 512, 512), 512), half] = mm(low_t[...], g_pack[:, cols])
        return carry

    lax.fori_loop(0, 6, weight, 0)
    for n in range(2):
        cols = slice(n * 256, (n + 1) * 256)
        grads[3 * D:, cols] = mm(ctx_t[...], g_att[:, cols])
    gain1[...] = jnp.zeros_like(gain1)

    def finish(rows):
        g_low = mm_nt(g_pack[rows, :], w_qkv[...]).astype(BF16).astype(F32)
        normed, inv_std = norm_stats(x_ref[rows, :].astype(F32))
        gain1[0:1, :] += jnp.sum(g_low * normed, 0, keepdims=True)
        gtok_win[rows, :] = (gmix[rows, :] + norm_back(g_low, normed, inv_std, gain_a)).astype(BF16)

    rows_loop(TOK, 288, finish)
    for k, win in enumerate((out_win, gtok_win)):
        for wr in range(2):
            at = (k * 2 + wr) * 2 * PIECE
            rims[at:at + 2 * PIECE, :] = mm(rim_back[...], win[wr * HALF:(wr + 1) * HALF, :]).astype(BF16)


def backward(*args):
    vm = pl.BlockSpec(memory_space=pltpu.VMEM)
    shape = jax.ShapeDtypeStruct
    return pl.pallas_call(
        backward_kernel,
        out_shape=(shape((4 * D, D), F32), shape((TOK, D), BF16), shape((8, D), F32), shape((8 * PIECE, D), BF16)),
        in_specs=[vm] * len(args),
        out_specs=(vm,) * 4,
        scratch_shapes=[
            pltpu.VMEM((TOK, D), BF16),
            pltpu.VMEM((TOK, D), BF16),
            pltpu.VMEM((TOK, 3 * D), BF16),
            pltpu.VMEM((D, TOK), BF16),
            pltpu.VMEM((D, TOK), BF16),
        ],
        compiler_params=pltpu.CompilerParams(vmem_limit_bytes=VMEM_BYTES),
        name="backward",
    )(*args)


ORDERS = ((0, 1, 2), (1, 2, 0), (2, 0, 1))
PART = 1024


def position():
    lon, lat = lax.axis_index("lon"), lax.axis_index("lat")
    y = lax.rem(lax.div(lat, 2), 2) * 2 + lax.rem(lon, 2)
    return [lax.div(lon, 2), y, lax.div(lat, 4)], lax.rem(lat, 2)


def device_at(place, core):
    x, y, z = place
    return (x * 2 + lax.rem(y, 2), z * 4 + lax.div(y, 2) * 2 + core)


def sum_kernel(
    g1, g2, gain1, gain2, rims, out_win, gtok_win, back,
    r1, r2, gains_out, lon_rims, lat_blocks,
    own, other, out_send, pair_recv, send1, recv1, sum1, recv2, sum2, recv3, send_blocks,
    gain_slots, load_sem, pair_s, pair_r, rs_s, rs_r, ag_s, ag_r, halo_s, halo_r, gain_s, gain_r,
):
    place, core = position()
    lon, lat = lax.axis_index("lon"), lax.axis_index("lat")
    n_lon, n_lat = lax.axis_size("lon"), lax.axis_size("lat")
    lon_m, lon_p = lax.rem(lon + n_lon - 1, n_lon), lax.rem(lon + 1, n_lon)
    lat_m, lat_p = lax.rem(lat + n_lat - 1, n_lat), lax.rem(lat + 1, n_lat)
    partner = device_at(place, 1 - core)

    def peer(axis, step):
        there = list(place)
        there[axis] = lax.rem(place[axis] + step, 4)
        return device_at(there, core), there[axis]

    barrier = pltpu.get_barrier_semaphore()
    greet = [partner, (lon_m, lat), (lon_p, lat), (lon, lat_m), (lon, lat_p)]
    greet += [peer(axis, step)[0] for axis in range(3) for step in (1, 2, 3)]
    for device in greet:
        pl.semaphore_signal(barrier, inc=1, device_id=device, device_id_type=MESH)

    def part_rows(which, part):
        return pl.ds(pl.multiple_of(which * 2048 + part * PART, PART), PART) if part < 2 else pl.ds(
            pl.multiple_of(which * PART, PART), PART
        )

    def source(part):
        return g1 if part < 2 else g2

    def result(part):
        return r1 if part < 2 else r2

    loads = []
    for part in range(3):
        for k, (which, dst) in enumerate(((1 - core, other), (core, own))):
            copy = pltpu.make_async_copy(source(part).at[part_rows(which, part)], dst.at[part], load_sem.at[part, k])
            copy.start()
            loads.append(copy)

    def remote(src, dst, s, r, device):
        copy = pltpu.make_async_remote_copy(
            src_ref=src, dst_ref=dst, send_sem=s, recv_sem=r, device_id=device, device_id_type=MESH
        )
        copy.start()
        return copy

    pl.semaphore_wait(barrier, len(greet))
    waits = []
    halo1 = remote(rims, lon_rims, halo_s.at[0], halo_r.at[0], (lon_p, lat))
    gain_slots[0, 0, 0:1, :] = gain1[0:1, :]
    gain_slots[0, 0, 1:2, :] = gain2[0:1, :]
    gain_slots[0, 0, 2:8, :] = jnp.zeros((6, D), F32)
    gain_pair = remote(gain_slots.at[0, 0], gain_slots.at[0, 1], gain_s.at[0, 0], gain_r.at[0, 0], partner)

    pairs = []
    for part in range(3):
        loads[2 * part].wait()

        def lower(rows, part=part):
            out_send[part, rows, :] = other[part, rows, :].astype(BF16)

        rows_loop(PART, 128, lower)
        pairs.append(
            remote(out_send.at[part], pair_recv.at[part], pair_s.at[part], pair_r.at[part], partner)
        )

    stage1 = []
    for part in range(3):
        loads[2 * part + 1].wait()
        pairs[part].wait_recv()
        axis = ORDERS[part][0]

        def add(rows, part=part):
            own[part, rows, :] += pair_recv[part, rows, :].astype(F32)

        rows_loop(PART, 128, add)
        for step in (1, 2, 3):
            device, at = peer(axis, step)
            rows = pl.ds(pl.multiple_of(at * 256, 256), 256)
            send1[part, step - 1] = own[part, rows, :].astype(BF16)
            stage1.append(
                remote(send1.at[part, step - 1], recv1.at[part, step - 1],
                       rs_s.at[0, part, step - 1], rs_r.at[0, part, step - 1], device)
            )
    gain_pair.wait()
    gain_total = gain_slots[0, 0] + gain_slots[0, 1]

    def gains_along(level, total):
        axis = level - 1
        mine = place[axis]
        gain_slots[level, mine] = total
        copies = []
        for step in (1, 2, 3):
            device, _ = peer(axis, step)
            copies.append(
                remote(gain_slots.at[level, mine], gain_slots.at[level, mine],
                       gain_s.at[level, step - 1], gain_r.at[level, step - 1], device)
            )
        return copies

    def gains_sum(level, copies):
        for copy in copies:
            copy.wait()
        return (gain_slots[level, 0] + gain_slots[level, 1]) + (gain_slots[level, 2] + gain_slots[level, 3])

    gain_copies = gains_along(1, gain_total)

    halo1.wait()
    for k, win in enumerate((out_win, gtok_win)):
        at = (k * 2 + 1) * 2 * PIECE
        for lev in range(2):
            pick = slice((lev * 2 + 1) * BLOCK, (lev * 2 + 2) * BLOCK)
            send_blocks[(k * 2 + lev) * BLOCK:(k * 2 + lev + 1) * BLOCK, :] = (
                mm(back[pick, :HALF], win[HALF:, :])
                + mm(back[pick, HALF:], lon_rims[at:at + 2 * PIECE, :])
            ).astype(BF16)
    halo2 = remote(send_blocks, lat_blocks, halo_s.at[1], halo_r.at[1], (lon, lat_p))

    stage2 = []
    for part in range(3):
        for k in range(3):
            stage1[part * 3 + k].wait_recv()
        mine = pl.ds(pl.multiple_of(place[ORDERS[part][0]] * 256, 256), 256)
        sum1[part] = (own[part, mine, :] + recv1[part, 0].astype(F32)) + (
            recv1[part, 1].astype(F32) + recv1[part, 2].astype(F32)
        )
        axis = ORDERS[part][1]
        for step in (1, 2, 3):
            device, at = peer(axis, step)
            rows = pl.ds(pl.multiple_of(at * 64, 64), 64)
            stage2.append(
                remote(sum1.at[part, rows], recv2.at[part, step - 1],
                       rs_s.at[1, part, step - 1], rs_r.at[1, part, step - 1], device)
            )
    gain_total = gains_sum(1, gain_copies)
    gain_copies = gains_along(2, gain_total)
    stage3 = []
    for part in range(3):
        for k in range(3):
            stage2[part * 3 + k].wait_recv()
        mine = pl.ds(pl.multiple_of(place[ORDERS[part][1]] * 64, 64), 64)
        sum2[part] = (sum1[part, mine, :] + recv2[part, 0]) + (recv2[part, 1] + recv2[part, 2])
        axis = ORDERS[part][2]
        for step in (1, 2, 3):
            device, at = peer(axis, step)
            rows = pl.ds(pl.multiple_of(at * 16, 16), 16)
            stage3.append(
                remote(sum2.at[part, rows], recv3.at[part, step - 1],
                       rs_s.at[2, part, step - 1], rs_r.at[2, part, step - 1], device)
            )
    gain_total = gains_sum(2, gain_copies)
    gain_copies = gains_along(3, gain_total)
    scale = np.float32(147456 ** (-0.5))

    def spread(level, part, rows):
        sent = []
        axis = ORDERS[part][2 - level]
        for step in (1, 2, 3):
            device, _ = peer(axis, step)
            sent.append(
                remote(result(part).at[rows], result(part).at[rows],
                       ag_s.at[level, part, step - 1], ag_r.at[level, part, step - 1], device)
            )
        return sent

    def at_rows(part, length):
        base = (core * 2048 + part * PART) if part < 2 else core * PART
        first, second, third = (place[axis] for axis in ORDERS[part])
        for amount, value in ((256, first), (64, second), (16, third)):
            if amount >= length:
                base = base + value * amount
        return pl.ds(pl.multiple_of(base, length), length)

    level0 = []
    for part in range(3):
        for k in range(3):
            stage3[part * 3 + k].wait_recv()
        mine = pl.ds(pl.multiple_of(place[ORDERS[part][2]] * 16, 16), 16)
        total = (sum2[part, mine, :] + recv3[part, 0]) + (recv3[part, 1] + recv3[part, 2])
        rows = at_rows(part, 16)
        result(part)[rows, :] = (total * scale).astype(BF16)
        level0.append(spread(0, part, rows))
    gain_total = gains_sum(3, gain_copies)
    gains_out[...] = gain_total * scale
    level1 = []
    for part in range(3):
        for copy in level0[part]:
            copy.wait()
        level1.append(spread(1, part, at_rows(part, 64)))
    level2 = []
    for part in range(3):
        for copy in level1[part]:
            copy.wait()
        level2.append(spread(2, part, at_rows(part, 256)))
    last = []
    for part in range(3):
        for copy in level2[part]:
            copy.wait()
        rows = part_rows(core, part)
        last.append(remote(result(part).at[rows], result(part).at[rows], ag_s.at[3, part, 0], ag_r.at[3, part, 0], partner))
    for copy in pairs + stage1 + stage2 + stage3:
        copy.wait_send()
    halo2.wait()
    for copy in last:
        copy.wait()


def sum_all(*args):
    vm = pl.BlockSpec(memory_space=pltpu.VMEM)
    hbm = pl.BlockSpec(memory_space=pl.ANY)
    shape = jax.ShapeDtypeStruct
    dma = pltpu.SemaphoreType.DMA
    return pl.pallas_call(
        sum_kernel,
        out_shape=(
            shape((2 * FF, D), BF16),
            shape((4 * D, D), BF16),
            shape((8, D), F32),
            shape((8 * PIECE, D), BF16),
            shape((4 * BLOCK, D), BF16),
        ),
        in_specs=[hbm, hbm] + [vm] * (len(args) - 2),
        out_specs=(vm,) * 5,
        scratch_shapes=[
            pltpu.VMEM((3, PART, D), F32),
            pltpu.VMEM((3, PART, D), F32),
            pltpu.VMEM((3, PART, D), BF16),
            pltpu.VMEM((3, PART, D), BF16),
            pltpu.VMEM((3, 3, 256, D), BF16),
            pltpu.VMEM((3, 3, 256, D), BF16),
            pltpu.VMEM((3, 256, D), F32),
            pltpu.VMEM((3, 3, 64, D), F32),
            pltpu.VMEM((3, 64, D), F32),
            pltpu.VMEM((3, 3, 16, D), F32),
            pltpu.VMEM((4 * BLOCK, D), BF16),
            pltpu.VMEM((4, 4, 8, D), F32),
            dma((3, 2)),
            dma((3,)),
            dma((3,)),
            dma((3, 3, 3)),
            dma((3, 3, 3)),
            dma((4, 3, 3)),
            dma((4, 3, 3)),
            dma((2,)),
            dma((2,)),
            dma((4, 3)),
            dma((4, 3)),
        ],
        compiler_params=pltpu.CompilerParams(collective_id=1, has_side_effects=True, vmem_limit_bytes=VMEM_BYTES),
        name="sum_all",
    )(*args)


def finish_kernel(r1, r2, out_win, gtok_win, lon_rims, lat_blocks, back, outputs, g_tok, g_qkv, g_out, g_up, g_down, src):
    for n in range(4):
        g_up[:, n * D:(n + 1) * D] = r1[n * D:(n + 1) * D, :].astype(F32)
    g_down[...] = r1[FF:, :].astype(F32)
    for n in range(3):
        g_qkv[:, n * D:(n + 1) * D] = r2[n * D:(n + 1) * D, :].astype(F32)
    g_out[...] = r2[3 * D:, :].astype(F32)
    for k, (win, full) in enumerate(((out_win, outputs), (gtok_win, g_tok))):
        for wr in range(2):
            at = (k * 2 + wr) * 2 * PIECE
            src[:HALF, :] = win[wr * HALF:(wr + 1) * HALF, :]
            src[HALF:, :] = lon_rims[at:at + 2 * PIECE, :]
            for lev in range(2):
                if wr == 0:
                    pick, length = slice(lev * 288, (lev + 1) * 288), 288
                    to = lev * HALF + 144
                else:
                    pick, length = slice(lev * 288, lev * 288 + 144), 144
                    to = lev * HALF + 432
                full[to:to + length, :] = mm(back[pick, :], src[...]).astype(BF16)
        for lev in range(2):
            full[lev * HALF:lev * HALF + BLOCK, :] = lat_blocks[(k * 2 + lev) * BLOCK:(k * 2 + lev + 1) * BLOCK, :]


def finish_all(*args):
    vm = pl.BlockSpec(memory_space=pltpu.VMEM)
    shape = jax.ShapeDtypeStruct
    return pl.pallas_call(
        finish_kernel,
        out_shape=(
            shape((TOK, D), BF16),
            shape((TOK, D), BF16),
            shape((D, 3 * D), F32),
            shape((D, D), F32),
            shape((D, FF), F32),
            shape((FF, D), F32),
        ),
        in_specs=[vm] * len(args),
        out_specs=(vm,) * 6,
        scratch_shapes=[pltpu.VMEM((HALF + 2 * PIECE, D), BF16)],
        compiler_params=pltpu.CompilerParams(vmem_limit_bytes=VMEM_BYTES),
        name="finish",
    )(*args)


def on_device(tokens, cotangent, valid, w_qkv, w_out, w_up, w_down, gains):
    into, back, rim_in, rim_back = gather_maps()
    tok = tokens.reshape(TOK, D)
    cot = cotangent.reshape(TOK, D)
    usable = jnp.where(valid == 1, 0.0, LOW).astype(F32)
    usable = usable.reshape(2, 12, 4, 6).transpose(0, 2, 1, 3).reshape(8, 1, 72)
    key_bias = jnp.broadcast_to(usable, (8, 2, 72)).reshape(TOK, 1)
    lat_t, lat_c, rim_t, rim_c = halo(tok, cot, rim_in)
    x, packed, lowered, context, out_win, gmix, g1, gain2 = forward(
        tok, cot, lat_t, lat_c, rim_t, rim_c, into, key_bias, w_qkv, w_out, w_up, w_down, gains
    )
    g2, gtok_win, gain1, rims = backward(
        x, packed, lowered, context, out_win, gmix, key_bias, w_qkv, w_out, gains, rim_back
    )
    r1, r2, gain_sums, lon_rims, lat_blocks = sum_all(g1, g2, gain1, gain2, rims, out_win, gtok_win, back)
    outputs, g_tok, g_qkv, g_out, g_up, g_down = finish_all(r1, r2, out_win, gtok_win, lon_rims, lat_blocks, back)
    return (
        outputs.reshape(tokens.shape),
        g_tok.reshape(tokens.shape),
        g_qkv,
        g_out,
        g_up,
        g_down,
        gain_sums[:2],
    )


def solution(mesh):
    field = P(None, "lat", "lon", None)
    in_specs = (field, field, P("lat", "lon"), P(), P(), P(), P(), P())
    out_specs = (field, field, P(), P(), P(), P(), P())
    return jax.shard_map(on_device, mesh=mesh, in_specs=in_specs, out_specs=out_specs, check_vma=False)
```

```python
import jax
import jax.numpy as jnp
import numpy as np
from jax import lax
from jax.experimental import pallas as pl
from jax.experimental.pallas import tpu as pltpu
from jax.sharding import PartitionSpec as P

F32 = jnp.float32
BF16 = jnp.bfloat16
MESH = pl.DeviceIdType.MESH
HEAD = 64
WIN = 144
TOK = 1152
HALF = 576
D = 512
FF = 2048
COLS = 24
BLOCK = 144
PIECE = 48
epsilon = 1e-05
LOW = -1e30
SCALE = np.float32(147456 ** (-0.5))
ORDERS = ((0, 1, 2), (1, 2, 0), (2, 0, 1))
VMEM_BYTES = 63 * 1024 * 1024


def gather_maps():
    into = np.zeros((HALF, HALF + 2 * PIECE), np.float32)
    back = np.zeros((HALF, HALF + 2 * PIECE), np.float32)
    rim_in = np.zeros((4 * PIECE, TOK), np.float32)
    rim_back = np.zeros((2 * PIECE, HALF), np.float32)
    for lev in range(2):
        for half in range(2):
            for r in range(6):
                for col in range(COLS):
                    window = (col // 6) * WIN + lev * 72 + half * 36 + r * 6 + col % 6
                    chunk = (lev * 2 + half) * BLOCK + r * COLS
                    if col + 3 < COLS:
                        into[window, chunk + col + 3] = 1
                        back[chunk + col + 3, window] = 1
                    else:
                        rim = half * PIECE + lev * 18 + r * 3 + col + 3 - COLS
                        into[window, HALF + rim] = 1
                        back[chunk + col + 3 - COLS, HALF + rim] = 1
                        rim_back[rim, window] = 1
    for lev in range(2):
        for block in range(4):
            for r in range(6):
                for col in range(3):
                    rim_in[block * PIECE + lev * 18 + r * 3 + col, lev * HALF + block * BLOCK + r * COLS + col] = 1
    return [jnp.asarray(m, BF16) for m in (into, back, rim_in, rim_back)]


def mm(a, b):
    return lax.dot_general(a, b, (((1,), (0,)), ((), ())), preferred_element_type=F32)


def mm_nt(a, b):
    return lax.dot_general(a, b, (((1,), (1,)), ((), ())), preferred_element_type=F32)


def mm_tn(a, b):
    return lax.dot_general(a, b, (((0,), (0,)), ((), ())), preferred_element_type=F32)


def norm_stats(values):
    centred = values - jnp.mean(values, -1, keepdims=True)
    inv_std = lax.rsqrt(jnp.mean(centred * centred, -1, keepdims=True) + epsilon)
    return centred * inv_std, inv_std


def norm_back(grad_value, normed, inv_std, gain_row):
    scaled = grad_value * gain_row
    return inv_std * (
        scaled
        - jnp.mean(scaled, -1, keepdims=True)
        - normed * jnp.mean(scaled * normed, -1, keepdims=True)
    )


def rows_loop(total, step, body):
    def run(i, carry):
        body(pl.ds(pl.multiple_of(i * step, step), step))
        return carry

    lax.fori_loop(0, total // step, run, 0)


def window_bias(key_bias, split):
    rows = lax.broadcasted_iota(jnp.int32, (WIN, WIN), 0)
    cols = lax.broadcasted_iota(jnp.int32, (WIN, WIN), 1)
    bias = jnp.where(rows == cols, 0.0, jnp.broadcast_to(key_bias, (WIN, WIN)))
    apart = ((rows // 36) % 2) != ((cols // 36) % 2)
    return bias + jnp.where(apart, split, 0.0)


def scores_t(key2, query_m, bias):
    s = mm_nt(key2, query_m) * HEAD ** (-0.5) + bias
    e = jnp.exp(s - jnp.max(s, 0, keepdims=True))
    return e * (1.0 / jnp.sum(e, 0, keepdims=True))


def head_masks():
    lane = lax.broadcasted_iota(jnp.int32, (WIN, 128), 1)
    return [lane < HEAD, lane >= HEAD]


def split_amount(window):
    last = (lax.axis_index("lat") == lax.axis_size("lat") - 1) & (window >= 4)
    return jnp.where(last, LOW, 0.0).astype(F32)


def position():
    lon, lat = lax.axis_index("lon"), lax.axis_index("lat")
    y = lax.rem(lax.div(lat, 2), 2) * 2 + lax.rem(lon, 2)
    return [lax.div(lon, 2), y, lax.div(lat, 4)], lax.rem(lat, 2)


def device_at(place, core):
    x, y, z = place
    return (x * 2 + lax.rem(y, 2), z * 4 + lax.div(y, 2) * 2 + core)


def remote(src, dst, s, r, device):
    return pltpu.make_async_remote_copy(
        src_ref=src, dst_ref=dst, send_sem=s, recv_sem=r, device_id=device, device_id_type=MESH
    )


def loop(first, last, body):
    def run(i, carry):
        body(i)
        return carry

    lax.fori_loop(first, last, run, 0)


class Sum:
    def __init__(self, order, start, size, own, out, recv1, sum1, recv2, sum2, recv3, fin, result, base, sems, fine):
        self.order, self.start, self.size, self.fine = order, start, size, fine
        self.own, self.out, self.recv1, self.sum1, self.recv2, self.sum2, self.recv3, self.fin = (
            own, out, recv1, sum1, recv2, sum2, recv3, fin
        )
        self.result, self.base, self.sems = result, base, sems
        self.place, self.core = position()
        self.lengths = (size // 4, size // 16, size // 64)

    def peer(self, level, step):
        axis = self.order[level]
        there = list(self.place)
        there[axis] = lax.rem(self.place[axis] + step, 4)
        return device_at(there, self.core), there[axis]

    def mine(self, level):
        return self.place[self.order[level]]

    def block(self, at, level, base=0):
        length = self.lengths[level]
        return pl.ds(pl.multiple_of(base + at * length, length), length)

    def down(self, level, step):
        s, r = self.sems.at[0, level, step - 1], self.sems.at[1, level, step - 1]
        device, at = self.peer(level, step)
        if level == 0:
            return remote(self.out.at[self.block(at, 0, self.start)], self.recv1.at[step - 1], s, r, device)
        if level == 1:
            return remote(self.sum1.at[self.block(at, 1)], self.recv2.at[step - 1], s, r, device)
        if self.fine:
            return remote(self.sum2.at[self.block(at, 2)], self.recv3.at[step - 1], s, r, device)
        slot = self.recv3.at[self.mine(2)]
        return remote(slot, slot, s, r, device)

    def result_rows(self, level):
        at = self.base + self.start
        for k in range(level + 1):
            at = at + self.mine(k) * self.lengths[k]
        return pl.ds(pl.multiple_of(at, self.lengths[level]), self.lengths[level])

    def up(self, level, step):
        s, r = self.sems.at[2, level, step - 1], self.sems.at[3, level, step - 1]
        device, _ = self.peer(level, step)
        rows = self.result.at[self.result_rows(level)]
        top = 2 if self.fine else 1
        return remote(self.fin if level == top else rows, rows, s, r, device)

    def hand(self):
        rows = pl.ds(pl.multiple_of(self.base + self.start, self.size), self.size)
        rows = self.result.at[rows]
        return remote(rows, rows, self.sems.at[0, 3, 0], self.sems.at[1, 3, 0], device_at(self.place, 1 - self.core))

    def keep(self):
        top = 2 if self.fine else 1
        return pltpu.make_async_copy(self.fin, self.result.at[self.result_rows(top)], self.sems.at[0, 3, 1])

    def received(self, make, level):
        for step in (1, 2, 3):
            make(level, step).wait_recv()

    def send(self, make, level):
        for step in (1, 2, 3):
            make(level, step).start()

    def begin(self):
        for step in (1, 2, 3):
            _, at = self.peer(0, step)
            rows = self.block(at, 0, self.start)
            self.out[rows, :] = self.own[rows, :].astype(BF16)
        self.send(self.down, 0)

    def second(self):
        self.received(self.down, 0)
        rows = self.block(self.mine(0), 0, self.start)
        self.sum1[...] = (self.own[rows, :] + self.recv1[0].astype(F32)) + (
            self.recv1[1].astype(F32) + self.recv1[2].astype(F32)
        )
        self.send(self.down, 1)

    def third(self):
        self.received(self.down, 1)
        rows = self.block(self.mine(1), 1)
        total = (self.sum1[rows, :] + self.recv2[0]) + (self.recv2[1] + self.recv2[2])
        if self.fine:
            self.sum2[...] = total
        else:
            self.recv3[self.mine(2)] = total
        self.send(self.down, 2)

    def gather(self):
        self.received(self.down, 2)
        if self.fine:
            rows = self.block(self.mine(2), 2)
            total = (self.sum2[rows, :] + self.recv3[0]) + (self.recv3[1] + self.recv3[2])
        else:
            total = (self.recv3[0] + self.recv3[1]) + (self.recv3[2] + self.recv3[3])
        self.fin[...] = (total * SCALE).astype(BF16)
        self.keep().start()
        self.send(self.up, 2 if self.fine else 1)
        self.keep().wait()

    def gather_next(self, level):
        self.received(self.up, level + 1)
        self.send(self.up, level)

    def gather_pair(self):
        self.received(self.up, 0)
        self.hand().start()

    def end(self):
        for level in range(3):
            for step in (1, 2, 3):
                self.down(level, step).wait_send()
                if level < 2 or self.fine:
                    self.up(level, step).wait_send()
        self.hand().wait()


def block_kernel(
    tok, cot, rim_in, into, rim_back, back_last, key_bias, w_qkv_h, w_out_h, w_up_h, w_down_h, gains,
    r1, r2, gains_out, out_win, gtok_win, lon_rims, lat_blocks,
    w_qkv, w_out, w_up, w_down, lat_t, lat_c, rim_t, rim_c, pack_t, pack_c,
    x_ref, c_ref, lowered, context, hid, hid_t, c_t, g_ctx, packed, g_pack, src, mixed, acc_out, acc_in,
    own1, out1, pair1, recv1a, sum1a, recv2a, sum2a, recv3a, fin_a,
    own2, out2, pair2, recv1b, sum1b, recv2b, recv3b, fin_b,
    rims, send_blocks, gain_slots, gain_part,
    load_sem, halo_s, halo_r, back_s, back_r, pair1_s, pair1_r, pair2_s, pair2_r, sums_a, sums_b, gain_s, gain_r,
):
    place, core = position()
    lon, lat = lax.axis_index("lon"), lax.axis_index("lat")
    n_lon, n_lat = lax.axis_size("lon"), lax.axis_size("lat")
    lon_m, lon_p = lax.rem(lon + n_lon - 1, n_lon), lax.rem(lon + 1, n_lon)
    lat_m, lat_p = lax.rem(lat + n_lat - 1, n_lat), lax.rem(lat + 1, n_lat)
    partner = device_at(place, 1 - core)
    gain_a = gains[0:1, :]
    gain_b = gains[1:2, :]
    masks = head_masks()

    def peer(axis, step):
        there = list(place)
        there[axis] = lax.rem(place[axis] + step, 4)
        return device_at(there, core)

    barrier = pltpu.get_barrier_semaphore()
    greet = [(lon, lat_m), (lon, lat_p), (lon_m, lat), (lon_p, lat), (lon_m, lat_m), (lon_p, lat_p), partner]
    greet += [peer(axis, step) for axis in range(3) for step in (1, 2, 3)]
    for device in greet:
        pl.semaphore_signal(barrier, inc=1, device_id=device, device_id_type=MESH)
    loads = [
        pltpu.make_async_copy(a, b, load_sem.at[k])
        for k, (a, b) in enumerate(
            ((tok, context), (cot, out_win), (w_qkv_h, w_qkv), (w_out_h, w_out), (w_up_h, w_up), (w_down_h, w_down))
        )
    ]
    for copy in loads:
        copy.start()
    loads[0].wait()
    pack_t[...] = mm(rim_in[...], context[...]).astype(BF16)
    loads[1].wait()
    pack_c[...] = mm(rim_in[...], out_win[...]).astype(BF16)
    pl.semaphore_wait(barrier, len(greet))

    halos = []
    rest = pl.ds(PIECE, 3 * PIECE)
    corner = pl.ds(0, PIECE)
    for pack, rim, lat_rim, full in ((pack_t, rim_t, lat_t, context), (pack_c, rim_c, lat_c, out_win)):
        wanted = [
            (pack.at[rest], rim.at[rest], (lon_m, lat)),
            (pack.at[corner], rim.at[corner], (lon_m, lat_m)),
        ]
        for lev in range(2):
            wanted.append(
                (full.at[pl.ds(lev * HALF, BLOCK)], lat_rim.at[pl.ds(lev * BLOCK, BLOCK)], (lon, lat_m))
            )
        for a, b, device in wanted:
            k = len(halos)
            halos.append(remote(a, b, halo_s.at[k], halo_r.at[k], device))
            halos[k].start()

    def enter(full, lat_rim, rim, dst, wr):
        for lev in range(2):
            if wr == 0:
                src[lev * 288:(lev + 1) * 288, :] = full[lev * HALF + 144:lev * HALF + 432, :]
            else:
                src[lev * 288:lev * 288 + 144, :] = full[lev * HALF + 432:lev * HALF + 576, :]
                src[lev * 288 + 144:(lev + 1) * 288, :] = lat_rim[lev * BLOCK:(lev + 1) * BLOCK, :]
        if wr == 0:
            src[HALF:, :] = rim[PIECE:3 * PIECE, :]
        else:
            src[HALF:HALF + PIECE, :] = rim[3 * PIECE:, :]
            src[HALF + PIECE:, :] = rim[:PIECE, :]
        for n in range(2):
            cols = slice(n * 256, (n + 1) * 256)
            dst[wr * HALF:(wr + 1) * HALF, cols] = mm(into[...], src[:, cols]).astype(BF16)

    def attend(w):
        rows = pl.ds(pl.multiple_of(w * WIN, WIN), WIN)
        bias = window_bias(key_bias[rows, :], split_amount(w))
        for pair in range(4):
            lanes = slice(pair * 128, (pair + 1) * 128)
            query = packed[rows, lanes]
            key = packed[rows, D + pair * 128:D + (pair + 1) * 128]
            value = packed[rows, 2 * D + pair * 128:2 * D + (pair + 1) * 128]
            total = None
            for mask in masks:
                probs = scores_t(key, jnp.where(mask, query, 0), bias)
                part = mm_tn(probs.astype(BF16), jnp.where(mask, value, 0))
                total = part if total is None else total + part
            hid[rows, lanes] = total.astype(BF16)

    for wr in range(2):
        for copy in (halos[0:1] if wr == 0 else halos[1:4]):
            copy.wait_recv()
        enter(context, lat_t, rim_t, x_ref, wr)
        if wr == 0:
            loads[2].wait()

        def first_norm(i, wr=wr):
            rows = pl.ds(pl.multiple_of(wr * HALF + i * WIN, WIN), WIN)
            normed, _ = norm_stats(x_ref[rows, :].astype(F32))
            lowered[rows, :] = (normed * gain_a).astype(BF16)

        loop(0, 4, first_norm)
        band = slice(wr * HALF, (wr + 1) * HALF)

        def project(n, band=band):
            cols = pl.ds(pl.multiple_of(n * 256, 256), 256)
            packed[band, cols] = mm(lowered[band, :], w_qkv[:, cols]).astype(BF16)

        loop(0, 6, project)
        loop(4 * wr, 4 * wr + 4, attend)
    for copy in halos[4:8]:
        copy.wait_recv()
    for wr in range(2):
        enter(out_win, lat_c, rim_c, c_ref, wr)
    for copy in halos:
        copy.wait_send()
    loads[3].wait()
    context[...] = hid[...]

    def second_norm(rows):
        attended = mm(context[rows, :], w_out[...]).astype(BF16)
        m = x_ref[rows, :].astype(F32) + attended.astype(F32)
        mixed[rows, :] = m
        normed, _ = norm_stats(m)
        hid[rows, :] = (normed * gain_b).astype(BF16)

    rows_loop(TOK, 288, second_norm)
    hid_t[...] = hid[...].T
    c_t[...] = c_ref[...].T
    acc_out[...] = jnp.zeros_like(acc_out)
    acc_in[...] = jnp.zeros_like(acc_in)
    loads[4].wait()
    loads[5].wait()

    sum_a = [
        Sum(ORDERS[p], p * 1024, 1024, own1, out1, recv1a.at[p], sum1a.at[p], recv2a.at[p], sum2a.at[p], recv3a.at[p],
            fin_a.at[p], r1, core * 2048, sums_a.at[p], True)
        for p in range(2)
    ]
    sum_b = [
        Sum(ORDERS[2 - 2 * p], p * 512, 512, own2, out2, recv1b.at[p], sum1b.at[p], recv2b.at[p], None, recv3b.at[p],
            fin_b.at[p], r2, core * 1024, sums_b.at[p], False)
        for p in range(2)
    ]

    def unit(n, length):
        return pl.ds(pl.multiple_of(n * length, length), length)

    def hand1(n):
        rows = unit(n, 256)
        return remote(out1.at[rows], pair1.at[rows], pair1_s.at[n], pair1_r.at[n], partner)

    def hand2(n):
        rows = unit(n, 128)
        return remote(out2.at[rows], pair2.at[rows], pair2_s.at[n], pair2_r.at[n], partner)

    def share(left, right, flip, own, out, at):
        rows = pl.ds(pl.multiple_of(at, 128), 128)
        for which, dst in ((core, own), (1 - core, out)):
            part = mm(left[pl.ds(pl.multiple_of(which * 256, 256), 256), :], right)
            if flip:
                part = part.T
            part = part.astype(dst.dtype)
            dst[rows, 0:256] = part[0:128]
            dst[rows, 256:512] = part[128:256]

    def absorb1(n):
        hand1(n).wait_recv()
        rows = unit(n, 256)
        own1[rows, :] += pair1[rows, :].astype(F32)

    def begin_a(p):
        for n in range(4 * p, 4 * p + 4):
            hand1(n).wait_send()
        sum_a[p].begin()

    wide = 256

    def columns(n):
        cols = pl.ds(pl.multiple_of(n * wide, wide), wide)
        raised = mm(hid[...], w_up[:, cols])
        slope = np.float32(np.sqrt(2 / np.pi))
        square = raised * raised
        t = jnp.tanh(slope * (raised + np.float32(0.044715) * (square * raised)))
        cdf = 0.5 * (1.0 + t)
        activated = (raised * cdf).astype(BF16)
        deriv = cdf + 0.5 * raised * (1.0 - t * t) * (slope * (1.0 + np.float32(3 * 0.044715) * square))
        grad_act = mm_nt(c_ref[...], w_down[cols, :])
        grad_raised = (grad_act * deriv).astype(BF16)
        acc_out[...] += mm(activated, w_down[cols, :])
        acc_in[...] += mm_nt(grad_raised, w_up[:, cols])
        share(hid_t, grad_raised, False, own1, out1, n * 256)
        share(c_t, activated, True, own1, out1, n * 256 + 128)
        hand1(n).start()

        @pl.when(n > 0)
        def _():
            absorb1(n - 1)

        @pl.when(n == 5)
        def _():
            begin_a(0)

    loop(0, FF // wide, columns)
    absorb1(FF // wide - 1)
    begin_a(1)
    gain_part[...] = jnp.zeros_like(gain_part)

    def finish(rows):
        m = mixed[rows, :]
        out_win[rows, :] = (m + acc_out[rows, :]).astype(BF16)
        normed, inv_std = norm_stats(m)
        grad_in = acc_in[rows, :]
        gain_part[1:2, :] += jnp.sum(grad_in * normed, 0, keepdims=True)
        g = c_ref[rows, :].astype(F32) + norm_back(grad_in, normed, inv_std, gain_b)
        acc_in[rows, :] = g
        g = g.astype(BF16)
        hid[rows, :] = g
        g_ctx[rows, :] = mm_nt(g, w_out[...]).astype(BF16)

    rows_loop(TOK, WIN, finish)
    gmix, g_att = acc_in, hid

    hid_t[...] = lowered[...].T
    c_t[...] = context[...].T
    for n in range(2):
        share(c_t, g_att[:, n * 256:(n + 1) * 256], False, own2, out2, (6 + n) * 128)
        hand2(6 + n).start()

    def attend_back(w):
        rows = pl.ds(pl.multiple_of(w * WIN, WIN), WIN)
        bias = window_bias(key_bias[rows, :], split_amount(w))
        for pair in range(4):
            lanes = slice(pair * 128, (pair + 1) * 128)
            key_lanes = slice(D + pair * 128, D + (pair + 1) * 128)
            value_lanes = slice(2 * D + pair * 128, 2 * D + (pair + 1) * 128)
            query = packed[rows, lanes]
            key = packed[rows, key_lanes]
            value = packed[rows, value_lanes]
            grad = g_ctx[rows, lanes]
            sums = [None, None, None]
            for mask in masks:
                query_m = jnp.where(mask, query, 0)
                grad_m = jnp.where(mask, grad, 0)
                probs = scores_t(key, query_m, bias)
                g_weights = mm_nt(value, grad_m)
                inner = jnp.sum(probs * g_weights, 0, keepdims=True)
                g_scores = (probs * (g_weights - inner) * HEAD ** (-0.5)).astype(BF16)
                parts = (
                    mm_tn(g_scores, jnp.where(mask, key, 0)),
                    mm(g_scores, query_m),
                    mm(probs.astype(BF16), grad_m),
                )
                sums = [b if a is None else a + b for a, b in zip(sums, parts)]
            g_pack[rows, lanes] = sums[0].astype(BF16)
            g_pack[rows, key_lanes] = sums[1].astype(BF16)
            g_pack[rows, value_lanes] = sums[2].astype(BF16)
        for when, steps in (
            (0, [sum_a[0].second]),
            (3, [sum_a[1].second, sum_a[0].third]),
            (5, [sum_a[0].gather, sum_a[1].third]),
            (6, [lambda: sum_a[0].gather_next(1), sum_a[1].gather]),
            (7, [lambda: sum_a[0].gather_next(0), lambda: sum_a[1].gather_next(1)]),
        ):
            @pl.when(w == when)
            def _(steps=steps):
                for step in steps:
                    step()

    loop(0, 8, attend_back)
    sum_a[1].gather_next(0)

    def weight(n):
        cols = pl.ds(pl.multiple_of(n * 256, 256), 256)
        share(hid_t, g_pack[:, cols], False, own2, out2, n * 128)
        hand2(n).start()

    loop(0, 6, weight)
    for n in (6, 7, 0, 1, 2, 3, 4, 5):
        hand2(n).wait()
        rows = unit(n, 128)
        own2[rows, :] += pair2[rows, :].astype(F32)
    for part in sum_b:
        part.begin()

    def finish_back(rows):
        g_low = mm_nt(g_pack[rows, :], w_qkv[...]).astype(BF16).astype(F32)
        normed, inv_std = norm_stats(x_ref[rows, :].astype(F32))
        gain_part[0:1, :] += jnp.sum(g_low * normed, 0, keepdims=True)
        gtok_win[rows, :] = (gmix[rows, :] + norm_back(g_low, normed, inv_std, gain_a)).astype(BF16)

    rows_loop(TOK, 288, finish_back)

    gain_slots[0, 0] = gain_part[...]
    gain_pair = remote(gain_slots.at[0, 0], gain_slots.at[0, 1], gain_s.at[0, 0], gain_r.at[0, 0], partner)
    gain_pair.start()
    for k, win in enumerate((out_win, gtok_win)):
        for wr in range(2):
            at = (k * 2 + wr) * 2 * PIECE
            rims[at:at + 2 * PIECE, :] = mm(rim_back[...], win[wr * HALF:(wr + 1) * HALF, :]).astype(BF16)
    halo1 = remote(rims, lon_rims, back_s.at[0], back_r.at[0], (lon_p, lat))
    halo1.start()

    def gains_along(level, total):
        axis = level - 1
        slot = gain_slots.at[level, place[axis]]
        gain_slots[level, place[axis]] = total
        copies = [
            remote(slot, slot, gain_s.at[level, step - 1], gain_r.at[level, step - 1], peer(axis, step))
            for step in (1, 2, 3)
        ]
        for copy in copies:
            copy.start()
        return copies

    def gains_sum(level, copies):
        for copy in copies:
            copy.wait()
        return (gain_slots[level, 0] + gain_slots[level, 1]) + (gain_slots[level, 2] + gain_slots[level, 3])

    for part in sum_b:
        part.second()
    gain_pair.wait()
    gain_copies = gains_along(1, gain_slots[0, 0] + gain_slots[0, 1])
    halo1.wait()
    for k, win in enumerate((out_win, gtok_win)):
        at = (k * 2 + 1) * 2 * PIECE
        for lev in range(2):
            pick = slice(lev * BLOCK, (lev + 1) * BLOCK)
            send_blocks[(k * 2 + lev) * BLOCK:(k * 2 + lev + 1) * BLOCK, :] = (
                mm(back_last[pick, :HALF], win[HALF:, :])
                + mm(back_last[pick, HALF:], lon_rims[at:at + 2 * PIECE, :])
            ).astype(BF16)
    halo2 = remote(send_blocks, lat_blocks, back_s.at[1], back_r.at[1], (lon, lat_p))
    halo2.start()
    for part in sum_a:
        part.gather_pair()
    for part in sum_b:
        part.third()
    gain_copies = gains_along(2, gains_sum(1, gain_copies))
    for part in sum_b:
        part.gather()
    gain_copies = gains_along(3, gains_sum(2, gain_copies))
    for part in sum_b:
        part.gather_next(0)
    gains_out[...] = gains_sum(3, gain_copies) * SCALE
    for part in sum_b:
        part.gather_pair()
    for part in sum_a + sum_b:
        part.end()
    halo2.wait()


def block(*args):
    vm = pl.BlockSpec(memory_space=pltpu.VMEM)
    hbm = pl.BlockSpec(memory_space=pl.ANY)
    shape = jax.ShapeDtypeStruct
    dma = pltpu.SemaphoreType.DMA
    vmem = pltpu.VMEM
    field = vmem((TOK, D), BF16)
    field_t = vmem((D, TOK), BF16)
    wide = vmem((TOK, D), F32)
    rim = vmem((4 * PIECE, D), BF16)
    lat_rim = vmem((2 * BLOCK, D), BF16)
    return pl.pallas_call(
        block_kernel,
        out_shape=(
            shape((2 * FF, D), BF16),
            shape((4 * D, D), BF16),
            shape((8, D), F32),
            shape((TOK, D), BF16),
            shape((TOK, D), BF16),
            shape((8 * PIECE, D), BF16),
            shape((4 * BLOCK, D), BF16),
        ),
        in_specs=[hbm, hbm] + [vm] * 5 + [hbm] * 4 + [vm],
        out_specs=(hbm, hbm) + (vm,) * 5,
        scratch_shapes=[
            vmem((D, 3 * D), BF16), vmem((D, D), BF16), vmem((D, FF), BF16), vmem((FF, D), BF16),
            lat_rim, lat_rim, rim, rim, rim, rim,
            field, field, field, field, field, field_t, field_t, field,
            vmem((TOK, 3 * D), BF16), vmem((TOK, 3 * D), BF16), vmem((HALF + 2 * PIECE, D), BF16),
            wide, wide, wide,
            vmem((FF, D), F32), vmem((FF, D), BF16), vmem((FF, D), BF16),
            vmem((2, 3, 256, D), BF16), vmem((2, 256, D), F32), vmem((2, 3, 64, D), F32), vmem((2, 64, D), F32),
            vmem((2, 3, 16, D), F32), vmem((2, 16, D), BF16),
            vmem((2 * D, D), F32), vmem((2 * D, D), BF16), vmem((2 * D, D), BF16),
            vmem((2, 3, 128, D), BF16), vmem((2, 128, D), F32), vmem((2, 3, 32, D), F32),
            vmem((2, 4, 32, D), F32), vmem((2, 32, D), BF16),
            vmem((8 * PIECE, D), BF16), vmem((4 * BLOCK, D), BF16), vmem((4, 4, 8, D), F32), vmem((8, D), F32),
            dma((6,)), dma((8,)), dma((8,)), dma((2,)), dma((2,)), dma((8,)), dma((8,)), dma((8,)), dma((8,)),
            dma((2, 4, 4, 3)), dma((2, 4, 4, 3)), dma((4, 3)), dma((4, 3)),
        ],
        compiler_params=pltpu.CompilerParams(collective_id=0, has_side_effects=True, vmem_limit_bytes=VMEM_BYTES),
        name="block",
    )(*args)


def finish_kernel(r1, r2, out_win, gtok_win, lon_rims, lat_blocks, back, outputs, g_tok, g_qkv, g_out, g_up, g_down, src):
    for core in range(2):
        for n in range(8):
            for k in range(2):
                lanes = slice(k * 256, (k + 1) * 256)
                rows = slice(core * 256 + k * 128, core * 256 + (k + 1) * 128)
                at = core * 2048 + n * 256
                g_up[rows, n * 256:(n + 1) * 256] = r1[at:at + 128, lanes].astype(F32)
                g_down[n * 256 + k * 128:n * 256 + (k + 1) * 128, core * 256:(core + 1) * 256] = (
                    r1[at + 128:at + 256, lanes].astype(F32)
                )
                at = core * 1024 + n * 128
                if n < 6:
                    g_qkv[rows, n * 256:(n + 1) * 256] = r2[at:at + 128, lanes].astype(F32)
                else:
                    g_out[rows, (n - 6) * 256:(n - 5) * 256] = r2[at:at + 128, lanes].astype(F32)

    for k, (win, full) in enumerate(((out_win, outputs), (gtok_win, g_tok))):
        for wr in range(2):
            at = (k * 2 + wr) * 2 * PIECE
            src[:HALF, :] = win[wr * HALF:(wr + 1) * HALF, :]
            src[HALF:, :] = lon_rims[at:at + 2 * PIECE, :]
            for lev in range(2):
                if wr == 0:
                    pick, length = slice(lev * 288, (lev + 1) * 288), 288
                    to = lev * HALF + 144
                else:
                    pick, length = slice(lev * 288, lev * 288 + 144), 144
                    to = lev * HALF + 432
                full[to:to + length, :] = mm(back[pick, :], src[...]).astype(BF16)
        for lev in range(2):
            full[lev * HALF:lev * HALF + BLOCK, :] = lat_blocks[(k * 2 + lev) * BLOCK:(k * 2 + lev + 1) * BLOCK, :]


def finish_all(*args):
    vm = pl.BlockSpec(memory_space=pltpu.VMEM)
    shape = jax.ShapeDtypeStruct
    return pl.pallas_call(
        finish_kernel,
        out_shape=(
            shape((TOK, D), BF16),
            shape((TOK, D), BF16),
            shape((D, 3 * D), F32),
            shape((D, D), F32),
            shape((D, FF), F32),
            shape((FF, D), F32),
        ),
        in_specs=[vm] * len(args),
        out_specs=(vm,) * 6,
        scratch_shapes=[pltpu.VMEM((HALF + 2 * PIECE, D), BF16)],
        compiler_params=pltpu.CompilerParams(vmem_limit_bytes=VMEM_BYTES),
        name="finish",
    )(*args)


def on_device(tokens, cotangent, valid, w_qkv, w_out, w_up, w_down, gains):
    into, back, rim_in, rim_back = gather_maps()
    tok = tokens.reshape(TOK, D)
    cot = cotangent.reshape(TOK, D)
    usable = jnp.where(valid == 1, 0.0, LOW).astype(F32)
    usable = usable.reshape(2, 12, 4, 6).transpose(0, 2, 1, 3).reshape(8, 1, 72)
    key_bias = jnp.broadcast_to(usable, (8, 2, 72)).reshape(TOK, 1)
    back_last = jnp.concatenate([back[BLOCK:2 * BLOCK], back[3 * BLOCK:]], 0)
    r1, r2, gain_sums, out_win, gtok_win, lon_rims, lat_blocks = block(
        tok, cot, rim_in, into, rim_back, back_last, key_bias, w_qkv, w_out, w_up, w_down, gains
    )
    outputs, g_tok, g_qkv, g_out, g_up, g_down = finish_all(r1, r2, out_win, gtok_win, lon_rims, lat_blocks, back)
    return (
        outputs.reshape(tokens.shape),
        g_tok.reshape(tokens.shape),
        g_qkv,
        g_out,
        g_up,
        g_down,
        gain_sums[:2],
    )


def solution(mesh):
    field = P(None, "lat", "lon", None)
    in_specs = (field, field, P("lat", "lon"), P(), P(), P(), P(), P())
    out_specs = (field, field, P(), P(), P(), P(), P())
    return jax.shard_map(on_device, mesh=mesh, in_specs=in_specs, out_specs=out_specs, check_vma=False)
```

```python
import jax
import jax.numpy as jnp
import numpy as np
from jax import lax
from jax.experimental import pallas as pl
from jax.experimental.pallas import tpu as pltpu
from jax.sharding import PartitionSpec as P

F32 = jnp.float32
BF16 = jnp.bfloat16
MESH = pl.DeviceIdType.MESH
HEAD = 64
WIN = 144
TOK = 1152
HALF = 576
D = 512
FF = 2048
COLS = 24
BLOCK = 144
PIECE = 48
epsilon = 1e-05
LOW = -1e30
SCALE = np.float32(147456 ** (-0.5))
VMEM_BYTES = 63 * 1024 * 1024


def gather_maps():
    into = np.zeros((HALF, HALF + 2 * PIECE), np.float32)
    back = np.zeros((HALF, HALF + 2 * PIECE), np.float32)
    rim_in = np.zeros((4 * PIECE, TOK), np.float32)
    rim_back = np.zeros((2 * PIECE, HALF), np.float32)
    for lev in range(2):
        for half in range(2):
            for r in range(6):
                for col in range(COLS):
                    window = (col // 6) * WIN + lev * 72 + half * 36 + r * 6 + col % 6
                    chunk = (lev * 2 + half) * BLOCK + r * COLS
                    if col + 3 < COLS:
                        into[window, chunk + col + 3] = 1
                        back[chunk + col + 3, window] = 1
                    else:
                        rim = half * PIECE + lev * 18 + r * 3 + col + 3 - COLS
                        into[window, HALF + rim] = 1
                        back[chunk + col + 3 - COLS, HALF + rim] = 1
                        rim_back[rim, window] = 1
    for lev in range(2):
        for block in range(4):
            for r in range(6):
                for col in range(3):
                    rim_in[block * PIECE + lev * 18 + r * 3 + col, lev * HALF + block * BLOCK + r * COLS + col] = 1
    return [jnp.asarray(m, BF16) for m in (into, back, rim_in, rim_back)]


def mm(a, b):
    return lax.dot_general(a, b, (((1,), (0,)), ((), ())), preferred_element_type=F32)


def mm_nt(a, b):
    return lax.dot_general(a, b, (((1,), (1,)), ((), ())), preferred_element_type=F32)


def mm_tn(a, b):
    return lax.dot_general(a, b, (((0,), (0,)), ((), ())), preferred_element_type=F32)


def norm_stats(values):
    centred = values - jnp.mean(values, -1, keepdims=True)
    inv_std = lax.rsqrt(jnp.mean(centred * centred, -1, keepdims=True) + epsilon)
    return centred * inv_std, inv_std


def norm_back(grad_value, normed, inv_std, gain_row):
    scaled = grad_value * gain_row
    return inv_std * (
        scaled
        - jnp.mean(scaled, -1, keepdims=True)
        - normed * jnp.mean(scaled * normed, -1, keepdims=True)
    )


def rows_loop(total, step, body):
    def run(i, carry):
        body(pl.ds(pl.multiple_of(i * step, step), step))
        return carry

    lax.fori_loop(0, total // step, run, 0)


def window_bias(key_bias, split):
    rows = lax.broadcasted_iota(jnp.int32, (WIN, WIN), 0)
    cols = lax.broadcasted_iota(jnp.int32, (WIN, WIN), 1)
    bias = jnp.where(rows == cols, 0.0, jnp.broadcast_to(key_bias, (WIN, WIN)))
    apart = ((rows // 36) % 2) != ((cols // 36) % 2)
    return bias + jnp.where(apart, split, 0.0)


def scores_t(key2, query_m, bias):
    s = mm_nt(key2, query_m) * HEAD ** (-0.5) + bias
    e = jnp.exp(s - jnp.max(s, 0, keepdims=True))
    return e * (1.0 / jnp.sum(e, 0, keepdims=True))


def head_masks():
    lane = lax.broadcasted_iota(jnp.int32, (WIN, 128), 1)
    return [lane < HEAD, lane >= HEAD]


def split_amount(window):
    last = (lax.axis_index("lat") == lax.axis_size("lat") - 1) & (window >= 4)
    return jnp.where(last, LOW, 0.0).astype(F32)


def position():
    lon, lat = lax.axis_index("lon"), lax.axis_index("lat")
    y = lax.rem(lax.div(lat, 2), 2) * 2 + lax.rem(lon, 2)
    return [lax.div(lon, 2), y, lax.div(lat, 4)], lax.rem(lat, 2)


def device_at(place, core):
    x, y, z = place
    return (x * 2 + lax.rem(y, 2), z * 4 + lax.div(y, 2) * 2 + core)


def remote(src, dst, s, r, device):
    return pltpu.make_async_remote_copy(
        src_ref=src, dst_ref=dst, send_sem=s, recv_sem=r, device_id=device, device_id_type=MESH
    )


def loop(first, last, body):
    def run(i, carry):
        body(i)
        return carry

    lax.fori_loop(first, last, run, 0)


class Sums:
    def __init__(self, own, out, pair, recv1, sum1, recv2, recv3, fin, result, sems, pair_sems):
        self.own, self.out, self.pair = own, out, pair
        self.recv1, self.sum1, self.recv2, self.recv3, self.fin = recv1, sum1, recv2, recv3, fin
        self.result, self.sems, self.pair_sems = result, sems, pair_sems
        self.place, self.core = position()
        self.partner = device_at(self.place, 1 - self.core)
        self.base = self.core * own.shape[0]

    def flags(self, u, level):
        turn = lax.rem(u + level, 3) if not isinstance(u, int) else (u + level) % 3
        first, last = (2 - turn) // 2, turn // 2
        return first, 1 - first - last, last

    def peer(self, u, level, step):
        flags = self.flags(u, level)
        return device_at([lax.rem(at + flag * step, 4) for at, flag in zip(self.place, flags)], self.core)

    def mine(self, u, level):
        x, y, z = (at * flag for at, flag in zip(self.place, self.flags(u, level)))
        return x + y + z

    def rows(self, u):
        return pl.ds(pl.multiple_of(u * 256, 256), 256)

    def rows1(self, u, at):
        return pl.ds(pl.multiple_of(u * 256 + at * 64, 64), 64)

    def result_rows(self, u, level):
        at = self.base + u * 256
        if level < 0:
            return pl.ds(pl.multiple_of(at, 256), 256)
        at = at + self.mine(u, 0) * 64
        if level == 0:
            return pl.ds(pl.multiple_of(at, 64), 64)
        return pl.ds(pl.multiple_of(at + self.mine(u, 1) * 16, 16), 16)

    def down(self, u, level, step):
        s, r = self.sems.at[u, 0, level], self.sems.at[u, 1, level]
        device = self.peer(u, level, step)
        if level == 0:
            there = lax.rem(self.mine(u, 0) + step, 4)
            return remote(self.out.at[self.rows1(u, there)], self.recv1.at[u, step - 1], s, r, device)
        if level == 1:
            there = lax.rem(self.mine(u, 1) + step, 4)
            rows = pl.ds(pl.multiple_of(there * 16, 16), 16)
            return remote(self.sum1.at[u, rows], self.recv2.at[u, step - 1], s, r, device)
        slot = self.recv3.at[u, self.mine(u, 2)]
        return remote(slot, slot, s, r, device)

    def up(self, u, level, step):
        s, r = self.sems.at[u, 2, level], self.sems.at[u, 3, level]
        rows = self.result.at[self.result_rows(u, level)]
        return remote(self.fin.at[u] if level == 1 else rows, rows, s, r, self.peer(u, level, step))

    def hand(self, u):
        rows = self.rows(u)
        return remote(
            self.out.at[rows], self.pair.at[rows], self.pair_sems.at[u, 0], self.pair_sems.at[u, 1], self.partner
        )

    def hand_back(self, u):
        rows = self.result.at[self.result_rows(u, -1)]
        return remote(rows, rows, self.pair_sems.at[u, 2], self.pair_sems.at[u, 3], self.partner)

    def keep(self, u):
        return pltpu.make_async_copy(self.fin.at[u], self.result.at[self.result_rows(u, 1)], self.pair_sems.at[u, 4])

    def done(self, u, kind, level):
        if kind < 2:
            three = (self.recv1.at[u], self.recv2.at[u], self.recv3.at[u, pl.ds(0, 3)])[level]
        else:
            three = (self.recv1.at[u], self.recv1.at[u, 0, pl.ds(0, 48)])[level]
        pltpu.make_async_copy(three, three, self.sems.at[u, kind, level]).wait()

    def send(self, make, u, level):
        for step in (1, 2, 3):
            make(u, level, step).start()

    def begin(self, u):
        self.hand(u).wait()
        rows = self.rows(u)
        total = self.own[rows, :] + self.pair[rows, :].astype(F32)
        self.own[rows, :] = total
        self.out[rows, :] = total.astype(BF16)
        self.send(self.down, u, 0)

    def second(self, u):
        self.done(u, 1, 0)
        rows = self.rows1(u, self.mine(u, 0))
        self.sum1[u] = (self.own[rows, :] + self.recv1[u, 0].astype(F32)) + (
            self.recv1[u, 1].astype(F32) + self.recv1[u, 2].astype(F32)
        )
        self.send(self.down, u, 1)

    def third(self, u):
        self.done(u, 1, 1)
        rows = pl.ds(pl.multiple_of(self.mine(u, 1) * 16, 16), 16)
        self.recv3[u, self.mine(u, 2)] = (self.sum1[u, rows, :] + self.recv2[u, 0]) + (
            self.recv2[u, 1] + self.recv2[u, 2]
        )
        self.send(self.down, u, 2)

    def gather(self, u):
        self.done(u, 1, 2)
        total = (self.recv3[u, 0] + self.recv3[u, 1]) + (self.recv3[u, 2] + self.recv3[u, 3])
        self.fin[u] = (total * SCALE).astype(BF16)
        self.keep(u).start()
        self.send(self.up, u, 1)

    def gather_next(self, u):
        self.keep(u).wait()
        self.done(u, 3, 1)
        self.send(self.up, u, 0)

    def gather_pair(self, u):
        self.done(u, 3, 0)
        self.hand_back(u).start()

    def end(self, u):
        for level in range(3):
            self.done(u, 0, level)
        for level in range(2):
            self.done(u, 2, level)
        self.hand_back(u).wait()

    def stages(self):
        return (self.begin, self.second, self.third, self.gather, self.gather_next, self.gather_pair)


def block_kernel(
    tok, cot, rim_in, into, rim_back, back_last, valid, w_qkv_h, w_out_h, w_up_h, w_down_h, gains,
    r1, r2, r3, gains_out, out_win, gtok_win, lon_rims, lat_blocks,
    w_qkv, w_out, w_up, w_down, lat_t, lat_c, rim_t, rim_c, pack_t, pack_c, key_bias,
    x_ref, c_ref, lowered, context, hid, hid_t, c_t, g_ctx, packed, g_pack, src, mixed, acc_out, acc_in,
    *rest_refs,
):
    place, core = position()
    lon, lat = lax.axis_index("lon"), lax.axis_index("lat")
    n_lon, n_lat = lax.axis_size("lon"), lax.axis_size("lat")
    lon_m, lon_p = lax.rem(lon + n_lon - 1, n_lon), lax.rem(lon + 1, n_lon)
    lat_m, lat_p = lax.rem(lat + n_lat - 1, n_lat), lax.rem(lat + 1, n_lat)
    partner = device_at(place, 1 - core)
    gain_a = gains[0:1, :]
    gain_b = gains[1:2, :]
    masks = head_masks()
    refs = iter(rest_refs)
    results = (r1, r2, r3)
    sum_a, sum_b, sum_c = (
        Sums(*[next(refs) for _ in range(8)], results[k], next(refs), next(refs)) for k in range(3)
    )
    (rims, send_blocks, gain_slots, gain_part,
     load_sem, halo_s, halo_r, back_s, back_r, gain_s, gain_r) = refs

    def peer(axis, step):
        there = list(place)
        there[axis] = lax.rem(place[axis] + step, 4)
        return device_at(there, core)

    barrier = pltpu.get_barrier_semaphore()
    greet = [(lon, lat_m), (lon, lat_p), (lon_m, lat), (lon_p, lat), (lon_m, lat_m), (lon_p, lat_p), partner]
    greet += [peer(axis, step) for axis in range(3) for step in (1, 2, 3)]
    for device in greet:
        pl.semaphore_signal(barrier, inc=1, device_id=device, device_id_type=MESH)
    loads = [
        pltpu.make_async_copy(a, b, load_sem.at[k])
        for k, (a, b) in enumerate(
            ((tok, context), (cot, out_win), (w_out_h, w_out), (w_up_h, w_up), (w_down_h, w_down))
        )
    ]
    loads += [
        pltpu.make_async_copy(
            w_qkv_h.at[:, pl.ds(part * D + pair * 128, 128)],
            w_qkv.at[:, pl.ds(pair * 384 + part * 128, 128)],
            load_sem.at[5 + part * 4 + pair],
        )
        for part in range(3)
        for pair in range(4)
    ]
    for copy in loads:
        copy.start()
    loads[0].wait()
    pack_t[...] = mm(rim_in[...], context[...]).astype(BF16)
    pl.semaphore_wait(barrier, len(greet))

    halos = []
    rest = pl.ds(PIECE, 3 * PIECE)
    corner = pl.ds(0, PIECE)

    def send_halos(pack, rim, lat_rim, full):
        wanted = [
            (pack.at[rest], rim.at[rest], (lon_m, lat)),
            (pack.at[corner], rim.at[corner], (lon_m, lat_m)),
        ]
        for lev in range(2):
            wanted.append(
                (full.at[pl.ds(lev * HALF, BLOCK)], lat_rim.at[pl.ds(lev * BLOCK, BLOCK)], (lon, lat_m))
            )
        for a, b, device in wanted:
            k = len(halos)
            halos.append(remote(a, b, halo_s.at[k], halo_r.at[k], device))
            halos[k].start()

    send_halos(pack_t, rim_t, lat_t, context)
    usable = jnp.where(valid[...] == 1, 1.0, 0.0).astype(BF16)
    spot = lax.broadcasted_iota(jnp.int32, (WIN, COLS), 0)
    lane = lax.broadcasted_iota(jnp.int32, (WIN, COLS), 1)
    for wr in range(2):
        lat_at = wr * 12 + ((spot // 36) % 2) * 6 + (spot // 6) % 6
        picked = mm(jnp.where(lane == lat_at, 1.0, 0.0).astype(BF16), usable)
        for k in range(4):
            ok = jnp.sum(jnp.where(lane == 6 * k + spot % 6, picked, 0.0), 1, keepdims=True)
            key_bias[(wr * 4 + k) * WIN:(wr * 4 + k + 1) * WIN, :] = jnp.where(ok > 0.5, 0.0, LOW)

    def own_rows(full, wr):
        for lev in range(2):
            if wr == 0:
                src[lev * 288:(lev + 1) * 288, :] = full[lev * HALF + 144:lev * HALF + 432, :]
            else:
                src[lev * 288:lev * 288 + 144, :] = full[lev * HALF + 432:lev * HALF + 576, :]

    def rim_rows(lat_rim, rim, wr):
        if wr == 0:
            src[HALF:, :] = rim[PIECE:3 * PIECE, :]
        else:
            for lev in range(2):
                src[lev * 288 + 144:(lev + 1) * 288, :] = lat_rim[lev * BLOCK:(lev + 1) * BLOCK, :]
            src[HALF:HALF + PIECE, :] = rim[3 * PIECE:, :]
            src[HALF + PIECE:, :] = rim[:PIECE, :]

    def enter(dst, wr, first, last, depth):
        for n in range(2):
            cols = slice(n * 256, (n + 1) * 256)
            dst[wr * HALF + first:wr * HALF + last, cols] = mm(into[first:last, :depth], src[:depth, cols]).astype(BF16)

    def attend(w):
        rows = pl.ds(pl.multiple_of(w * WIN, WIN), WIN)
        bias = window_bias(key_bias[rows, :], split_amount(w))
        for pair in range(4):
            lanes = slice(pair * 128, (pair + 1) * 128)
            query, key, value = (packed[rows, pair * 384 + k * 128:pair * 384 + (k + 1) * 128] for k in range(3))
            total = None
            for mask in masks:
                probs = scores_t(key, jnp.where(mask, query, 0), bias)
                part = mm_tn(probs.astype(BF16), jnp.where(mask, value, 0))
                total = part if total is None else total + part
            hid[rows, lanes] = total.astype(BF16)

    def first_part(first, last):
        band = slice(first * WIN, last * WIN)

        def first_norm(i):
            rows = pl.ds(pl.multiple_of(i * WIN, WIN), WIN)
            normed, _ = norm_stats(x_ref[rows, :].astype(F32))
            lowered[rows, :] = (normed * gain_a).astype(BF16)

        loop(first, last, first_norm)

        def project(n):
            cols = pl.ds(pl.multiple_of(n * 256, 256), 256)
            packed[band, cols] = mm(lowered[band, :], w_qkv[:, cols]).astype(BF16)

        loop(0, 6, project)
        loop(first, last, attend)

    own_rows(context, 0)
    enter(x_ref, 0, 0, 3 * WIN, HALF)
    for copy in loads[5:]:
        copy.wait()
    first_part(0, 3)
    loads[1].wait()
    pack_c[...] = mm(rim_in[...], out_win[...]).astype(BF16)
    send_halos(pack_c, rim_c, lat_c, out_win)
    for copy in halos[0:4]:
        copy.wait_recv()
    rim_rows(lat_t, rim_t, 0)
    enter(x_ref, 0, 3 * WIN, HALF, HALF + 2 * PIECE)
    own_rows(context, 1)
    rim_rows(lat_t, rim_t, 1)
    enter(x_ref, 1, 0, HALF, HALF + 2 * PIECE)
    first_part(3, 8)
    for copy in halos[4:8]:
        copy.wait_recv()
    for wr in range(2):
        own_rows(out_win, wr)
        rim_rows(lat_c, rim_c, wr)
        enter(c_ref, wr, 0, HALF, HALF + 2 * PIECE)
    for copy in halos:
        copy.wait_send()
    loads[2].wait()
    context[...] = hid[...]

    def second_norm(rows):
        attended = mm(context[rows, :], w_out[...]).astype(BF16)
        m = x_ref[rows, :].astype(F32) + attended.astype(F32)
        mixed[rows, :] = m
        normed, _ = norm_stats(m)
        hid[rows, :] = (normed * gain_b).astype(BF16)

    rows_loop(TOK, 288, second_norm)
    hid_t[...] = hid[...].T
    c_t[...] = c_ref[...].T
    acc_out[...] = jnp.zeros_like(acc_out)
    acc_in[...] = jnp.zeros_like(acc_in)
    loads[3].wait()
    loads[4].wait()

    def tick(t):
        for stage, lag in reversed(list(zip(sum_a.stages(), LAGS))):
            u = t - lag
            if isinstance(t, int):
                if 0 <= u < 8:
                    stage(u)
            else:
                @pl.when((u >= 0) & (u < 8))
                def _(stage=stage, u=u):
                    stage(u)

    def share(left, right, flip, own, out, at):
        rows = pl.ds(pl.multiple_of(at, 128), 128)
        for which, dst in ((core, own), (1 - core, out)):
            part = mm(left[pl.ds(pl.multiple_of(which * 256, 256), 256), :], right)
            if flip:
                part = part.T
            part = part.astype(dst.dtype)
            dst[rows, 0:256] = part[0:128]
            dst[rows, 256:512] = part[128:256]

    wide = 256

    def columns(n):
        cols = pl.ds(pl.multiple_of(n * wide, wide), wide)
        raised = mm(hid[...], w_up[:, cols])
        slope = np.float32(np.sqrt(2 / np.pi))
        square = raised * raised
        t = jnp.tanh(slope * (raised + np.float32(0.044715) * (square * raised)))
        cdf = 0.5 * (1.0 + t)
        activated = (raised * cdf).astype(BF16)
        deriv = cdf + 0.5 * raised * (1.0 - t * t) * (slope * (1.0 + np.float32(3 * 0.044715) * square))
        grad_act = mm_nt(c_ref[...], w_down[cols, :])
        grad_raised = (grad_act * deriv).astype(BF16)
        acc_out[...] += mm(activated, w_down[cols, :])
        acc_in[...] += mm_nt(grad_raised, w_up[:, cols])
        share(hid_t, grad_raised, False, sum_a.own, sum_a.out, n * 256)
        share(c_t, activated, True, sum_a.own, sum_a.out, n * 256 + 128)
        sum_a.hand(n).start()
        tick(n)

    loop(0, FF // wide, columns)
    tick(8)
    gain_part[...] = jnp.zeros_like(gain_part)

    def finish(rows):
        m = mixed[rows, :]
        out_win[rows, :] = (m + acc_out[rows, :]).astype(BF16)
        normed, inv_std = norm_stats(m)
        grad_in = acc_in[rows, :]
        gain_part[1:2, :] += jnp.sum(grad_in * normed, 0, keepdims=True)
        g = c_ref[rows, :].astype(F32) + norm_back(grad_in, normed, inv_std, gain_b)
        acc_in[rows, :] = g
        g = g.astype(BF16)
        hid[rows, :] = g
        g_ctx[rows, :] = mm_nt(g, w_out[...]).astype(BF16)

    rows_loop(TOK, WIN, finish)
    backs = []

    def send_back(k, win):
        for wr in range(2):
            at = (k * 2 + wr) * 2 * PIECE
            rims[at:at + 2 * PIECE, :] = mm(rim_back[...], win[wr * HALF:(wr + 1) * HALF, :]).astype(BF16)
        send_blocks[k * 2 * BLOCK:(k + 1) * 2 * BLOCK, :] = mm(back_last[...], win[HALF:, :]).astype(BF16)
        near = pl.ds(k * 4 * PIECE, 3 * PIECE)
        far = pl.ds(k * 4 * PIECE + 3 * PIECE, PIECE)
        blocks = pl.ds(k * 2 * BLOCK, 2 * BLOCK)
        for a, b, device in (
            (send_blocks.at[blocks], lat_blocks.at[blocks], (lon, lat_p)),
            (rims.at[near], lon_rims.at[near], (lon_p, lat)),
            (rims.at[far], lon_rims.at[far], (lon_p, lat_p)),
        ):
            n = len(backs)
            backs.append(remote(a, b, back_s.at[n], back_r.at[n], device))
            backs[n].start()

    send_back(0, out_win)
    gmix, g_att = acc_in, hid

    tick(9)
    hid_t[...] = lowered[...].T
    c_t[...] = context[...].T
    for which, dst in ((core, sum_c.own), (1 - core, sum_c.out)):
        part = mm(c_t[pl.ds(pl.multiple_of(which * 256, 256), 256), :], g_att[...])
        dst[...] = part.astype(dst.dtype)
    sum_c.hand(0).start()
    tick(10)

    def attend_back(w, pair):
        rows = pl.ds(pl.multiple_of(w * WIN, WIN), WIN)
        bias = window_bias(key_bias[rows, :], split_amount(w))
        lanes = [pl.ds(pl.multiple_of(pair * 384 + k * 128, 128), 128) for k in range(3)]
        query, key, value = (packed[rows, at] for at in lanes)
        grad = g_ctx[rows, pl.ds(pl.multiple_of(pair * 128, 128), 128)]
        sums = [None, None, None]
        for mask in masks:
            query_m = jnp.where(mask, query, 0)
            grad_m = jnp.where(mask, grad, 0)
            probs = scores_t(key, query_m, bias)
            g_weights = mm_nt(value, grad_m)
            inner = jnp.sum(probs * g_weights, 0, keepdims=True)
            g_scores = (probs * (g_weights - inner) * HEAD ** (-0.5)).astype(BF16)
            parts = (
                mm_tn(g_scores, jnp.where(mask, key, 0)),
                mm(g_scores, query_m),
                mm(probs.astype(BF16), grad_m),
            )
            sums = [b if a is None else a + b for a, b in zip(sums, parts)]
        for at, value in zip(lanes, sums):
            g_pack[rows, at] = value.astype(BF16)

    both = (sum_b, sum_c)

    def heads(pair):
        def some(k):
            for w in range(4):
                attend_back(k * 4 + w, pair)
            now = 2 * pair + k
            for when, which, stage, u in LATE:
                @pl.when(now == when)
                def _(which=which, stage=stage, u=u):
                    both[which].stages()[stage](u)

            tick(11 + now)

        loop(0, 2, some)
        cols = pl.ds(pl.multiple_of(pair * 384, 384), 384)
        rows = pl.ds(pl.multiple_of(pair * 256, 256), 256)
        for which, dst in ((core, sum_b.own), (1 - core, sum_b.out)):
            part = mm(hid_t[pl.ds(pl.multiple_of(which * 256, 256), 256), :], g_pack[:, cols])
            dst[rows, :] = part.astype(dst.dtype)
        sum_b.hand(pair).start()

    loop(0, 4, heads)
    tick(19)

    def finish_back(rows):
        g_low = mm_nt(g_pack[rows, :], w_qkv[...]).astype(BF16).astype(F32)
        normed, inv_std = norm_stats(x_ref[rows, :].astype(F32))
        gain_part[0:1, :] += jnp.sum(g_low * normed, 0, keepdims=True)
        gtok_win[rows, :] = (gmix[rows, :] + norm_back(g_low, normed, inv_std, gain_a)).astype(BF16)

    def later(phase):
        for which, stage, u in PHASES[phase]:
            both[which].stages()[stage](u)

    rows_loop(TOK // 2, 288, finish_back)
    later(0)
    tick(20)
    rows_loop(TOK // 2, 288, lambda rows: finish_back(pl.ds(pl.multiple_of(rows.start + TOK // 2, 288), 288)))
    send_back(1, gtok_win)
    later(1)
    tick(21)
    gain_slots[0, 0] = gain_part[...]
    gain_pair = remote(gain_slots.at[0, 0], gain_slots.at[0, 1], gain_s.at[0, 0], gain_r.at[0, 0], partner)
    gain_pair.start()
    def gains_along(level, total):
        axis = level - 1
        slot = gain_slots.at[level, place[axis]]
        gain_slots[level, place[axis]] = total
        copies = [
            remote(slot, slot, gain_s.at[level, step - 1], gain_r.at[level, step - 1], peer(axis, step))
            for step in (1, 2, 3)
        ]
        for copy in copies:
            copy.start()
        return copies

    def gains_sum(level, copies):
        for copy in copies:
            copy.wait()
        return (gain_slots[level, 0] + gain_slots[level, 1]) + (gain_slots[level, 2] + gain_slots[level, 3])

    gain_pair.wait()
    gain_copies = gains_along(1, gain_slots[0, 0] + gain_slots[0, 1])
    later(2)
    gain_copies = gains_along(2, gains_sum(1, gain_copies))
    later(3)
    gain_copies = gains_along(3, gains_sum(2, gain_copies))
    later(4)
    gains_out[...] = gains_sum(3, gain_copies) * SCALE
    later(5)
    loop(0, 8, sum_a.end)
    sum_c.end(0)
    loop(0, 4, sum_b.end)
    for copy in backs:
        copy.wait()


LAGS = (1, 4, 6, 8, 10, 13)
LATE = (
    (0, 1, 0, 0), (2, 1, 1, 0), (4, 1, 2, 0), (6, 1, 3, 0),
    (6, 0, 2, 0), (4, 0, 1, 0), (2, 0, 0, 0), (6, 0, 1, 1), (4, 0, 0, 1), (6, 0, 0, 2),
)
PHASES = (
    ((1, 4, 0), (0, 3, 0), (0, 2, 1), (0, 1, 2), (0, 0, 3)),
    ((1, 5, 0), (0, 4, 0), (0, 3, 1), (0, 2, 2), (0, 1, 3)),
    ((0, 5, 0), (0, 4, 1), (0, 3, 2), (0, 2, 3)),
    ((0, 5, 1), (0, 4, 2), (0, 3, 3)),
    ((0, 5, 2), (0, 4, 3)),
    ((0, 5, 3),),
)


def sums_scratch(units, lanes):
    vmem = pltpu.VMEM
    return [
        vmem((units * 256, lanes), F32), vmem((units * 256, lanes), BF16), vmem((units * 256, lanes), BF16),
        vmem((units, 3, 64, lanes), BF16), vmem((units, 64, lanes), F32), vmem((units, 3, 16, lanes), F32),
        vmem((units, 4, 16, lanes), F32), vmem((units, 16, lanes), BF16),
        pltpu.SemaphoreType.DMA((units, 4, 3)), pltpu.SemaphoreType.DMA((units, 5)),
    ]


def block(*args):
    vm = pl.BlockSpec(memory_space=pltpu.VMEM)
    hbm = pl.BlockSpec(memory_space=pl.ANY)
    shape = jax.ShapeDtypeStruct
    dma = pltpu.SemaphoreType.DMA
    vmem = pltpu.VMEM
    field = vmem((TOK, D), BF16)
    field_t = vmem((D, TOK), BF16)
    wide = vmem((TOK, D), F32)
    rim = vmem((4 * PIECE, D), BF16)
    lat_rim = vmem((2 * BLOCK, D), BF16)
    return pl.pallas_call(
        block_kernel,
        out_shape=(
            shape((2 * FF, D), BF16),
            shape((4 * D, 384), BF16),
            shape((D, D), BF16),
            shape((8, D), F32),
            shape((TOK, D), BF16),
            shape((TOK, D), BF16),
            shape((8 * PIECE, D), BF16),
            shape((4 * BLOCK, D), BF16),
        ),
        in_specs=[hbm, hbm] + [vm] * 5 + [hbm] * 4 + [vm],
        out_specs=(hbm,) * 3 + (vm,) * 5,
        scratch_shapes=[
            vmem((D, 3 * D), BF16), vmem((D, D), BF16), vmem((D, FF), BF16), vmem((FF, D), BF16),
            lat_rim, lat_rim, rim, rim, rim, rim, vmem((TOK, 1), F32),
            field, field, field, field, field, field_t, field_t, field,
            vmem((TOK, 3 * D), BF16), vmem((TOK, 3 * D), BF16), vmem((HALF + 2 * PIECE, D), BF16),
            wide, wide, wide,
            *sums_scratch(8, D), *sums_scratch(4, 384), *sums_scratch(1, D),
            vmem((8 * PIECE, D), BF16), vmem((4 * BLOCK, D), BF16), vmem((4, 4, 8, D), F32), vmem((8, D), F32),
            dma((17,)), dma((8,)), dma((8,)), dma((6,)), dma((6,)), dma((4, 3)), dma((4, 3)),
        ],
        compiler_params=pltpu.CompilerParams(collective_id=0, has_side_effects=True, vmem_limit_bytes=VMEM_BYTES),
        name="block",
    )(*args)


def finish_kernel(
    r1, r2, r3, gain_sums, out_win, gtok_win, lon_rims, lat_blocks, back,
    outputs, g_tok, g_qkv, g_out, g_up, g_down, g_gains,
    v1, v2, v3, w1, w2, rims, blocks, src, full, f_up, f_down, f_qkv, f_out, sem_in, sem_out,
):
    loads = [
        pltpu.make_async_copy(a, b, sem_in.at[k])
        for k, (a, b) in enumerate(
            [(r1.at[pl.ds(core * FF + n * 1024, 1024)], v1.at[pl.ds(core * FF + n * 1024, 1024)])
             for n in range(2) for core in range(2)]
            + [(r2, v2), (r3, v3), (out_win, w1), (lon_rims, rims), (lat_blocks, blocks), (gtok_win, w2)]
        )
    ]
    for copy in loads:
        copy.start()
    stores = []

    def store(a, b):
        copy = pltpu.make_async_copy(a, b, sem_out.at[len(stores)])
        copy.start()
        stores.append(copy)

    g_gains[...] = gain_sums[0:2, :]
    for n in range(8):
        if n % 4 == 0:
            loads[n // 2].wait()
            loads[n // 2 + 1].wait()
        for core in range(2):
            for k in range(2):
                lanes = slice(k * 256, (k + 1) * 256)
                at = core * FF + n * 256
                f_up[core * 256 + k * 128:core * 256 + (k + 1) * 128, n * 256:(n + 1) * 256] = (
                    v1[at:at + 128, lanes].astype(F32)
                )
                f_down[n * 256 + k * 128:n * 256 + (k + 1) * 128, core * 256:(core + 1) * 256] = (
                    v1[at + 128:at + 256, lanes].astype(F32)
                )
        if n % 2:
            cols = pl.ds((n - 1) * 256, 512)
            store(f_up.at[:, cols], g_up.at[:, cols])
            store(f_down.at[cols], g_down.at[cols])
    loads[4].wait()
    for part in range(3):
        for pair in range(4):
            for core in range(2):
                f_qkv[core * 256:(core + 1) * 256, part * D + pair * 128:part * D + (pair + 1) * 128] = (
                    v2[core * 1024 + pair * 256:core * 1024 + (pair + 1) * 256, part * 128:(part + 1) * 128].astype(F32)
                )
        cols = pl.ds(part * D, D)
        store(f_qkv.at[:, cols], g_qkv.at[:, cols])
    loads[5].wait()
    f_out[...] = v3[...].astype(F32)
    store(f_out, g_out)
    for copy in loads[6:]:
        copy.wait()
    for k, (win, out) in enumerate(((w1, outputs), (w2, g_tok))):
        for wr in range(2):
            at = (k * 2 + wr) * 2 * PIECE
            src[:HALF, :] = win[wr * HALF:(wr + 1) * HALF, :]
            src[HALF:, :] = rims[at:at + 2 * PIECE, :]
            for lev in range(2):
                if wr == 0:
                    pick, length = slice(lev * 288, (lev + 1) * 288), 288
                    to = lev * HALF + 144
                else:
                    pick, length = slice(lev * 288, lev * 288 + 144), 144
                    to = lev * HALF + 432
                full[k, to:to + length, :] = mm(back[pick, :], src[...]).astype(BF16)
        for lev in range(2):
            edge = mm(back[lev * 288 + BLOCK:(lev + 1) * 288, HALF:], src[HALF:, :])
            inner = blocks[(k * 2 + lev) * BLOCK:(k * 2 + lev + 1) * BLOCK, :].astype(F32)
            full[k, lev * HALF:lev * HALF + BLOCK, :] = (inner + edge).astype(BF16)
        store(full.at[k], out)
    for copy in stores:
        copy.wait()


def finish_all(*args):
    vm = pl.BlockSpec(memory_space=pltpu.VMEM)
    hbm = pl.BlockSpec(memory_space=pl.ANY)
    shape = jax.ShapeDtypeStruct
    vmem = pltpu.VMEM
    return pl.pallas_call(
        finish_kernel,
        out_shape=(
            shape((TOK, D), BF16),
            shape((TOK, D), BF16),
            shape((D, 3 * D), F32),
            shape((D, D), F32),
            shape((D, FF), F32),
            shape((FF, D), F32),
            shape((2, D), F32),
        ),
        in_specs=[hbm] * 3 + [vm] + [hbm] * 4 + [vm],
        out_specs=(hbm,) * 6 + (vm,),
        scratch_shapes=[
            vmem((2 * FF, D), BF16), vmem((4 * D, 384), BF16), vmem((D, D), BF16), vmem((TOK, D), BF16),
            vmem((TOK, D), BF16), vmem((8 * PIECE, D), BF16), vmem((4 * BLOCK, D), BF16),
            vmem((HALF + 2 * PIECE, D), BF16), vmem((2, TOK, D), BF16),
            vmem((D, FF), F32), vmem((FF, D), F32), vmem((D, 3 * D), F32), vmem((D, D), F32),
            pltpu.SemaphoreType.DMA((10,)), pltpu.SemaphoreType.DMA((14,)),
        ],
        compiler_params=pltpu.CompilerParams(vmem_limit_bytes=VMEM_BYTES),
        name="finish",
    )(*args)


def on_device(tokens, cotangent, valid, w_qkv, w_out, w_up, w_down, gains):
    into, back, rim_in, rim_back = gather_maps()
    tok = tokens.reshape(TOK, D)
    cot = cotangent.reshape(TOK, D)
    back_last = jnp.concatenate([back[BLOCK:2 * BLOCK, :HALF], back[3 * BLOCK:, :HALF]], 0)
    *sums, out_win, gtok_win, lon_rims, lat_blocks = block(
        tok, cot, rim_in, into, rim_back, back_last, valid, w_qkv, w_out, w_up, w_down, gains
    )
    outputs, g_tok, g_qkv, g_out, g_up, g_down, g_gains = finish_all(
        *sums, out_win, gtok_win, lon_rims, lat_blocks, back
    )
    return (
        outputs.reshape(tokens.shape),
        g_tok.reshape(tokens.shape),
        g_qkv,
        g_out,
        g_up,
        g_down,
        g_gains,
    )


def solution(mesh):
    field = P(None, "lat", "lon", None)
    in_specs = (field, field, P("lat", "lon"), P(), P(), P(), P(), P())
    out_specs = (field, field, P(), P(), P(), P(), P())
    return jax.shard_map(on_device, mesh=mesh, in_specs=in_specs, out_specs=out_specs, check_vma=False)
```

```python
import jax
import jax.numpy as jnp
import numpy as np
from jax import lax
from jax.experimental import pallas as pl
from jax.experimental.pallas import tpu as pltpu
from jax.sharding import PartitionSpec as P

F32 = jnp.float32
BF16 = jnp.bfloat16
MESH = pl.DeviceIdType.MESH
HEAD = 64
WIN = 144
TOK = 1152
HALF = 576
D = 512
FF = 2048
COLS = 24
BLOCK = 144
PIECE = 48
epsilon = 1e-05
LOW = -1e30
SCALE = np.float32(147456 ** (-0.5))
VMEM_BYTES = 63 * 1024 * 1024


def gather_maps():
    into = np.zeros((HALF, HALF + 2 * PIECE), np.float32)
    back = np.zeros((HALF, HALF + 2 * PIECE), np.float32)
    rim_in = np.zeros((4 * PIECE, TOK), np.float32)
    rim_back = np.zeros((2 * PIECE, HALF), np.float32)
    for lev in range(2):
        for half in range(2):
            for r in range(6):
                for col in range(COLS):
                    window = (col // 6) * WIN + lev * 72 + half * 36 + r * 6 + col % 6
                    chunk = (lev * 2 + half) * BLOCK + r * COLS
                    if col + 3 < COLS:
                        into[window, chunk + col + 3] = 1
                        back[chunk + col + 3, window] = 1
                    else:
                        rim = half * PIECE + lev * 18 + r * 3 + col + 3 - COLS
                        into[window, HALF + rim] = 1
                        back[chunk + col + 3 - COLS, HALF + rim] = 1
                        rim_back[rim, window] = 1
    for lev in range(2):
        for block in range(4):
            for r in range(6):
                for col in range(3):
                    rim_in[block * PIECE + lev * 18 + r * 3 + col, lev * HALF + block * BLOCK + r * COLS + col] = 1
    return [jnp.asarray(m, BF16) for m in (into, back, rim_in, rim_back)]


def mm(a, b):
    return lax.dot_general(a, b, (((1,), (0,)), ((), ())), preferred_element_type=F32)


def mm_nt(a, b):
    return lax.dot_general(a, b, (((1,), (1,)), ((), ())), preferred_element_type=F32)


def mm_tn(a, b):
    return lax.dot_general(a, b, (((0,), (0,)), ((), ())), preferred_element_type=F32)


def norm_stats(values):
    centred = values - jnp.mean(values, -1, keepdims=True)
    inv_std = lax.rsqrt(jnp.mean(centred * centred, -1, keepdims=True) + epsilon)
    return centred * inv_std, inv_std


def norm_back(grad_value, normed, inv_std, gain_row):
    scaled = grad_value * gain_row
    return inv_std * (
        scaled
        - jnp.mean(scaled, -1, keepdims=True)
        - normed * jnp.mean(scaled * normed, -1, keepdims=True)
    )


def rows_loop(total, step, body):
    def run(i, carry):
        body(pl.ds(pl.multiple_of(i * step, step), step))
        return carry

    lax.fori_loop(0, total // step, run, 0)


def window_bias(key_bias, split):
    rows = lax.broadcasted_iota(jnp.int32, (WIN, WIN), 0)
    cols = lax.broadcasted_iota(jnp.int32, (WIN, WIN), 1)
    bias = jnp.where(rows == cols, 0.0, jnp.broadcast_to(key_bias, (WIN, WIN)))
    apart = ((rows // 36) % 2) != ((cols // 36) % 2)
    return bias + jnp.where(apart, split, 0.0)


def scores_t(key2, query_m, bias):
    return mm_nt(key2, query_m) + bias


def head_masks():
    lane = lax.broadcasted_iota(jnp.int32, (WIN, 128), 1)
    return [lane < HEAD, lane >= HEAD]


def split_amount(window):
    last = (lax.axis_index("lat") == lax.axis_size("lat") - 1) & (window >= 4)
    return jnp.where(last, LOW, 0.0).astype(F32)


def position():
    lon, lat = lax.axis_index("lon"), lax.axis_index("lat")
    y = lax.rem(lax.div(lat, 2), 2) * 2 + lax.rem(lon, 2)
    return [lax.div(lon, 2), y, lax.div(lat, 4)], lax.rem(lat, 2)


def device_at(place, core):
    x, y, z = place
    return (x * 2 + lax.rem(y, 2), z * 4 + lax.div(y, 2) * 2 + core)


def remote(src, dst, s, r, device):
    return pltpu.make_async_remote_copy(
        src_ref=src, dst_ref=dst, send_sem=s, recv_sem=r, device_id=device, device_id_type=MESH
    )


def loop(first, last, body):
    def run(i, carry):
        body(i)
        return carry

    lax.fori_loop(first, last, run, 0)


class Sums:
    def __init__(self, own, out, pair, recv1, sum1, recv2, recv3, fin, result, sems, pair_sems):
        self.own, self.out, self.pair = own, out, pair
        self.recv1, self.sum1, self.recv2, self.recv3, self.fin = recv1, sum1, recv2, recv3, fin
        self.result, self.sems, self.pair_sems = result, sems, pair_sems
        self.place, self.core = position()
        self.partner = device_at(self.place, 1 - self.core)
        self.base = self.core * own.shape[0]

    def flags(self, u, level):
        turn = lax.rem(u + level, 3) if not isinstance(u, int) else (u + level) % 3
        first, last = (2 - turn) // 2, turn // 2
        return first, 1 - first - last, last

    def peer(self, u, level, step):
        flags = self.flags(u, level)
        return device_at([lax.rem(at + flag * step, 4) for at, flag in zip(self.place, flags)], self.core)

    def mine(self, u, level):
        x, y, z = (at * flag for at, flag in zip(self.place, self.flags(u, level)))
        return x + y + z

    def rows(self, u):
        return pl.ds(pl.multiple_of(u * 256, 256), 256)

    def rows1(self, u, at):
        return pl.ds(pl.multiple_of(u * 256 + at * 64, 64), 64)

    def result_rows(self, u, level):
        at = self.base + u * 256
        if level < 0:
            return pl.ds(pl.multiple_of(at, 256), 256)
        at = at + self.mine(u, 0) * 64
        if level == 0:
            return pl.ds(pl.multiple_of(at, 64), 64)
        return pl.ds(pl.multiple_of(at + self.mine(u, 1) * 16, 16), 16)

    def down(self, u, level, step):
        s, r = self.sems.at[u, 0, level], self.sems.at[u, 1, level]
        device = self.peer(u, level, step)
        if level == 0:
            there = lax.rem(self.mine(u, 0) + step, 4)
            return remote(self.out.at[self.rows1(u, there)], self.recv1.at[u, step - 1], s, r, device)
        if level == 1:
            there = lax.rem(self.mine(u, 1) + step, 4)
            rows = pl.ds(pl.multiple_of(there * 16, 16), 16)
            return remote(self.sum1.at[u, rows], self.recv2.at[u, step - 1], s, r, device)
        slot = self.recv3.at[u, self.mine(u, 2)]
        return remote(slot, slot, s, r, device)

    def up(self, u, level, step):
        s, r = self.sems.at[u, 2, level], self.sems.at[u, 3, level]
        rows = self.result.at[self.result_rows(u, level)]
        return remote(self.fin.at[u] if level == 1 else rows, rows, s, r, self.peer(u, level, step))

    def hand(self, u):
        rows = self.rows(u)
        return remote(
            self.out.at[rows], self.pair.at[rows], self.pair_sems.at[u, 0], self.pair_sems.at[u, 1], self.partner
        )

    def hand_back(self, u):
        rows = self.result.at[self.result_rows(u, -1)]
        return remote(rows, rows, self.pair_sems.at[u, 2], self.pair_sems.at[u, 3], self.partner)

    def keep(self, u):
        return pltpu.make_async_copy(self.fin.at[u], self.result.at[self.result_rows(u, 1)], self.pair_sems.at[u, 4])

    def done(self, u, kind, level):
        if kind < 2:
            three = (self.recv1.at[u], self.recv2.at[u], self.recv3.at[u, pl.ds(0, 3)])[level]
        else:
            three = (self.recv1.at[u], self.recv1.at[u, 0, pl.ds(0, 48)])[level]
        pltpu.make_async_copy(three, three, self.sems.at[u, kind, level]).wait()

    def send(self, make, u, level):
        for step in (1, 2, 3):
            make(u, level, step).start()

    def begin(self, u):
        self.hand(u).wait()
        rows = self.rows(u)
        total = self.own[rows, :] + self.pair[rows, :].astype(F32)
        self.own[rows, :] = total
        self.out[rows, :] = total.astype(BF16)
        self.send(self.down, u, 0)

    def second(self, u):
        self.done(u, 1, 0)
        rows = self.rows1(u, self.mine(u, 0))
        self.sum1[u] = (self.own[rows, :] + self.recv1[u, 0].astype(F32)) + (
            self.recv1[u, 1].astype(F32) + self.recv1[u, 2].astype(F32)
        )
        self.send(self.down, u, 1)

    def third(self, u):
        self.done(u, 1, 1)
        rows = pl.ds(pl.multiple_of(self.mine(u, 1) * 16, 16), 16)
        self.recv3[u, self.mine(u, 2)] = (self.sum1[u, rows, :] + self.recv2[u, 0]) + (
            self.recv2[u, 1] + self.recv2[u, 2]
        )
        self.send(self.down, u, 2)

    def gather(self, u):
        self.done(u, 1, 2)
        total = (self.recv3[u, 0] + self.recv3[u, 1]) + (self.recv3[u, 2] + self.recv3[u, 3])
        self.fin[u] = (total * SCALE).astype(BF16)
        self.keep(u).start()
        self.send(self.up, u, 1)

    def gather_next(self, u):
        self.keep(u).wait()
        self.done(u, 3, 1)
        self.send(self.up, u, 0)

    def gather_pair(self, u):
        self.done(u, 3, 0)
        self.hand_back(u).start()

    def end(self, u):
        for level in range(3):
            self.done(u, 0, level)
        for level in range(2):
            self.done(u, 2, level)
        self.hand_back(u).wait()

    def stages(self):
        return (self.begin, self.second, self.third, self.gather, self.gather_next, self.gather_pair)


def block_kernel(
    tok, cot, rim_in, into, rim_back, back_last, valid, w_qkv_h, w_out_h, w_up_h, w_down_h, gains,
    r1, r2, r3, gains_out, out_win, gtok_win, lon_rims, lat_blocks,
    w_qkv, w_out, w_up, w_down, lat_t, lat_c, rim_t, rim_c, pack_t, pack_c, key_bias, log_sum,
    x_ref, c_ref, lowered, context, hid, hid_t, c_t, g_ctx, packed, g_pack, src, mixed, acc_out, acc_in,
    *rest_refs,
):
    place, core = position()
    lon, lat = lax.axis_index("lon"), lax.axis_index("lat")
    n_lon, n_lat = lax.axis_size("lon"), lax.axis_size("lat")
    lon_m, lon_p = lax.rem(lon + n_lon - 1, n_lon), lax.rem(lon + 1, n_lon)
    lat_m, lat_p = lax.rem(lat + n_lat - 1, n_lat), lax.rem(lat + 1, n_lat)
    partner = device_at(place, 1 - core)
    gain_a = gains[0:1, :]
    gain_b = gains[1:2, :]
    masks = head_masks()
    refs = iter(rest_refs)
    results = (r1, r2, r3)
    sum_a, sum_b, sum_c = (
        Sums(*[next(refs) for _ in range(8)], results[k], next(refs), next(refs)) for k in range(3)
    )
    (rims, send_blocks, gain_slots, gain_part,
     load_sem, halo_s, halo_r, back_s, back_r, gain_s, gain_r) = refs

    def peer(axis, step):
        there = list(place)
        there[axis] = lax.rem(place[axis] + step, 4)
        return device_at(there, core)

    barrier = pltpu.get_barrier_semaphore()
    greet = [(lon, lat_m), (lon, lat_p), (lon_m, lat), (lon_p, lat), (lon_m, lat_m), (lon_p, lat_p), partner]
    greet += [peer(axis, step) for axis in range(3) for step in (1, 2, 3)]
    for device in greet:
        pl.semaphore_signal(barrier, inc=1, device_id=device, device_id_type=MESH)
    loads = [
        pltpu.make_async_copy(a, b, load_sem.at[k])
        for k, (a, b) in enumerate(
            ((tok, context), (cot, out_win), (w_out_h, w_out), (w_up_h, w_up), (w_down_h, w_down))
        )
    ]
    loads += [
        pltpu.make_async_copy(
            w_qkv_h.at[:, pl.ds(part * D + pair * 128, 128)],
            w_qkv.at[:, pl.ds(pair * 384 + part * 128, 128)],
            load_sem.at[5 + part * 4 + pair],
        )
        for part in range(3)
        for pair in range(4)
    ]
    for copy in loads:
        copy.start()
    loads[0].wait()
    pack_t[...] = mm(rim_in[...], context[...]).astype(BF16)
    pl.semaphore_wait(barrier, len(greet))

    halos = []
    rest = pl.ds(PIECE, 3 * PIECE)
    corner = pl.ds(0, PIECE)

    def send_halos(pack, rim, lat_rim, full):
        wanted = [
            (pack.at[rest], rim.at[rest], (lon_m, lat)),
            (pack.at[corner], rim.at[corner], (lon_m, lat_m)),
        ]
        for lev in range(2):
            wanted.append(
                (full.at[pl.ds(lev * HALF, BLOCK)], lat_rim.at[pl.ds(lev * BLOCK, BLOCK)], (lon, lat_m))
            )
        for a, b, device in wanted:
            k = len(halos)
            halos.append(remote(a, b, halo_s.at[k], halo_r.at[k], device))
            halos[k].start()

    send_halos(pack_t, rim_t, lat_t, context)
    usable = jnp.where(valid[...] == 1, 1.0, 0.0).astype(BF16)
    spot = lax.broadcasted_iota(jnp.int32, (WIN, COLS), 0)
    lane = lax.broadcasted_iota(jnp.int32, (WIN, COLS), 1)
    for wr in range(2):
        lat_at = wr * 12 + ((spot // 36) % 2) * 6 + (spot // 6) % 6
        picked = mm(jnp.where(lane == lat_at, 1.0, 0.0).astype(BF16), usable)
        for k in range(4):
            ok = jnp.sum(jnp.where(lane == 6 * k + spot % 6, picked, 0.0), 1, keepdims=True)
            key_bias[(wr * 4 + k) * WIN:(wr * 4 + k + 1) * WIN, :] = jnp.where(ok > 0.5, 0.0, LOW)

    def own_rows(full, wr):
        for lev in range(2):
            if wr == 0:
                src[lev * 288:(lev + 1) * 288, :] = full[lev * HALF + 144:lev * HALF + 432, :]
            else:
                src[lev * 288:lev * 288 + 144, :] = full[lev * HALF + 432:lev * HALF + 576, :]

    def rim_rows(lat_rim, rim, wr):
        if wr == 0:
            src[HALF:, :] = rim[PIECE:3 * PIECE, :]
        else:
            for lev in range(2):
                src[lev * 288 + 144:(lev + 1) * 288, :] = lat_rim[lev * BLOCK:(lev + 1) * BLOCK, :]
            src[HALF:HALF + PIECE, :] = rim[3 * PIECE:, :]
            src[HALF + PIECE:, :] = rim[:PIECE, :]

    def enter(dst, wr, first, last, depth):
        for n in range(2):
            cols = slice(n * 256, (n + 1) * 256)
            dst[wr * HALF + first:wr * HALF + last, cols] = mm(into[first:last, :depth], src[:depth, cols]).astype(BF16)

    def attend(w):
        rows = pl.ds(pl.multiple_of(w * WIN, WIN), WIN)
        bias = window_bias(key_bias[rows, :], split_amount(w))
        for pair in range(4):
            lanes = slice(pair * 128, (pair + 1) * 128)
            query, key, value = (packed[rows, pair * 384 + k * 128:pair * 384 + (k + 1) * 128] for k in range(3))
            total = None
            for half, mask in enumerate(masks):
                scores = scores_t(key, jnp.where(mask, query, 0), bias)
                largest = jnp.max(scores, 0, keepdims=True)
                probs = jnp.exp(scores - largest)
                total_e = jnp.sum(probs, 0, keepdims=True)
                probs = probs * (1.0 / total_e)
                log_sum[pl.ds(w * 8 + pair * 2 + half, 1), :] = largest + jnp.log(total_e)
                part = mm_tn(probs.astype(BF16), jnp.where(mask, value, 0))
                total = part if total is None else total + part
            hid[rows, lanes] = total.astype(BF16)

    def first_part(first, last):
        band = slice(first * WIN, last * WIN)

        def first_norm(i):
            rows = pl.ds(pl.multiple_of(i * WIN, WIN), WIN)
            normed, _ = norm_stats(x_ref[rows, :].astype(F32))
            lowered[rows, :] = (normed * gain_a).astype(BF16)

        loop(first, last, first_norm)

        def project(n):
            cols = pl.ds(pl.multiple_of(n * 256, 256), 256)
            lane = n * 256 + lax.broadcasted_iota(jnp.int32, (1, 256), 1)
            factor = jnp.where(lax.rem(lane, 384) < 128, HEAD ** (-0.5), 1.0)
            packed[band, cols] = (mm(lowered[band, :], w_qkv[:, cols]) * factor).astype(BF16)

        loop(0, 6, project)
        loop(first, last, attend)

    own_rows(context, 0)
    enter(x_ref, 0, 0, 3 * WIN, HALF)
    for copy in loads[5:]:
        copy.wait()
    first_part(0, 3)
    loads[1].wait()
    pack_c[...] = mm(rim_in[...], out_win[...]).astype(BF16)
    send_halos(pack_c, rim_c, lat_c, out_win)
    for copy in halos[0:4]:
        copy.wait_recv()
    rim_rows(lat_t, rim_t, 0)
    enter(x_ref, 0, 3 * WIN, HALF, HALF + 2 * PIECE)
    own_rows(context, 1)
    rim_rows(lat_t, rim_t, 1)
    enter(x_ref, 1, 0, HALF, HALF + 2 * PIECE)
    first_part(3, 8)
    for copy in halos[4:8]:
        copy.wait_recv()
    for wr in range(2):
        own_rows(out_win, wr)
        rim_rows(lat_c, rim_c, wr)
        enter(c_ref, wr, 0, HALF, HALF + 2 * PIECE)
    for copy in halos:
        copy.wait_send()
    loads[2].wait()
    context[...] = hid[...]

    def second_norm(rows):
        attended = mm(context[rows, :], w_out[...]).astype(BF16)
        m = x_ref[rows, :].astype(F32) + attended.astype(F32)
        mixed[rows, :] = m
        normed, _ = norm_stats(m)
        hid[rows, :] = (normed * gain_b).astype(BF16)

    rows_loop(TOK, 288, second_norm)
    hid_t[...] = hid[...].T
    c_t[...] = c_ref[...].T
    acc_out[...] = jnp.zeros_like(acc_out)
    acc_in[...] = jnp.zeros_like(acc_in)
    loads[3].wait()
    loads[4].wait()

    def tick(t):
        for stage, lag in reversed(list(zip(sum_a.stages(), LAGS))):
            u = t - lag
            if isinstance(t, int):
                if 0 <= u < 8:
                    stage(u)
            else:
                @pl.when((u >= 0) & (u < 8))
                def _(stage=stage, u=u):
                    stage(u)

    def share(left, right, flip, own, out, at):
        rows = pl.ds(pl.multiple_of(at, 128), 128)
        for which, dst in ((core, own), (1 - core, out)):
            part = mm(left[pl.ds(pl.multiple_of(which * 256, 256), 256), :], right)
            if flip:
                part = part.T
            part = part.astype(dst.dtype)
            dst[rows, 0:256] = part[0:128]
            dst[rows, 256:512] = part[128:256]

    wide = 256

    def columns(n):
        cols = pl.ds(pl.multiple_of(n * wide, wide), wide)
        raised = mm(hid[...], w_up[:, cols])
        slope = np.float32(np.sqrt(2 / np.pi))
        square = raised * raised
        t = jnp.tanh(slope * (raised + np.float32(0.044715) * (square * raised)))
        cdf = 0.5 * (1.0 + t)
        activated = (raised * cdf).astype(BF16)
        deriv = cdf + 0.5 * raised * (1.0 - t * t) * (slope * (1.0 + np.float32(3 * 0.044715) * square))
        grad_act = mm_nt(c_ref[...], w_down[cols, :])
        grad_raised = (grad_act * deriv).astype(BF16)
        acc_out[...] += mm(activated, w_down[cols, :])
        acc_in[...] += mm_nt(grad_raised, w_up[:, cols])
        share(hid_t, grad_raised, False, sum_a.own, sum_a.out, n * 256)
        share(c_t, activated, True, sum_a.own, sum_a.out, n * 256 + 128)
        sum_a.hand(n).start()
        tick(n)

    loop(0, FF // wide, columns)
    tick(8)
    gain_part[...] = jnp.zeros_like(gain_part)

    def finish(rows):
        m = mixed[rows, :]
        out_win[rows, :] = (m + acc_out[rows, :]).astype(BF16)
        normed, inv_std = norm_stats(m)
        grad_in = acc_in[rows, :]
        gain_part[1:2, :] += jnp.sum(grad_in * normed, 0, keepdims=True)
        g = c_ref[rows, :].astype(F32) + norm_back(grad_in, normed, inv_std, gain_b)
        acc_in[rows, :] = g
        g = g.astype(BF16)
        hid[rows, :] = g
        g_ctx[rows, :] = mm_nt(g, w_out[...]).astype(BF16)

    rows_loop(TOK, WIN, finish)
    backs = []

    def send_back(k, win):
        for wr in range(2):
            at = (k * 2 + wr) * 2 * PIECE
            rims[at:at + 2 * PIECE, :] = mm(rim_back[...], win[wr * HALF:(wr + 1) * HALF, :]).astype(BF16)
        send_blocks[k * 2 * BLOCK:(k + 1) * 2 * BLOCK, :] = mm(back_last[...], win[HALF:, :]).astype(BF16)
        near = pl.ds(k * 4 * PIECE, 3 * PIECE)
        far = pl.ds(k * 4 * PIECE + 3 * PIECE, PIECE)
        blocks = pl.ds(k * 2 * BLOCK, 2 * BLOCK)
        for a, b, device in (
            (send_blocks.at[blocks], lat_blocks.at[blocks], (lon, lat_p)),
            (rims.at[near], lon_rims.at[near], (lon_p, lat)),
            (rims.at[far], lon_rims.at[far], (lon_p, lat_p)),
        ):
            n = len(backs)
            backs.append(remote(a, b, back_s.at[n], back_r.at[n], device))
            backs[n].start()

    send_back(0, out_win)
    gmix, g_att = acc_in, hid

    tick(9)
    hid_t[...] = lowered[...].T
    c_t[...] = context[...].T
    for which, dst in ((core, sum_c.own), (1 - core, sum_c.out)):
        part = mm(c_t[pl.ds(pl.multiple_of(which * 256, 256), 256), :], g_att[...])
        dst[...] = part.astype(dst.dtype)
    sum_c.hand(0).start()
    tick(10)

    def attend_back(w, pair):
        rows = pl.ds(pl.multiple_of(w * WIN, WIN), WIN)
        bias = window_bias(key_bias[rows, :], split_amount(w))
        lanes = [pl.ds(pl.multiple_of(pair * 384 + k * 128, 128), 128) for k in range(3)]
        query, key, value = (packed[rows, at] for at in lanes)
        grad = g_ctx[rows, pl.ds(pl.multiple_of(pair * 128, 128), 128)]
        sums = [None, None, None]
        for half, mask in enumerate(masks):
            query_m = jnp.where(mask, query, 0)
            grad_m = jnp.where(mask, grad, 0)
            probs = jnp.exp(scores_t(key, query_m, bias) - log_sum[pl.ds(w * 8 + pair * 2 + half, 1), :])
            g_weights = mm_nt(value, grad_m)
            inner = jnp.sum(probs * g_weights, 0, keepdims=True)
            g_scores = (probs * (g_weights - inner)).astype(BF16)
            parts = (
                mm_tn(g_scores, jnp.where(mask, key, 0)),
                mm(g_scores, query_m),
                mm(probs.astype(BF16), grad_m),
            )
            sums = [b if a is None else a + b for a, b in zip(sums, parts)]
        sums[0] = sums[0] * HEAD ** (-0.5)
        for at, value in zip(lanes, sums):
            g_pack[rows, at] = value.astype(BF16)

    both = (sum_b, sum_c)

    def heads(pair):
        def some(k):
            for w in range(4):
                attend_back(k * 4 + w, pair)
            now = 2 * pair + k
            for when, which, stage, u in LATE:
                @pl.when(now == when)
                def _(which=which, stage=stage, u=u):
                    both[which].stages()[stage](u)

            tick(11 + now)

        loop(0, 2, some)
        cols = pl.ds(pl.multiple_of(pair * 384, 384), 384)
        rows = pl.ds(pl.multiple_of(pair * 256, 256), 256)
        for which, dst in ((1 - core, sum_b.out), (core, sum_b.own)):
            part = mm(hid_t[pl.ds(pl.multiple_of(which * 256, 256), 256), :], g_pack[:, cols])
            dst[rows, :] = part.astype(dst.dtype)
            if dst is sum_b.out:
                sum_b.hand(pair).start()

    loop(0, 4, heads)
    tick(19)

    def finish_back(rows):
        g_low = mm_nt(g_pack[rows, :], w_qkv[...]).astype(BF16).astype(F32)
        normed, inv_std = norm_stats(x_ref[rows, :].astype(F32))
        gain_part[0:1, :] += jnp.sum(g_low * normed, 0, keepdims=True)
        gtok_win[rows, :] = (gmix[rows, :] + norm_back(g_low, normed, inv_std, gain_a)).astype(BF16)

    def later(phase):
        for which, stage, u in PHASES[phase]:
            both[which].stages()[stage](u)

    rows_loop(TOK // 2, 288, finish_back)
    later(0)
    tick(20)
    rows_loop(TOK // 2, 288, lambda rows: finish_back(pl.ds(pl.multiple_of(rows.start + TOK // 2, 288), 288)))
    send_back(1, gtok_win)
    later(1)
    tick(21)
    gain_slots[0, 0] = gain_part[...]
    gain_pair = remote(gain_slots.at[0, 0], gain_slots.at[0, 1], gain_s.at[0, 0], gain_r.at[0, 0], partner)
    gain_pair.start()
    def gains_along(level, total):
        axis = level - 1
        slot = gain_slots.at[level, place[axis]]
        gain_slots[level, place[axis]] = total
        copies = [
            remote(slot, slot, gain_s.at[level, step - 1], gain_r.at[level, step - 1], peer(axis, step))
            for step in (1, 2, 3)
        ]
        for copy in copies:
            copy.start()
        return copies

    def gains_sum(level, copies):
        for copy in copies:
            copy.wait()
        return (gain_slots[level, 0] + gain_slots[level, 1]) + (gain_slots[level, 2] + gain_slots[level, 3])

    gain_pair.wait()
    gain_copies = gains_along(1, gain_slots[0, 0] + gain_slots[0, 1])
    later(2)
    tick(22)
    gain_copies = gains_along(2, gains_sum(1, gain_copies))
    later(3)
    tick(23)
    gain_copies = gains_along(3, gains_sum(2, gain_copies))
    later(4)
    gains_out[...] = gains_sum(3, gain_copies) * SCALE
    later(5)
    loop(0, 8, sum_a.end)
    sum_c.end(0)
    loop(0, 4, sum_b.end)
    for copy in backs:
        copy.wait()


LAGS = (1, 4, 7, 10, 13, 16)
LATE = (
    (0, 1, 0, 0), (2, 1, 1, 0), (4, 1, 2, 0), (6, 1, 3, 0),
    (6, 0, 2, 0), (4, 0, 1, 0), (2, 0, 0, 0), (6, 0, 1, 1), (4, 0, 0, 1), (6, 0, 0, 2),
)
PHASES = (
    ((1, 4, 0), (0, 3, 0), (0, 2, 1), (0, 1, 2), (0, 0, 3)),
    ((1, 5, 0), (0, 4, 0), (0, 3, 1), (0, 2, 2), (0, 1, 3)),
    ((0, 5, 0), (0, 4, 1), (0, 3, 2), (0, 2, 3)),
    ((0, 5, 1), (0, 4, 2), (0, 3, 3)),
    ((0, 5, 2), (0, 4, 3)),
    ((0, 5, 3),),
)


def sums_scratch(units, lanes):
    vmem = pltpu.VMEM
    return [
        vmem((units * 256, lanes), F32), vmem((units * 256, lanes), BF16), vmem((units * 256, lanes), BF16),
        vmem((units, 3, 64, lanes), BF16), vmem((units, 64, lanes), F32), vmem((units, 3, 16, lanes), F32),
        vmem((units, 4, 16, lanes), F32), vmem((units, 16, lanes), BF16),
        pltpu.SemaphoreType.DMA((units, 4, 3)), pltpu.SemaphoreType.DMA((units, 5)),
    ]


def block(*args):
    vm = pl.BlockSpec(memory_space=pltpu.VMEM)
    hbm = pl.BlockSpec(memory_space=pl.ANY)
    shape = jax.ShapeDtypeStruct
    dma = pltpu.SemaphoreType.DMA
    vmem = pltpu.VMEM
    field = vmem((TOK, D), BF16)
    field_t = vmem((D, TOK), BF16)
    wide = vmem((TOK, D), F32)
    rim = vmem((4 * PIECE, D), BF16)
    lat_rim = vmem((2 * BLOCK, D), BF16)
    return pl.pallas_call(
        block_kernel,
        out_shape=(
            shape((2 * FF, D), BF16),
            shape((4 * D, 384), BF16),
            shape((D, D), BF16),
            shape((8, D), F32),
            shape((TOK, D), BF16),
            shape((TOK, D), BF16),
            shape((8 * PIECE, D), BF16),
            shape((4 * BLOCK, D), BF16),
        ),
        in_specs=[hbm, hbm] + [vm] * 5 + [hbm] * 4 + [vm],
        out_specs=(hbm,) * 3 + (vm,) * 5,
        scratch_shapes=[
            vmem((D, 3 * D), BF16), vmem((D, D), BF16), vmem((D, FF), BF16), vmem((FF, D), BF16),
            lat_rim, lat_rim, rim, rim, rim, rim, vmem((TOK, 1), F32), vmem((64, WIN), F32),
            field, field, field, field, field, field_t, field_t, field,
            vmem((TOK, 3 * D), BF16), vmem((TOK, 3 * D), BF16), vmem((HALF + 2 * PIECE, D), BF16),
            wide, wide, wide,
            *sums_scratch(8, D), *sums_scratch(4, 384), *sums_scratch(1, D),
            vmem((8 * PIECE, D), BF16), vmem((4 * BLOCK, D), BF16), vmem((4, 4, 8, D), F32), vmem((8, D), F32),
            dma((17,)), dma((8,)), dma((8,)), dma((6,)), dma((6,)), dma((4, 3)), dma((4, 3)),
        ],
        compiler_params=pltpu.CompilerParams(collective_id=0, has_side_effects=True, vmem_limit_bytes=VMEM_BYTES),
        name="block",
    )(*args)


def finish_kernel(
    r1, r2, r3, gain_sums, out_win, gtok_win, lon_rims, lat_blocks, back,
    outputs, g_tok, g_qkv, g_out, g_up, g_down, g_gains,
    v1, v2, v3, w1, w2, rims, blocks, src, full, f_up, f_down, f_qkv, f_out, sem_in, sem_out,
):
    halves = [
        [(r1.at[pl.ds(core * FF + n * 1024, 1024)], v1.at[pl.ds(core * FF + n * 1024, 1024)]) for core in range(2)]
        for n in range(2)
    ]
    wanted = halves[0] + [(out_win, w1), (lon_rims, rims), (lat_blocks, blocks)] + halves[1]
    wanted += [(gtok_win, w2), (r2, v2), (r3, v3)]
    loads = [pltpu.make_async_copy(a, b, sem_in.at[k]) for k, (a, b) in enumerate(wanted)]
    for copy in loads:
        copy.start()
    stores = []

    def store(a, b):
        copy = pltpu.make_async_copy(a, b, sem_out.at[len(stores)])
        copy.start()
        stores.append(copy)

    def wide(n):
        for core in range(2):
            for k in range(2):
                lanes = slice(k * 256, (k + 1) * 256)
                at = core * FF + n * 256
                f_up[core * 256 + k * 128:core * 256 + (k + 1) * 128, n * 256:(n + 1) * 256] = (
                    v1[at:at + 128, lanes].astype(F32)
                )
                f_down[n * 256 + k * 128:n * 256 + (k + 1) * 128, core * 256:(core + 1) * 256] = (
                    v1[at + 128:at + 256, lanes].astype(F32)
                )
        if n % 2:
            cols = pl.ds((n - 1) * 256, 512)
            store(f_up.at[:, cols], g_up.at[:, cols])
            store(f_down.at[cols], g_down.at[cols])

    def field(k, win, out):
        for wr in range(2):
            at = (k * 2 + wr) * 2 * PIECE
            src[:HALF, :] = win[wr * HALF:(wr + 1) * HALF, :]
            src[HALF:, :] = rims[at:at + 2 * PIECE, :]
            for lev in range(2):
                if wr == 0:
                    pick, length = slice(lev * 288, (lev + 1) * 288), 288
                    to = lev * HALF + 144
                else:
                    pick, length = slice(lev * 288, lev * 288 + 144), 144
                    to = lev * HALF + 432
                full[k, to:to + length, :] = mm(back[pick, :], src[...]).astype(BF16)
        for lev in range(2):
            edge = mm(back[lev * 288 + BLOCK:(lev + 1) * 288, HALF:], src[HALF:, :])
            inner = blocks[(k * 2 + lev) * BLOCK:(k * 2 + lev + 1) * BLOCK, :].astype(F32)
            full[k, lev * HALF:lev * HALF + BLOCK, :] = (inner + edge).astype(BF16)
        store(full.at[k], out)

    g_gains[...] = gain_sums[0:2, :]
    for copy in loads[0:2]:
        copy.wait()
    for n in range(4):
        wide(n)
    for copy in loads[2:5]:
        copy.wait()
    field(0, w1, outputs)
    for copy in loads[5:7]:
        copy.wait()
    for n in range(4, 8):
        wide(n)
    loads[7].wait()
    field(1, w2, g_tok)
    loads[8].wait()
    for part in range(3):
        for pair in range(4):
            for core in range(2):
                f_qkv[core * 256:(core + 1) * 256, part * D + pair * 128:part * D + (pair + 1) * 128] = (
                    v2[core * 1024 + pair * 256:core * 1024 + (pair + 1) * 256, part * 128:(part + 1) * 128].astype(F32)
                )
        cols = pl.ds(part * D, D)
        store(f_qkv.at[:, cols], g_qkv.at[:, cols])
    loads[9].wait()
    f_out[...] = v3[...].astype(F32)
    store(f_out, g_out)
    for copy in stores:
        copy.wait()


def finish_all(*args):
    vm = pl.BlockSpec(memory_space=pltpu.VMEM)
    hbm = pl.BlockSpec(memory_space=pl.ANY)
    shape = jax.ShapeDtypeStruct
    vmem = pltpu.VMEM
    return pl.pallas_call(
        finish_kernel,
        out_shape=(
            shape((TOK, D), BF16),
            shape((TOK, D), BF16),
            shape((D, 3 * D), F32),
            shape((D, D), F32),
            shape((D, FF), F32),
            shape((FF, D), F32),
            shape((2, D), F32),
        ),
        in_specs=[hbm] * 3 + [vm] + [hbm] * 4 + [vm],
        out_specs=(hbm,) * 6 + (vm,),
        scratch_shapes=[
            vmem((2 * FF, D), BF16), vmem((4 * D, 384), BF16), vmem((D, D), BF16), vmem((TOK, D), BF16),
            vmem((TOK, D), BF16), vmem((8 * PIECE, D), BF16), vmem((4 * BLOCK, D), BF16),
            vmem((HALF + 2 * PIECE, D), BF16), vmem((2, TOK, D), BF16),
            vmem((D, FF), F32), vmem((FF, D), F32), vmem((D, 3 * D), F32), vmem((D, D), F32),
            pltpu.SemaphoreType.DMA((10,)), pltpu.SemaphoreType.DMA((14,)),
        ],
        compiler_params=pltpu.CompilerParams(vmem_limit_bytes=VMEM_BYTES),
        name="finish",
    )(*args)


def on_device(tokens, cotangent, valid, w_qkv, w_out, w_up, w_down, gains):
    into, back, rim_in, rim_back = gather_maps()
    tok = tokens.reshape(TOK, D)
    cot = cotangent.reshape(TOK, D)
    back_last = jnp.concatenate([back[BLOCK:2 * BLOCK, :HALF], back[3 * BLOCK:, :HALF]], 0)
    *sums, out_win, gtok_win, lon_rims, lat_blocks = block(
        tok, cot, rim_in, into, rim_back, back_last, valid, w_qkv, w_out, w_up, w_down, gains
    )
    outputs, g_tok, g_qkv, g_out, g_up, g_down, g_gains = finish_all(
        *sums, out_win, gtok_win, lon_rims, lat_blocks, back
    )
    return (
        outputs.reshape(tokens.shape),
        g_tok.reshape(tokens.shape),
        g_qkv,
        g_out,
        g_up,
        g_down,
        g_gains,
    )


def solution(mesh):
    field = P(None, "lat", "lon", None)
    in_specs = (field, field, P("lat", "lon"), P(), P(), P(), P(), P())
    out_specs = (field, field, P(), P(), P(), P(), P())
    return jax.shard_map(on_device, mesh=mesh, in_specs=in_specs, out_specs=out_specs, check_vma=False)
```

```python
import jax
import jax.numpy as jnp
import numpy as np
from jax import lax
from jax.experimental import pallas as pl
from jax.experimental.pallas import tpu as pltpu
from jax.sharding import PartitionSpec as P

F32 = jnp.float32
BF16 = jnp.bfloat16
MESH = pl.DeviceIdType.MESH
HEAD = 64
WIN = 144
TOK = 1152
HALF = 576
D = 512
FF = 2048
COLS = 24
BLOCK = 144
PIECE = 48
epsilon = 1e-05
LOW = -1e30
SCALE = np.float32(147456 ** (-0.5))
VMEM_BYTES = 63 * 1024 * 1024


def gather_maps():
    into = np.zeros((HALF, HALF + 2 * PIECE), np.float32)
    back = np.zeros((HALF, HALF + 2 * PIECE), np.float32)
    rim_in = np.zeros((4 * PIECE, TOK), np.float32)
    rim_back = np.zeros((2 * PIECE, HALF), np.float32)
    for lev in range(2):
        for half in range(2):
            for r in range(6):
                for col in range(COLS):
                    window = (col // 6) * WIN + lev * 72 + half * 36 + r * 6 + col % 6
                    chunk = (lev * 2 + half) * BLOCK + r * COLS
                    if col + 3 < COLS:
                        into[window, chunk + col + 3] = 1
                        back[chunk + col + 3, window] = 1
                    else:
                        rim = half * PIECE + lev * 18 + r * 3 + col + 3 - COLS
                        into[window, HALF + rim] = 1
                        back[chunk + col + 3 - COLS, HALF + rim] = 1
                        rim_back[rim, window] = 1
    for lev in range(2):
        for block in range(4):
            for r in range(6):
                for col in range(3):
                    rim_in[block * PIECE + lev * 18 + r * 3 + col, lev * HALF + block * BLOCK + r * COLS + col] = 1
    return [jnp.asarray(m, BF16) for m in (into, back, rim_in, rim_back)]


def mm(a, b):
    return lax.dot_general(a, b, (((1,), (0,)), ((), ())), preferred_element_type=F32)


def mm_nt(a, b):
    return lax.dot_general(a, b, (((1,), (1,)), ((), ())), preferred_element_type=F32)


def mm_tn(a, b):
    return lax.dot_general(a, b, (((0,), (0,)), ((), ())), preferred_element_type=F32)


def norm_stats(values):
    centred = values - jnp.mean(values, -1, keepdims=True)
    inv_std = lax.rsqrt(jnp.mean(centred * centred, -1, keepdims=True) + epsilon)
    return centred * inv_std, inv_std


def norm_back(grad_value, normed, inv_std, gain_row):
    scaled = grad_value * gain_row
    return inv_std * (
        scaled
        - jnp.mean(scaled, -1, keepdims=True)
        - normed * jnp.mean(scaled * normed, -1, keepdims=True)
    )


def rows_loop(total, step, body):
    def run(i, carry):
        body(pl.ds(pl.multiple_of(i * step, step), step))
        return carry

    lax.fori_loop(0, total // step, run, 0)


def window_bias(key_bias, split):
    rows = lax.broadcasted_iota(jnp.int32, (WIN, WIN), 0)
    cols = lax.broadcasted_iota(jnp.int32, (WIN, WIN), 1)
    bias = jnp.where(rows == cols, 0.0, jnp.broadcast_to(key_bias, (WIN, WIN)))
    apart = ((rows // 36) % 2) != ((cols // 36) % 2)
    return bias + jnp.where(apart, split, 0.0)


def scores_t(key2, query_m, bias):
    return mm_nt(key2, query_m) + bias


def head_masks():
    lane = lax.broadcasted_iota(jnp.int32, (WIN, 128), 1)
    return [lane < HEAD, lane >= HEAD]


def split_amount(window):
    last = (lax.axis_index("lat") == lax.axis_size("lat") - 1) & (window >= 4)
    return jnp.where(last, LOW, 0.0).astype(F32)


def position():
    lon, lat = lax.axis_index("lon"), lax.axis_index("lat")
    y = lax.rem(lax.div(lat, 2), 2) * 2 + lax.rem(lon, 2)
    return [lax.div(lon, 2), y, lax.div(lat, 4)], lax.rem(lat, 2)


def device_at(place, core):
    x, y, z = place
    return (x * 2 + lax.rem(y, 2), z * 4 + lax.div(y, 2) * 2 + core)


def remote(src, dst, s, r, device):
    return pltpu.make_async_remote_copy(
        src_ref=src, dst_ref=dst, send_sem=s, recv_sem=r, device_id=device, device_id_type=MESH
    )


def loop(first, last, body):
    def run(i, carry):
        body(i)
        return carry

    lax.fori_loop(first, last, run, 0)


class Sums:
    def __init__(self, turn, own, out, pair, recv1, sum1, recv2, recv3, fin, result, sems, pair_sems):
        self.turn = turn
        self.own, self.out, self.pair = own, out, pair
        self.recv1, self.sum1, self.recv2, self.recv3, self.fin = recv1, sum1, recv2, recv3, fin
        self.result, self.sems, self.pair_sems = result, sems, pair_sems
        self.place, self.core = position()
        self.partner = device_at(self.place, 1 - self.core)
        self.base = self.core * own.shape[0]

    def flags(self, u, level):
        turn = u + self.turn + level
        turn = turn % 3 if isinstance(u, int) else lax.rem(turn, 3)
        first, last = (2 - turn) // 2, turn // 2
        return first, 1 - first - last, last

    def peer(self, u, level, step):
        flags = self.flags(u, level)
        return device_at([lax.rem(at + flag * step, 4) for at, flag in zip(self.place, flags)], self.core)

    def mine(self, u, level):
        x, y, z = (at * flag for at, flag in zip(self.place, self.flags(u, level)))
        return x + y + z

    def rows(self, u):
        return pl.ds(pl.multiple_of(u * 256, 256), 256)

    def rows1(self, u, at):
        return pl.ds(pl.multiple_of(u * 256 + at * 64, 64), 64)

    def result_rows(self, u, level):
        at = self.base + u * 256
        if level < 0:
            return pl.ds(pl.multiple_of(at, 256), 256)
        at = at + self.mine(u, 0) * 64
        if level == 0:
            return pl.ds(pl.multiple_of(at, 64), 64)
        return pl.ds(pl.multiple_of(at + self.mine(u, 1) * 16, 16), 16)

    def down(self, u, level, step):
        s, r = self.sems.at[u, 0, level], self.sems.at[u, 1, level]
        device = self.peer(u, level, step)
        if level == 0:
            there = lax.rem(self.mine(u, 0) + step, 4)
            return remote(self.out.at[self.rows1(u, there)], self.recv1.at[u, step - 1], s, r, device)
        if level == 1:
            there = lax.rem(self.mine(u, 1) + step, 4)
            rows = pl.ds(pl.multiple_of(there * 16, 16), 16)
            return remote(self.sum1.at[u, rows], self.recv2.at[u, step - 1], s, r, device)
        slot = self.recv3.at[u, self.mine(u, 2)]
        return remote(slot, slot, s, r, device)

    def up(self, u, level, step):
        s, r = self.sems.at[u, 2, level], self.sems.at[u, 3, level]
        rows = self.result.at[self.result_rows(u, level)]
        return remote(self.fin.at[u] if level == 1 else rows, rows, s, r, self.peer(u, level, step))

    def hand(self, u):
        rows = self.rows(u)
        return remote(
            self.out.at[rows], self.pair.at[rows], self.pair_sems.at[u, 0], self.pair_sems.at[u, 1], self.partner
        )

    def hand_back(self, u):
        rows = self.result.at[self.result_rows(u, -1)]
        return remote(rows, rows, self.pair_sems.at[u, 2], self.pair_sems.at[u, 3], self.partner)

    def keep(self, u):
        return pltpu.make_async_copy(self.fin.at[u], self.result.at[self.result_rows(u, 1)], self.pair_sems.at[u, 4])

    def done(self, u, kind, level):
        if kind < 2:
            three = (self.recv1.at[u], self.recv2.at[u], self.recv3.at[u, pl.ds(0, 3)])[level]
        else:
            three = (self.recv1.at[u], self.recv1.at[u, 0, pl.ds(0, 48)])[level]
        pltpu.make_async_copy(three, three, self.sems.at[u, kind, level]).wait()

    def send(self, make, u, level):
        for step in (1, 2, 3):
            make(u, level, step).start()

    def begin(self, u):
        self.hand(u).wait()
        rows = self.rows(u)
        total = self.own[rows, :] + self.pair[rows, :].astype(F32)
        self.own[rows, :] = total
        self.out[rows, :] = total.astype(BF16)
        self.send(self.down, u, 0)

    def second(self, u):
        self.done(u, 1, 0)
        rows = self.rows1(u, self.mine(u, 0))
        self.sum1[u] = (self.own[rows, :] + self.recv1[u, 0].astype(F32)) + (
            self.recv1[u, 1].astype(F32) + self.recv1[u, 2].astype(F32)
        )
        self.send(self.down, u, 1)

    def third(self, u):
        self.done(u, 1, 1)
        rows = pl.ds(pl.multiple_of(self.mine(u, 1) * 16, 16), 16)
        self.recv3[u, self.mine(u, 2)] = (self.sum1[u, rows, :] + self.recv2[u, 0]) + (
            self.recv2[u, 1] + self.recv2[u, 2]
        )
        self.send(self.down, u, 2)

    def gather(self, u):
        self.done(u, 1, 2)
        total = (self.recv3[u, 0] + self.recv3[u, 1]) + (self.recv3[u, 2] + self.recv3[u, 3])
        self.fin[u] = (total * SCALE).astype(BF16)
        self.keep(u).start()
        self.send(self.up, u, 1)

    def gather_next(self, u):
        self.keep(u).wait()
        self.done(u, 3, 1)
        self.send(self.up, u, 0)

    def gather_pair(self, u):
        self.done(u, 3, 0)
        self.hand_back(u).start()

    def end(self, u):
        for level in range(3):
            self.done(u, 0, level)
        for level in range(2):
            self.done(u, 2, level)
        self.hand_back(u).wait()

    def stages(self):
        return (self.begin, self.second, self.third, self.gather, self.gather_next, self.gather_pair)


def block_kernel(
    tok, cot, rim_in, into, rim_back, back_last, valid, w_qkv_h, w_out_h, w_up_h, w_down_h, gains,
    r1, r2, r3, gains_out, out_win, gtok_win, lon_rims, lat_blocks,
    w_qkv, w_out, w_up, w_down, lat_t, lat_c, rim_t, rim_c, pack_t, pack_c, key_bias, log_sum,
    x_ref, c_ref, lowered, context, hid, hid_t, c_t, g_ctx, packed, g_pack, src, mixed, acc_out, acc_in,
    *rest_refs,
):
    place, core = position()
    lon, lat = lax.axis_index("lon"), lax.axis_index("lat")
    n_lon, n_lat = lax.axis_size("lon"), lax.axis_size("lat")
    lon_m, lon_p = lax.rem(lon + n_lon - 1, n_lon), lax.rem(lon + 1, n_lon)
    lat_m, lat_p = lax.rem(lat + n_lat - 1, n_lat), lax.rem(lat + 1, n_lat)
    partner = device_at(place, 1 - core)
    gain_a = gains[0:1, :]
    gain_b = gains[1:2, :]
    masks = head_masks()
    refs = iter(rest_refs)
    results = (r1, r2, r3)
    sum_a, sum_b, sum_c = (
        Sums(TURNS[k], *[next(refs) for _ in range(8)], results[k], next(refs), next(refs)) for k in range(3)
    )
    (rims, send_blocks, gain_slots, gain_part,
     load_sem, halo_s, halo_r, back_s, back_r, gain_s, gain_r) = refs

    def peer(axis, step):
        there = list(place)
        there[axis] = lax.rem(place[axis] + step, 4)
        return device_at(there, core)

    barrier = pltpu.get_barrier_semaphore()
    greet = [(lon, lat_m), (lon, lat_p), (lon_m, lat), (lon_p, lat), (lon_m, lat_m), (lon_p, lat_p), partner]
    greet += [peer(axis, step) for axis in range(3) for step in (1, 2, 3)]
    for device in greet:
        pl.semaphore_signal(barrier, inc=1, device_id=device, device_id_type=MESH)
    loads = [
        pltpu.make_async_copy(a, b, load_sem.at[k])
        for k, (a, b) in enumerate(
            ((tok, context), (cot, out_win), (w_out_h, w_out), (w_up_h, w_up), (w_down_h, w_down))
        )
    ]
    loads += [
        pltpu.make_async_copy(
            w_qkv_h.at[:, pl.ds(part * D + pair * 128, 128)],
            w_qkv.at[:, pl.ds(pair * 384 + part * 128, 128)],
            load_sem.at[5 + part * 4 + pair],
        )
        for part in range(3)
        for pair in range(4)
    ]
    for copy in loads:
        copy.start()
    loads[0].wait()
    pack_t[...] = mm(rim_in[...], context[...]).astype(BF16)
    pl.semaphore_wait(barrier, len(greet))

    halos = []
    rest = pl.ds(PIECE, 3 * PIECE)
    corner = pl.ds(0, PIECE)

    def send_halos(pack, rim, lat_rim, full):
        wanted = [
            (pack.at[rest], rim.at[rest], (lon_m, lat)),
            (pack.at[corner], rim.at[corner], (lon_m, lat_m)),
        ]
        for lev in range(2):
            wanted.append(
                (full.at[pl.ds(lev * HALF, BLOCK)], lat_rim.at[pl.ds(lev * BLOCK, BLOCK)], (lon, lat_m))
            )
        for a, b, device in wanted:
            k = len(halos)
            halos.append(remote(a, b, halo_s.at[k], halo_r.at[k], device))
            halos[k].start()

    send_halos(pack_t, rim_t, lat_t, context)
    usable = jnp.where(valid[...] == 1, 1.0, 0.0).astype(BF16)
    spot = lax.broadcasted_iota(jnp.int32, (WIN, COLS), 0)
    lane = lax.broadcasted_iota(jnp.int32, (WIN, COLS), 1)
    for wr in range(2):
        lat_at = wr * 12 + ((spot // 36) % 2) * 6 + (spot // 6) % 6
        picked = mm(jnp.where(lane == lat_at, 1.0, 0.0).astype(BF16), usable)
        for k in range(4):
            ok = jnp.sum(jnp.where(lane == 6 * k + spot % 6, picked, 0.0), 1, keepdims=True)
            key_bias[(wr * 4 + k) * WIN:(wr * 4 + k + 1) * WIN, :] = jnp.where(ok > 0.5, 0.0, LOW)

    def own_rows(full, wr):
        for lev in range(2):
            if wr == 0:
                src[lev * 288:(lev + 1) * 288, :] = full[lev * HALF + 144:lev * HALF + 432, :]
            else:
                src[lev * 288:lev * 288 + 144, :] = full[lev * HALF + 432:lev * HALF + 576, :]

    def rim_rows(lat_rim, rim, wr):
        if wr == 0:
            src[HALF:, :] = rim[PIECE:3 * PIECE, :]
        else:
            for lev in range(2):
                src[lev * 288 + 144:(lev + 1) * 288, :] = lat_rim[lev * BLOCK:(lev + 1) * BLOCK, :]
            src[HALF:HALF + PIECE, :] = rim[3 * PIECE:, :]
            src[HALF + PIECE:, :] = rim[:PIECE, :]

    def enter(dst, wr, first, last, depth):
        for n in range(2):
            cols = slice(n * 256, (n + 1) * 256)
            dst[wr * HALF + first:wr * HALF + last, cols] = mm(into[first:last, :depth], src[:depth, cols]).astype(BF16)

    def attend(w):
        rows = pl.ds(pl.multiple_of(w * WIN, WIN), WIN)
        bias = window_bias(key_bias[rows, :], split_amount(w))
        for pair in range(4):
            lanes = slice(pair * 128, (pair + 1) * 128)
            query, key, value = (packed[rows, pair * 384 + k * 128:pair * 384 + (k + 1) * 128] for k in range(3))
            total = None
            for half, mask in enumerate(masks):
                scores = scores_t(key, jnp.where(mask, query, 0), bias)
                largest = jnp.max(scores, 0, keepdims=True)
                probs = jnp.exp(scores - largest)
                total_e = jnp.sum(probs, 0, keepdims=True)
                probs = probs * (1.0 / total_e)
                log_sum[pl.ds(w * 8 + pair * 2 + half, 1), :] = largest + jnp.log(total_e)
                part = mm_tn(probs.astype(BF16), jnp.where(mask, value, 0))
                total = part if total is None else total + part
            hid[rows, lanes] = total.astype(BF16)

    def first_part(first, last):
        band = slice(first * WIN, last * WIN)

        def first_norm(i):
            rows = pl.ds(pl.multiple_of(i * WIN, WIN), WIN)
            normed, _ = norm_stats(x_ref[rows, :].astype(F32))
            lowered[rows, :] = (normed * gain_a).astype(BF16)

        loop(first, last, first_norm)

        def project(n):
            cols = pl.ds(pl.multiple_of(n * 256, 256), 256)
            lane = n * 256 + lax.broadcasted_iota(jnp.int32, (1, 256), 1)
            factor = jnp.where(lax.rem(lane, 384) < 128, HEAD ** (-0.5), 1.0)
            packed[band, cols] = (mm(lowered[band, :], w_qkv[:, cols]) * factor).astype(BF16)

        loop(0, 6, project)
        loop(first, last, attend)

    own_rows(context, 0)
    enter(x_ref, 0, 0, 3 * WIN, HALF)
    for copy in loads[5:]:
        copy.wait()
    first_part(0, 3)
    loads[1].wait()
    pack_c[...] = mm(rim_in[...], out_win[...]).astype(BF16)
    send_halos(pack_c, rim_c, lat_c, out_win)
    for copy in halos[0:4]:
        copy.wait_recv()
    rim_rows(lat_t, rim_t, 0)
    enter(x_ref, 0, 3 * WIN, HALF, HALF + 2 * PIECE)
    own_rows(context, 1)
    rim_rows(lat_t, rim_t, 1)
    enter(x_ref, 1, 0, HALF, HALF + 2 * PIECE)
    first_part(3, 8)
    for copy in halos[4:8]:
        copy.wait_recv()
    for wr in range(2):
        own_rows(out_win, wr)
        rim_rows(lat_c, rim_c, wr)
        enter(c_ref, wr, 0, HALF, HALF + 2 * PIECE)
    for copy in halos:
        copy.wait_send()
    loads[2].wait()
    context[...] = hid[...]

    def second_norm(rows):
        attended = mm(context[rows, :], w_out[...]).astype(BF16)
        m = x_ref[rows, :].astype(F32) + attended.astype(F32)
        mixed[rows, :] = m
        normed, _ = norm_stats(m)
        hid[rows, :] = (normed * gain_b).astype(BF16)

    rows_loop(TOK, 288, second_norm)
    hid_t[...] = hid[...].T
    c_t[...] = c_ref[...].T
    acc_out[...] = jnp.zeros_like(acc_out)
    acc_in[...] = jnp.zeros_like(acc_in)
    loads[3].wait()
    loads[4].wait()

    def tick(n):
        for stage, lag in reversed(list(zip(sum_a.stages(), LAGS))):
            @pl.when(n >= lag)
            def _(stage=stage, lag=lag):
                stage(n - lag)

    plan, tail = schedule()
    all_sums = (sum_a, sum_b, sum_c)

    def due(spot):
        for which, stage, u in plan.get(spot, ()):
            all_sums[which].stages()[stage](u)

    def share(left, right, flip, own, out, at):
        rows = pl.ds(pl.multiple_of(at, 128), 128)
        for which, dst in ((core, own), (1 - core, out)):
            part = mm(left[pl.ds(pl.multiple_of(which * 256, 256), 256), :], right)
            if flip:
                part = part.T
            part = part.astype(dst.dtype)
            dst[rows, 0:256] = part[0:128]
            dst[rows, 256:512] = part[128:256]

    wide = 256

    def columns(n):
        cols = pl.ds(pl.multiple_of(n * wide, wide), wide)
        raised = mm(hid[...], w_up[:, cols])
        slope = np.float32(np.sqrt(2 / np.pi))
        square = raised * raised
        t = jnp.tanh(slope * (raised + np.float32(0.044715) * (square * raised)))
        cdf = 0.5 * (1.0 + t)
        activated = (raised * cdf).astype(BF16)
        deriv = cdf + 0.5 * raised * (1.0 - t * t) * (slope * (1.0 + np.float32(3 * 0.044715) * square))
        grad_act = mm_nt(c_ref[...], w_down[cols, :])
        grad_raised = (grad_act * deriv).astype(BF16)
        acc_out[...] += mm(activated, w_down[cols, :])
        acc_in[...] += mm_nt(grad_raised, w_up[:, cols])
        share(hid_t, grad_raised, False, sum_a.own, sum_a.out, n * 256)
        share(c_t, activated, True, sum_a.own, sum_a.out, n * 256 + 128)
        sum_a.hand(n).start()
        tick(n)

    loop(0, FF // wide, columns)
    due(8)
    gain_part[...] = jnp.zeros_like(gain_part)

    def finish(rows):
        m = mixed[rows, :]
        out_win[rows, :] = (m + acc_out[rows, :]).astype(BF16)
        normed, inv_std = norm_stats(m)
        grad_in = acc_in[rows, :]
        gain_part[1:2, :] += jnp.sum(grad_in * normed, 0, keepdims=True)
        g = c_ref[rows, :].astype(F32) + norm_back(grad_in, normed, inv_std, gain_b)
        acc_in[rows, :] = g
        g = g.astype(BF16)
        hid[rows, :] = g
        g_ctx[rows, :] = mm_nt(g, w_out[...]).astype(BF16)

    rows_loop(TOK // 2, WIN, finish)
    due(8.5)
    rows_loop(TOK // 2, WIN, lambda rows: finish(pl.ds(pl.multiple_of(rows.start + TOK // 2, WIN), WIN)))
    backs = []

    def send_back(k, win):
        for wr in range(2):
            at = (k * 2 + wr) * 2 * PIECE
            rims[at:at + 2 * PIECE, :] = mm(rim_back[...], win[wr * HALF:(wr + 1) * HALF, :]).astype(BF16)
        send_blocks[k * 2 * BLOCK:(k + 1) * 2 * BLOCK, :] = mm(back_last[...], win[HALF:, :]).astype(BF16)
        near = pl.ds(k * 4 * PIECE, 3 * PIECE)
        far = pl.ds(k * 4 * PIECE + 3 * PIECE, PIECE)
        blocks = pl.ds(k * 2 * BLOCK, 2 * BLOCK)
        for a, b, device in (
            (send_blocks.at[blocks], lat_blocks.at[blocks], (lon, lat_p)),
            (rims.at[near], lon_rims.at[near], (lon_p, lat)),
            (rims.at[far], lon_rims.at[far], (lon_p, lat_p)),
        ):
            n = len(backs)
            backs.append(remote(a, b, back_s.at[n], back_r.at[n], device))
            backs[n].start()

    send_back(0, out_win)
    gmix, g_att = acc_in, hid

    due(9)
    hid_t[...] = lowered[...].T
    c_t[...] = context[...].T
    for which, dst in ((core, sum_c.own), (1 - core, sum_c.out)):
        part = mm(c_t[pl.ds(pl.multiple_of(which * 256, 256), 256), :], g_att[...])
        dst[...] = part.astype(dst.dtype)
    sum_c.hand(0).start()
    due(10)

    def attend_back(w, pair):
        rows = pl.ds(pl.multiple_of(w * WIN, WIN), WIN)
        bias = window_bias(key_bias[rows, :], split_amount(w))
        lanes = [pl.ds(pl.multiple_of(pair * 384 + k * 128, 128), 128) for k in range(3)]
        query, key, value = (packed[rows, at] for at in lanes)
        grad = g_ctx[rows, pl.ds(pl.multiple_of(pair * 128, 128), 128)]
        sums = [None, None, None]
        for half, mask in enumerate(masks):
            query_m = jnp.where(mask, query, 0)
            grad_m = jnp.where(mask, grad, 0)
            probs = jnp.exp(scores_t(key, query_m, bias) - log_sum[pl.ds(w * 8 + pair * 2 + half, 1), :])
            g_weights = mm_nt(value, grad_m)
            inner = jnp.sum(probs * g_weights, 0, keepdims=True)
            g_scores = (probs * (g_weights - inner)).astype(BF16)
            parts = (
                mm_tn(g_scores, jnp.where(mask, key, 0)),
                mm(g_scores, query_m),
                mm(probs.astype(BF16), grad_m),
            )
            sums = [b if a is None else a + b for a, b in zip(sums, parts)]
        sums[0] = sums[0] * HEAD ** (-0.5)
        for at, value in zip(lanes, sums):
            g_pack[rows, at] = value.astype(BF16)

    def heads(pair):
        def some(k):
            for w in range(4):
                attend_back(k * 4 + w, pair)
            for spot in range(11, 19):
                if spot in plan:
                    @pl.when(2 * pair + k == spot - 11)
                    def _(spot=spot):
                        due(spot)

        loop(0, 2, some)
        cols = pl.ds(pl.multiple_of(pair * 384, 384), 384)
        rows = pl.ds(pl.multiple_of(pair * 256, 256), 256)
        for which, dst in ((1 - core, sum_b.out), (core, sum_b.own)):
            part = mm(hid_t[pl.ds(pl.multiple_of(which * 256, 256), 256), :], g_pack[:, cols])
            dst[rows, :] = part.astype(dst.dtype)
            if dst is sum_b.out:
                sum_b.hand(pair).start()

    loop(0, 4, heads)
    due(19)

    def finish_back(rows):
        g_low = mm_nt(g_pack[rows, :], w_qkv[...]).astype(BF16).astype(F32)
        normed, inv_std = norm_stats(x_ref[rows, :].astype(F32))
        gain_part[0:1, :] += jnp.sum(g_low * normed, 0, keepdims=True)
        gtok_win[rows, :] = (gmix[rows, :] + norm_back(g_low, normed, inv_std, gain_a)).astype(BF16)

    rows_loop(TOK // 2, 288, finish_back)
    due(20)
    rows_loop(TOK // 2, 288, lambda rows: finish_back(pl.ds(pl.multiple_of(rows.start + TOK // 2, 288), 288)))
    send_back(1, gtok_win)
    gain_slots[0, 0] = gain_part[...]
    gain_pair = remote(gain_slots.at[0, 0], gain_slots.at[0, 1], gain_s.at[0, 0], gain_r.at[0, 0], partner)
    gain_pair.start()
    due(21)

    def gains_along(level, total):
        axis = level - 1
        slot = gain_slots.at[level, place[axis]]
        gain_slots[level, place[axis]] = total
        copies = [
            remote(slot, slot, gain_s.at[level, step - 1], gain_r.at[level, step - 1], peer(axis, step))
            for step in (1, 2, 3)
        ]
        for copy in copies:
            copy.start()
        return copies

    def gains_sum(level, copies):
        for copy in copies:
            copy.wait()
        return (gain_slots[level, 0] + gain_slots[level, 1]) + (gain_slots[level, 2] + gain_slots[level, 3])

    gain_copies = []
    for which, stage, u in tail:
        if which < 3:
            all_sums[which].stages()[stage](u)
        elif stage == 0:
            gain_pair.wait()
            gain_copies = gains_along(1, gain_slots[0, 0] + gain_slots[0, 1])
        elif stage < 3:
            gain_copies = gains_along(stage + 1, gains_sum(stage, gain_copies))
        else:
            gains_out[...] = gains_sum(3, gain_copies) * SCALE
    loop(0, 8, sum_a.end)
    sum_c.end(0)
    loop(0, 4, sum_b.end)
    for copy in backs:
        copy.wait()


LAGS = (1, 5, 8, 11, 14, 17)
BLOCK_US = 2.9
TURNS = (0, 2, 0)
SPOTS = dict(enumerate((23.2, 29.2, 32.2, 34.0, 35.7, 38.6, 40.3, 43.2, 44.9, 47.8, 49.5, 50.6, 52.8, 56.0), 8))
SPOTS[8.5] = 26.2
PAIRS_US = (36.8, 41.4, 46.0, 50.6)
STAGES_US = (2.0, 10.0, 8.0, 8.0, 7.0, 10.0)


def schedule():
    units = [(0, u, BLOCK_US * (u + 1)) for u in range(8)]
    units += [(2, 0, SPOTS[10])] + [(1, u, PAIRS_US[u]) for u in range(4)]
    plan, tail = {}, []
    for which, u, at in units:
        for stage, length in enumerate(STAGES_US):
            if which == 0 and u + LAGS[stage] < 8:
                at = BLOCK_US * (u + LAGS[stage] + 1)
                continue
            at = at + length
            spots = [k for k in sorted(SPOTS) if SPOTS[k] >= at - 0.3]
            if spots:
                plan.setdefault(spots[0], []).append((at, which, stage, u))
                at = max(at, SPOTS[spots[0]])
            else:
                tail.append((at, which, stage, u))
    tail += [(SPOTS[21] + 2.0 + 5.5 * stage, 3, stage, 0) for stage in range(4)]
    return {k: [e[1:] for e in sorted(v)] for k, v in plan.items()}, [e[1:] for e in sorted(tail)]


def sums_scratch(units, lanes):
    vmem = pltpu.VMEM
    return [
        vmem((units * 256, lanes), F32), vmem((units * 256, lanes), BF16), vmem((units * 256, lanes), BF16),
        vmem((units, 3, 64, lanes), BF16), vmem((units, 64, lanes), F32), vmem((units, 3, 16, lanes), F32),
        vmem((units, 4, 16, lanes), F32), vmem((units, 16, lanes), BF16),
        pltpu.SemaphoreType.DMA((units, 4, 3)), pltpu.SemaphoreType.DMA((units, 5)),
    ]


def block(*args):
    vm = pl.BlockSpec(memory_space=pltpu.VMEM)
    hbm = pl.BlockSpec(memory_space=pl.ANY)
    shape = jax.ShapeDtypeStruct
    dma = pltpu.SemaphoreType.DMA
    vmem = pltpu.VMEM
    field = vmem((TOK, D), BF16)
    field_t = vmem((D, TOK), BF16)
    wide = vmem((TOK, D), F32)
    rim = vmem((4 * PIECE, D), BF16)
    lat_rim = vmem((2 * BLOCK, D), BF16)
    return pl.pallas_call(
        block_kernel,
        out_shape=(
            shape((2 * FF, D), BF16),
            shape((4 * D, 384), BF16),
            shape((D, D), BF16),
            shape((8, D), F32),
            shape((TOK, D), BF16),
            shape((TOK, D), BF16),
            shape((8 * PIECE, D), BF16),
            shape((4 * BLOCK, D), BF16),
        ),
        in_specs=[hbm, hbm] + [vm] * 5 + [hbm] * 4 + [vm],
        out_specs=(hbm,) * 3 + (vm,) * 5,
        scratch_shapes=[
            vmem((D, 3 * D), BF16), vmem((D, D), BF16), vmem((D, FF), BF16), vmem((FF, D), BF16),
            lat_rim, lat_rim, rim, rim, rim, rim, vmem((TOK, 1), F32), vmem((64, WIN), F32),
            field, field, field, field, field, field_t, field_t, field,
            vmem((TOK, 3 * D), BF16), vmem((TOK, 3 * D), BF16), vmem((HALF + 2 * PIECE, D), BF16),
            wide, wide, wide,
            *sums_scratch(8, D), *sums_scratch(4, 384), *sums_scratch(1, D),
            vmem((8 * PIECE, D), BF16), vmem((4 * BLOCK, D), BF16), vmem((4, 4, 8, D), F32), vmem((8, D), F32),
            dma((17,)), dma((8,)), dma((8,)), dma((6,)), dma((6,)), dma((4, 3)), dma((4, 3)),
        ],
        compiler_params=pltpu.CompilerParams(collective_id=0, has_side_effects=True, vmem_limit_bytes=VMEM_BYTES),
        name="block",
    )(*args)


def finish_kernel(
    r1, r2, r3, gain_sums, out_win, gtok_win, lon_rims, lat_blocks, back,
    outputs, g_tok, g_qkv, g_out, g_up, g_down, g_gains,
    v1, v2, v3, w1, w2, rims, blocks, src, full, f_up, f_down, f_qkv, f_out, sem_in, sem_out,
):
    halves = [
        [(r1.at[pl.ds(core * FF + n * 1024, 1024)], v1.at[pl.ds(core * FF + n * 1024, 1024)]) for core in range(2)]
        for n in range(2)
    ]
    wanted = halves[0] + [(out_win, w1), (lon_rims, rims), (lat_blocks, blocks)] + halves[1]
    wanted += [(gtok_win, w2), (r2, v2), (r3, v3)]
    loads = [pltpu.make_async_copy(a, b, sem_in.at[k]) for k, (a, b) in enumerate(wanted)]
    for copy in loads:
        copy.start()
    stores = []

    def store(a, b):
        copy = pltpu.make_async_copy(a, b, sem_out.at[len(stores)])
        copy.start()
        stores.append(copy)

    def wide(n):
        for core in range(2):
            for k in range(2):
                lanes = slice(k * 256, (k + 1) * 256)
                at = core * FF + n * 256
                f_up[core * 256 + k * 128:core * 256 + (k + 1) * 128, n * 256:(n + 1) * 256] = (
                    v1[at:at + 128, lanes].astype(F32)
                )
                f_down[n * 256 + k * 128:n * 256 + (k + 1) * 128, core * 256:(core + 1) * 256] = (
                    v1[at + 128:at + 256, lanes].astype(F32)
                )
        if n % 2:
            cols = pl.ds((n - 1) * 256, 512)
            store(f_up.at[:, cols], g_up.at[:, cols])
            store(f_down.at[cols], g_down.at[cols])

    def field(k, win, out):
        for wr in range(2):
            at = (k * 2 + wr) * 2 * PIECE
            src[:HALF, :] = win[wr * HALF:(wr + 1) * HALF, :]
            src[HALF:, :] = rims[at:at + 2 * PIECE, :]
            for lev in range(2):
                if wr == 0:
                    pick, length = slice(lev * 288, (lev + 1) * 288), 288
                    to = lev * HALF + 144
                else:
                    pick, length = slice(lev * 288, lev * 288 + 144), 144
                    to = lev * HALF + 432
                full[k, to:to + length, :] = mm(back[pick, :], src[...]).astype(BF16)
        for lev in range(2):
            edge = mm(back[lev * 288 + BLOCK:(lev + 1) * 288, HALF:], src[HALF:, :])
            inner = blocks[(k * 2 + lev) * BLOCK:(k * 2 + lev + 1) * BLOCK, :].astype(F32)
            full[k, lev * HALF:lev * HALF + BLOCK, :] = (inner + edge).astype(BF16)
        store(full.at[k], out)

    g_gains[...] = gain_sums[0:2, :]
    for copy in loads[0:2]:
        copy.wait()
    for n in range(4):
        wide(n)
    for copy in loads[2:5]:
        copy.wait()
    field(0, w1, outputs)
    for copy in loads[5:7]:
        copy.wait()
    for n in range(4, 8):
        wide(n)
    loads[7].wait()
    field(1, w2, g_tok)
    loads[8].wait()
    for part in range(3):
        for pair in range(4):
            for core in range(2):
                f_qkv[core * 256:(core + 1) * 256, part * D + pair * 128:part * D + (pair + 1) * 128] = (
                    v2[core * 1024 + pair * 256:core * 1024 + (pair + 1) * 256, part * 128:(part + 1) * 128].astype(F32)
                )
        cols = pl.ds(part * D, D)
        store(f_qkv.at[:, cols], g_qkv.at[:, cols])
    loads[9].wait()
    f_out[...] = v3[...].astype(F32)
    store(f_out, g_out)
    for copy in stores:
        copy.wait()


def finish_all(*args):
    vm = pl.BlockSpec(memory_space=pltpu.VMEM)
    hbm = pl.BlockSpec(memory_space=pl.ANY)
    shape = jax.ShapeDtypeStruct
    vmem = pltpu.VMEM
    return pl.pallas_call(
        finish_kernel,
        out_shape=(
            shape((TOK, D), BF16),
            shape((TOK, D), BF16),
            shape((D, 3 * D), F32),
            shape((D, D), F32),
            shape((D, FF), F32),
            shape((FF, D), F32),
            shape((2, D), F32),
        ),
        in_specs=[hbm] * 3 + [vm] + [hbm] * 4 + [vm],
        out_specs=(hbm,) * 6 + (vm,),
        scratch_shapes=[
            vmem((2 * FF, D), BF16), vmem((4 * D, 384), BF16), vmem((D, D), BF16), vmem((TOK, D), BF16),
            vmem((TOK, D), BF16), vmem((8 * PIECE, D), BF16), vmem((4 * BLOCK, D), BF16),
            vmem((HALF + 2 * PIECE, D), BF16), vmem((2, TOK, D), BF16),
            vmem((D, FF), F32), vmem((FF, D), F32), vmem((D, 3 * D), F32), vmem((D, D), F32),
            pltpu.SemaphoreType.DMA((10,)), pltpu.SemaphoreType.DMA((14,)),
        ],
        compiler_params=pltpu.CompilerParams(vmem_limit_bytes=VMEM_BYTES),
        name="finish",
    )(*args)


def on_device(tokens, cotangent, valid, w_qkv, w_out, w_up, w_down, gains):
    into, back, rim_in, rim_back = gather_maps()
    tok = tokens.reshape(TOK, D)
    cot = cotangent.reshape(TOK, D)
    back_last = jnp.concatenate([back[BLOCK:2 * BLOCK, :HALF], back[3 * BLOCK:, :HALF]], 0)
    *sums, out_win, gtok_win, lon_rims, lat_blocks = block(
        tok, cot, rim_in, into, rim_back, back_last, valid, w_qkv, w_out, w_up, w_down, gains
    )
    outputs, g_tok, g_qkv, g_out, g_up, g_down, g_gains = finish_all(
        *sums, out_win, gtok_win, lon_rims, lat_blocks, back
    )
    return (
        outputs.reshape(tokens.shape),
        g_tok.reshape(tokens.shape),
        g_qkv,
        g_out,
        g_up,
        g_down,
        g_gains,
    )


def solution(mesh):
    field = P(None, "lat", "lon", None)
    in_specs = (field, field, P("lat", "lon"), P(), P(), P(), P(), P())
    out_specs = (field, field, P(), P(), P(), P(), P())
    return jax.shard_map(on_device, mesh=mesh, in_specs=in_specs, out_specs=out_specs, check_vma=False)
```

```python
import jax
import jax.numpy as jnp
import numpy as np
from jax import lax
from jax.experimental import pallas as pl
from jax.experimental.pallas import tpu as pltpu
from jax.sharding import PartitionSpec as P

F32 = jnp.float32
BF16 = jnp.bfloat16
MESH = pl.DeviceIdType.MESH
HEAD = 64
WIN = 144
TOK = 1152
HALF = 576
D = 512
FF = 2048
COLS = 24
BLOCK = 144
PIECE = 48
epsilon = 1e-05
LOW = -1e30
SCALE = np.float32(147456 ** (-0.5))
VMEM_BYTES = 63 * 1024 * 1024


def gather_maps():
    into = np.zeros((HALF, HALF + 2 * PIECE), np.float32)
    back = np.zeros((HALF, HALF + 2 * PIECE), np.float32)
    rim_in = np.zeros((4 * PIECE, TOK), np.float32)
    rim_back = np.zeros((2 * PIECE, HALF), np.float32)
    for lev in range(2):
        for half in range(2):
            for r in range(6):
                for col in range(COLS):
                    window = (col // 6) * WIN + lev * 72 + half * 36 + r * 6 + col % 6
                    chunk = (lev * 2 + half) * BLOCK + r * COLS
                    if col + 3 < COLS:
                        into[window, chunk + col + 3] = 1
                        back[chunk + col + 3, window] = 1
                    else:
                        rim = half * PIECE + lev * 18 + r * 3 + col + 3 - COLS
                        into[window, HALF + rim] = 1
                        back[chunk + col + 3 - COLS, HALF + rim] = 1
                        rim_back[rim, window] = 1
    for lev in range(2):
        for block in range(4):
            for r in range(6):
                for col in range(3):
                    rim_in[block * PIECE + lev * 18 + r * 3 + col, lev * HALF + block * BLOCK + r * COLS + col] = 1
    return [jnp.asarray(m, BF16) for m in (into, back, rim_in, rim_back)]


def mm(a, b):
    return lax.dot_general(a, b, (((1,), (0,)), ((), ())), preferred_element_type=F32)


def mm_nt(a, b):
    return lax.dot_general(a, b, (((1,), (1,)), ((), ())), preferred_element_type=F32)


def mm_tn(a, b):
    return lax.dot_general(a, b, (((0,), (0,)), ((), ())), preferred_element_type=F32)


def norm_stats(values):
    centred = values - jnp.mean(values, -1, keepdims=True)
    inv_std = lax.rsqrt(jnp.mean(centred * centred, -1, keepdims=True) + epsilon)
    return centred * inv_std, inv_std


def norm_back(grad_value, normed, inv_std, gain_row):
    scaled = grad_value * gain_row
    return inv_std * (
        scaled
        - jnp.mean(scaled, -1, keepdims=True)
        - normed * jnp.mean(scaled * normed, -1, keepdims=True)
    )


def rows_loop(total, step, body):
    def run(i, carry):
        body(pl.ds(pl.multiple_of(i * step, step), step))
        return carry

    lax.fori_loop(0, total // step, run, 0)


def window_bias(key_bias, split):
    rows = lax.broadcasted_iota(jnp.int32, (WIN, WIN), 0)
    cols = lax.broadcasted_iota(jnp.int32, (WIN, WIN), 1)
    bias = jnp.where(rows == cols, 0.0, jnp.broadcast_to(key_bias, (WIN, WIN)))
    apart = ((rows // 36) % 2) != ((cols // 36) % 2)
    return bias + jnp.where(apart, split, 0.0)


def scores_t(key2, query_m, bias):
    return mm_nt(key2, query_m) + bias


def head_masks():
    lane = lax.broadcasted_iota(jnp.int32, (WIN, 128), 1)
    return [lane < HEAD, lane >= HEAD]


def split_amount(window):
    last = (lax.axis_index("lat") == lax.axis_size("lat") - 1) & (window >= 4)
    return jnp.where(last, LOW, 0.0).astype(F32)


def position():
    lon, lat = lax.axis_index("lon"), lax.axis_index("lat")
    y = lax.rem(lax.div(lat, 2), 2) * 2 + lax.rem(lon, 2)
    return [lax.div(lon, 2), y, lax.div(lat, 4)], lax.rem(lat, 2)


def device_at(place, core):
    x, y, z = place
    return (x * 2 + lax.rem(y, 2), z * 4 + lax.div(y, 2) * 2 + core)


def remote(src, dst, s, r, device):
    return pltpu.make_async_remote_copy(
        src_ref=src, dst_ref=dst, send_sem=s, recv_sem=r, device_id=device, device_id_type=MESH
    )


def loop(first, last, body):
    def run(i, carry):
        body(i)
        return carry

    lax.fori_loop(first, last, run, 0)


class Sums:
    def __init__(self, turn, own, out, pair, recv1, sum1, recv2, recv3, fin, result, sems, pair_sems):
        self.turn = turn
        self.own, self.out, self.pair = own, out, pair
        self.recv1, self.sum1, self.recv2, self.recv3, self.fin = recv1, sum1, recv2, recv3, fin
        self.result, self.sems, self.pair_sems = result, sems, pair_sems
        self.place, self.core = position()
        self.partner = device_at(self.place, 1 - self.core)
        self.base = self.core * own.shape[0]

    def flags(self, u, level):
        turn = u + self.turn + level
        turn = turn % 3 if isinstance(u, int) else lax.rem(turn, 3)
        first, last = (2 - turn) // 2, turn // 2
        return first, 1 - first - last, last

    def peer(self, u, level, step):
        flags = self.flags(u, level)
        return device_at([lax.rem(at + flag * step, 4) for at, flag in zip(self.place, flags)], self.core)

    def mine(self, u, level):
        x, y, z = (at * flag for at, flag in zip(self.place, self.flags(u, level)))
        return x + y + z

    def rows(self, u):
        return pl.ds(pl.multiple_of(u * 256, 256), 256)

    def rows1(self, u, at):
        return pl.ds(pl.multiple_of(u * 256 + at * 64, 64), 64)

    def result_rows(self, u, level):
        at = self.base + u * 256
        if level < 0:
            return pl.ds(pl.multiple_of(at, 256), 256)
        at = at + self.mine(u, 0) * 64
        if level == 0:
            return pl.ds(pl.multiple_of(at, 64), 64)
        return pl.ds(pl.multiple_of(at + self.mine(u, 1) * 16, 16), 16)

    def down(self, u, level, step):
        s, r = self.sems.at[u, 0, level], self.sems.at[u, 1, level]
        device = self.peer(u, level, step)
        if level == 0:
            there = lax.rem(self.mine(u, 0) + step, 4)
            return remote(self.out.at[self.rows1(u, there)], self.recv1.at[u, step - 1], s, r, device)
        if level == 1:
            there = lax.rem(self.mine(u, 1) + step, 4)
            rows = pl.ds(pl.multiple_of(there * 16, 16), 16)
            return remote(self.sum1.at[u, rows], self.recv2.at[u, step - 1], s, r, device)
        slot = self.recv3.at[u, self.mine(u, 2)]
        return remote(slot, slot, s, r, device)

    def up(self, u, level, step):
        s, r = self.sems.at[u, 2, level], self.sems.at[u, 3, level]
        rows = self.result.at[self.result_rows(u, level)]
        return remote(self.fin.at[u] if level == 1 else rows, rows, s, r, self.peer(u, level, step))

    def hand(self, u):
        rows = self.rows(u)
        return remote(
            self.out.at[rows], self.pair.at[rows], self.pair_sems.at[u, 0], self.pair_sems.at[u, 1], self.partner
        )

    def hand_back(self, u):
        rows = self.result.at[self.result_rows(u, -1)]
        return remote(rows, rows, self.pair_sems.at[u, 2], self.pair_sems.at[u, 3], self.partner)

    def keep(self, u):
        return pltpu.make_async_copy(self.fin.at[u], self.result.at[self.result_rows(u, 1)], self.pair_sems.at[u, 4])

    def done(self, u, kind, level):
        if kind < 2:
            three = (self.recv1.at[u], self.recv2.at[u], self.recv3.at[u, pl.ds(0, 3)])[level]
        else:
            three = (self.recv1.at[u], self.recv1.at[u, 0, pl.ds(0, 48)])[level]
        pltpu.make_async_copy(three, three, self.sems.at[u, kind, level]).wait()

    def send(self, make, u, level):
        for step in (1, 2, 3):
            make(u, level, step).start()

    def begin(self, u):
        self.hand(u).wait()
        rows = self.rows(u)
        total = self.own[rows, :] + self.pair[rows, :].astype(F32)
        self.own[rows, :] = total
        self.out[rows, :] = total.astype(BF16)
        self.send(self.down, u, 0)

    def second(self, u):
        self.done(u, 1, 0)
        rows = self.rows1(u, self.mine(u, 0))
        self.sum1[u] = (self.own[rows, :] + self.recv1[u, 0].astype(F32)) + (
            self.recv1[u, 1].astype(F32) + self.recv1[u, 2].astype(F32)
        )
        self.send(self.down, u, 1)

    def third(self, u):
        self.done(u, 1, 1)
        rows = pl.ds(pl.multiple_of(self.mine(u, 1) * 16, 16), 16)
        self.recv3[u, self.mine(u, 2)] = (self.sum1[u, rows, :] + self.recv2[u, 0]) + (
            self.recv2[u, 1] + self.recv2[u, 2]
        )
        self.send(self.down, u, 2)

    def gather(self, u):
        self.done(u, 1, 2)
        total = (self.recv3[u, 0] + self.recv3[u, 1]) + (self.recv3[u, 2] + self.recv3[u, 3])
        self.fin[u] = (total * SCALE).astype(BF16)
        self.keep(u).start()
        self.send(self.up, u, 1)

    def gather_next(self, u):
        self.keep(u).wait()
        self.done(u, 3, 1)
        self.send(self.up, u, 0)

    def gather_pair(self, u):
        self.done(u, 3, 0)
        self.hand_back(u).start()

    def end(self, u):
        for level in range(3):
            self.done(u, 0, level)
        for level in range(2):
            self.done(u, 2, level)
        self.hand_back(u).wait()

    def stages(self):
        return (self.begin, self.second, self.third, self.gather, self.gather_next, self.gather_pair)


def block_kernel(
    tok, cot, rim_in, into, rim_back, back_last, valid, w_qkv_h, w_out_h, w_up_h, w_down_h, gains,
    r1, r2, r3, gains_out, out_win, gtok_win, lon_rims, lat_blocks,
    w_qkv, w_out, w_up, w_down, lat_t, lat_c, rim_t, rim_c, pack_t, pack_c, key_bias, log_sum,
    x_ref, c_ref, lowered, context, hid, hid_t, c_t, g_ctx, packed, g_pack, src, mixed, acc_out, acc_in,
    *rest_refs,
):
    place, core = position()
    lon, lat = lax.axis_index("lon"), lax.axis_index("lat")
    n_lon, n_lat = lax.axis_size("lon"), lax.axis_size("lat")
    lon_m, lon_p = lax.rem(lon + n_lon - 1, n_lon), lax.rem(lon + 1, n_lon)
    lat_m, lat_p = lax.rem(lat + n_lat - 1, n_lat), lax.rem(lat + 1, n_lat)
    partner = device_at(place, 1 - core)
    gain_a = gains[0:1, :]
    gain_b = gains[1:2, :]
    masks = head_masks()
    refs = iter(rest_refs)
    results = (r1, r2, r3)
    sum_a, sum_b, sum_c = (
        Sums(TURNS[k], *[next(refs) for _ in range(8)], results[k], next(refs), next(refs)) for k in range(3)
    )
    (rims, send_blocks, gain_slots, gain_part,
     load_sem, halo_s, halo_r, back_s, back_r, gain_s, gain_r) = refs

    def peer(axis, step):
        there = list(place)
        there[axis] = lax.rem(place[axis] + step, 4)
        return device_at(there, core)

    barrier = pltpu.get_barrier_semaphore()
    greet = [(lon, lat_m), (lon, lat_p), (lon_m, lat), (lon_p, lat), (lon_m, lat_m), (lon_p, lat_p), partner]
    greet += [peer(axis, step) for axis in range(3) for step in (1, 2, 3)]
    for device in greet:
        pl.semaphore_signal(barrier, inc=1, device_id=device, device_id_type=MESH)
    loads = [
        pltpu.make_async_copy(a, b, load_sem.at[k])
        for k, (a, b) in enumerate(
            ((tok, context), (cot, out_win), (w_out_h, w_out), (w_up_h, w_up), (w_down_h, w_down))
        )
    ]
    loads += [
        pltpu.make_async_copy(
            w_qkv_h.at[:, pl.ds(part * D + pair * 128, 128)],
            w_qkv.at[:, pl.ds(pair * 384 + part * 128, 128)],
            load_sem.at[5 + part * 4 + pair],
        )
        for part in range(3)
        for pair in range(4)
    ]
    for copy in loads:
        copy.start()
    loads[0].wait()
    pack_t[...] = mm(rim_in[...], context[...]).astype(BF16)
    pl.semaphore_wait(barrier, len(greet))

    halos = []
    rest = pl.ds(PIECE, 3 * PIECE)
    corner = pl.ds(0, PIECE)

    def send_halos(pack, rim, lat_rim, full):
        wanted = [
            (pack.at[rest], rim.at[rest], (lon_m, lat)),
            (pack.at[corner], rim.at[corner], (lon_m, lat_m)),
        ]
        for lev in range(2):
            wanted.append(
                (full.at[pl.ds(lev * HALF, BLOCK)], lat_rim.at[pl.ds(lev * BLOCK, BLOCK)], (lon, lat_m))
            )
        for a, b, device in wanted:
            k = len(halos)
            halos.append(remote(a, b, halo_s.at[k], halo_r.at[k], device))
            halos[k].start()

    send_halos(pack_t, rim_t, lat_t, context)
    usable = jnp.where(valid[...] == 1, 1.0, 0.0).astype(BF16)
    spot = lax.broadcasted_iota(jnp.int32, (WIN, COLS), 0)
    lane = lax.broadcasted_iota(jnp.int32, (WIN, COLS), 1)
    for wr in range(2):
        lat_at = wr * 12 + ((spot // 36) % 2) * 6 + (spot // 6) % 6
        picked = mm(jnp.where(lane == lat_at, 1.0, 0.0).astype(BF16), usable)
        for k in range(4):
            ok = jnp.sum(jnp.where(lane == 6 * k + spot % 6, picked, 0.0), 1, keepdims=True)
            key_bias[(wr * 4 + k) * WIN:(wr * 4 + k + 1) * WIN, :] = jnp.where(ok > 0.5, 0.0, LOW)

    def own_rows(full, wr):
        for lev in range(2):
            if wr == 0:
                src[lev * 288:(lev + 1) * 288, :] = full[lev * HALF + 144:lev * HALF + 432, :]
            else:
                src[lev * 288:lev * 288 + 144, :] = full[lev * HALF + 432:lev * HALF + 576, :]

    def rim_rows(lat_rim, rim, wr):
        if wr == 0:
            src[HALF:, :] = rim[PIECE:3 * PIECE, :]
        else:
            for lev in range(2):
                src[lev * 288 + 144:(lev + 1) * 288, :] = lat_rim[lev * BLOCK:(lev + 1) * BLOCK, :]
            src[HALF:HALF + PIECE, :] = rim[3 * PIECE:, :]
            src[HALF + PIECE:, :] = rim[:PIECE, :]

    def enter(dst, wr, first, last, depth):
        for n in range(2):
            cols = slice(n * 256, (n + 1) * 256)
            dst[wr * HALF + first:wr * HALF + last, cols] = mm(into[first:last, :depth], src[:depth, cols]).astype(BF16)

    def attend(w):
        rows = pl.ds(pl.multiple_of(w * WIN, WIN), WIN)
        bias = window_bias(key_bias[rows, :], split_amount(w))
        for pair in range(4):
            lanes = slice(pair * 128, (pair + 1) * 128)
            query, key, value = (packed[rows, pair * 384 + k * 128:pair * 384 + (k + 1) * 128] for k in range(3))
            total = None
            for half, mask in enumerate(masks):
                scores = scores_t(key, jnp.where(mask, query, 0), bias)
                largest = jnp.max(scores, 0, keepdims=True)
                probs = jnp.exp(scores - largest)
                total_e = jnp.sum(probs, 0, keepdims=True)
                probs = probs * (1.0 / total_e)
                log_sum[pl.ds(w * 8 + pair * 2 + half, 1), :] = largest + jnp.log(total_e)
                part = mm_tn(probs.astype(BF16), jnp.where(mask, value, 0))
                total = part if total is None else total + part
            hid[rows, lanes] = total.astype(BF16)

    def first_part(first, last):
        band = slice(first * WIN, last * WIN)

        normed, _ = norm_stats(x_ref[band, :].astype(F32))
        lowered[band, :] = (normed * gain_a).astype(BF16)

        def project(n):
            cols = pl.ds(pl.multiple_of(n * 256, 256), 256)
            lane = n * 256 + lax.broadcasted_iota(jnp.int32, (1, 256), 1)
            factor = jnp.where(lax.rem(lane, 384) < 128, HEAD ** (-0.5), 1.0)
            packed[band, cols] = (mm(lowered[band, :], w_qkv[:, cols]) * factor).astype(BF16)

        loop(0, 6, project)
        loop(first, last, attend)

    own_rows(context, 0)
    enter(x_ref, 0, 0, 3 * WIN, HALF)
    for copy in loads[5:]:
        copy.wait()
    first_part(0, 3)
    loads[1].wait()
    pack_c[...] = mm(rim_in[...], out_win[...]).astype(BF16)
    send_halos(pack_c, rim_c, lat_c, out_win)
    for copy in halos[0:4]:
        copy.wait_recv()
    rim_rows(lat_t, rim_t, 0)
    enter(x_ref, 0, 3 * WIN, HALF, HALF + 2 * PIECE)
    own_rows(context, 1)
    rim_rows(lat_t, rim_t, 1)
    enter(x_ref, 1, 0, HALF, HALF + 2 * PIECE)
    first_part(3, 8)
    for copy in halos[4:8]:
        copy.wait_recv()
    for wr in range(2):
        own_rows(out_win, wr)
        rim_rows(lat_c, rim_c, wr)
        enter(c_ref, wr, 0, HALF, HALF + 2 * PIECE)
    for copy in halos:
        copy.wait_send()
    loads[2].wait()
    context[...] = hid[...]

    def second_norm(rows):
        attended = mm(context[rows, :], w_out[...]).astype(BF16)
        m = x_ref[rows, :].astype(F32) + attended.astype(F32)
        mixed[rows, :] = m
        normed, _ = norm_stats(m)
        hid[rows, :] = (normed * gain_b).astype(BF16)

    rows_loop(TOK, 576, second_norm)
    hid_t[...] = hid[...].T
    c_t[...] = c_ref[...].T
    acc_out[...] = jnp.zeros_like(acc_out)
    acc_in[...] = jnp.zeros_like(acc_in)
    loads[3].wait()
    loads[4].wait()

    def tick(n):
        for stage, lag in reversed(list(zip(sum_a.stages(), LAGS))):
            @pl.when(n >= lag)
            def _(stage=stage, lag=lag):
                stage(n - lag)

    plan, tail = schedule()
    all_sums = (sum_a, sum_b, sum_c)

    def due(spot):
        for which, stage, u in plan.get(spot, ()):
            all_sums[which].stages()[stage](u)

    def share(left, right, flip, own, out, at):
        rows = pl.ds(pl.multiple_of(at, 128), 128)
        for which, dst in ((core, own), (1 - core, out)):
            part = mm(left[pl.ds(pl.multiple_of(which * 256, 256), 256), :], right)
            if flip:
                part = part.T
            part = part.astype(dst.dtype)
            dst[rows, 0:256] = part[0:128]
            dst[rows, 256:512] = part[128:256]

    wide = 256

    def columns(n):
        cols = pl.ds(pl.multiple_of(n * wide, wide), wide)
        raised = mm(hid[...], w_up[:, cols])
        slope = np.float32(np.sqrt(2 / np.pi))
        square = raised * raised
        t = jnp.tanh(slope * (raised + np.float32(0.044715) * (square * raised)))
        cdf = 0.5 * (1.0 + t)
        activated = (raised * cdf).astype(BF16)
        deriv = cdf + 0.5 * raised * (1.0 - t * t) * (slope * (1.0 + np.float32(3 * 0.044715) * square))
        grad_act = mm_nt(c_ref[...], w_down[cols, :])
        grad_raised = (grad_act * deriv).astype(BF16)
        acc_out[...] += mm(activated, w_down[cols, :])
        acc_in[...] += mm_nt(grad_raised, w_up[:, cols])
        share(hid_t, grad_raised, False, sum_a.own, sum_a.out, n * 256)
        share(c_t, activated, True, sum_a.own, sum_a.out, n * 256 + 128)
        sum_a.hand(n).start()
        tick(n)

    loop(0, FF // wide, columns)
    due(8)
    gain_part[...] = jnp.zeros_like(gain_part)

    def finish(rows):
        m = mixed[rows, :]
        out_win[rows, :] = (m + acc_out[rows, :]).astype(BF16)
        normed, inv_std = norm_stats(m)
        grad_in = acc_in[rows, :]
        gain_part[1:2, :] += jnp.sum(grad_in * normed, 0, keepdims=True)
        g = c_ref[rows, :].astype(F32) + norm_back(grad_in, normed, inv_std, gain_b)
        acc_in[rows, :] = g
        g = g.astype(BF16)
        hid[rows, :] = g
        g_ctx[rows, :] = mm_nt(g, w_out[...]).astype(BF16)

    rows_loop(TOK // 2, 576, finish)
    due(8.5)
    rows_loop(TOK // 2, 576, lambda rows: finish(pl.ds(pl.multiple_of(rows.start + TOK // 2, 576), 576)))
    backs = []

    def send_back(k, win):
        for wr in range(2):
            at = (k * 2 + wr) * 2 * PIECE
            rims[at:at + 2 * PIECE, :] = mm(rim_back[...], win[wr * HALF:(wr + 1) * HALF, :]).astype(BF16)
        send_blocks[k * 2 * BLOCK:(k + 1) * 2 * BLOCK, :] = mm(back_last[...], win[HALF:, :]).astype(BF16)
        near = pl.ds(k * 4 * PIECE, 3 * PIECE)
        far = pl.ds(k * 4 * PIECE + 3 * PIECE, PIECE)
        blocks = pl.ds(k * 2 * BLOCK, 2 * BLOCK)
        for a, b, device in (
            (send_blocks.at[blocks], lat_blocks.at[blocks], (lon, lat_p)),
            (rims.at[near], lon_rims.at[near], (lon_p, lat)),
            (rims.at[far], lon_rims.at[far], (lon_p, lat_p)),
        ):
            n = len(backs)
            backs.append(remote(a, b, back_s.at[n], back_r.at[n], device))
            backs[n].start()

    send_back(0, out_win)
    gmix, g_att = acc_in, hid

    due(9)
    hid_t[...] = lowered[...].T
    c_t[...] = context[...].T
    for which, dst in ((core, sum_c.own), (1 - core, sum_c.out)):
        part = mm(c_t[pl.ds(pl.multiple_of(which * 256, 256), 256), :], g_att[...])
        dst[...] = part.astype(dst.dtype)
    sum_c.hand(0).start()
    due(10)

    def attend_back(w, pair):
        rows = pl.ds(pl.multiple_of(w * WIN, WIN), WIN)
        bias = window_bias(key_bias[rows, :], split_amount(w))
        lanes = [pl.ds(pl.multiple_of(pair * 384 + k * 128, 128), 128) for k in range(3)]
        query, key, value = (packed[rows, at] for at in lanes)
        grad = g_ctx[rows, pl.ds(pl.multiple_of(pair * 128, 128), 128)]
        sums = [None, None, None]
        for half, mask in enumerate(masks):
            query_m = jnp.where(mask, query, 0)
            grad_m = jnp.where(mask, grad, 0)
            probs = jnp.exp(scores_t(key, query_m, bias) - log_sum[pl.ds(w * 8 + pair * 2 + half, 1), :])
            g_weights = mm_nt(value, grad_m)
            inner = jnp.sum(probs * g_weights, 0, keepdims=True)
            g_scores = (probs * (g_weights - inner)).astype(BF16)
            parts = (
                mm_tn(g_scores, jnp.where(mask, key, 0)),
                mm(g_scores, query_m),
                mm(probs.astype(BF16), grad_m),
            )
            sums = [b if a is None else a + b for a, b in zip(sums, parts)]
        sums[0] = sums[0] * HEAD ** (-0.5)
        for at, value in zip(lanes, sums):
            g_pack[rows, at] = value.astype(BF16)

    def heads(pair):
        def some(k):
            for w in range(4):
                attend_back(k * 4 + w, pair)
            for spot in range(11, 19):
                if spot in plan:
                    @pl.when(2 * pair + k == spot - 11)
                    def _(spot=spot):
                        due(spot)

        loop(0, 2, some)
        cols = pl.ds(pl.multiple_of(pair * 384, 384), 384)
        rows = pl.ds(pl.multiple_of(pair * 256, 256), 256)
        for which, dst in ((1 - core, sum_b.out), (core, sum_b.own)):
            part = mm(hid_t[pl.ds(pl.multiple_of(which * 256, 256), 256), :], g_pack[:, cols])
            dst[rows, :] = part.astype(dst.dtype)
            if dst is sum_b.out:
                sum_b.hand(pair).start()

    loop(0, 4, heads)
    due(19)

    def finish_back(rows):
        g_low = mm_nt(g_pack[rows, :], w_qkv[...]).astype(BF16).astype(F32)
        normed, inv_std = norm_stats(x_ref[rows, :].astype(F32))
        gain_part[0:1, :] += jnp.sum(g_low * normed, 0, keepdims=True)
        gtok_win[rows, :] = (gmix[rows, :] + norm_back(g_low, normed, inv_std, gain_a)).astype(BF16)

    rows_loop(TOK // 2, 576, finish_back)
    due(20)
    rows_loop(TOK // 2, 576, lambda rows: finish_back(pl.ds(pl.multiple_of(rows.start + TOK // 2, 576), 576)))
    send_back(1, gtok_win)
    gain_slots[0, 0] = gain_part[...]
    gain_pair = remote(gain_slots.at[0, 0], gain_slots.at[0, 1], gain_s.at[0, 0], gain_r.at[0, 0], partner)
    gain_pair.start()
    due(21)

    def gains_along(level, total):
        axis = level - 1
        slot = gain_slots.at[level, place[axis]]
        gain_slots[level, place[axis]] = total
        copies = [
            remote(slot, slot, gain_s.at[level, step - 1], gain_r.at[level, step - 1], peer(axis, step))
            for step in (1, 2, 3)
        ]
        for copy in copies:
            copy.start()
        return copies

    def gains_sum(level, copies):
        for copy in copies:
            copy.wait()
        return (gain_slots[level, 0] + gain_slots[level, 1]) + (gain_slots[level, 2] + gain_slots[level, 3])

    gain_copies = []
    for which, stage, u in tail:
        if which < 3:
            all_sums[which].stages()[stage](u)
        elif stage == 0:
            gain_pair.wait()
            gain_copies = gains_along(1, gain_slots[0, 0] + gain_slots[0, 1])
        elif stage < 3:
            gain_copies = gains_along(stage + 1, gains_sum(stage, gain_copies))
        else:
            gains_out[...] = gains_sum(3, gain_copies) * SCALE
    loop(0, 8, sum_a.end)
    sum_c.end(0)
    loop(0, 4, sum_b.end)
    for copy in backs:
        copy.wait()


LAGS = (1, 5, 8, 11, 14, 17)
BLOCK_US = 2.9
TURNS = (0, 2, 0)
SPOTS = dict(enumerate((23.2, 27.2, 30.2, 32.0, 33.7, 36.6, 38.3, 41.2, 42.9, 45.8, 47.5, 48.6, 50.6, 53.5), 8))
SPOTS[8.5] = 25.0
PAIRS_US = (34.8, 39.4, 44.0, 48.6)
STAGES_US = (2.0, 10.0, 8.0, 8.0, 7.0, 10.0)


def schedule():
    units = [(0, u, BLOCK_US * (u + 1)) for u in range(8)]
    units += [(2, 0, SPOTS[10])] + [(1, u, PAIRS_US[u]) for u in range(4)]
    plan, tail = {}, []
    for which, u, at in units:
        for stage, length in enumerate(STAGES_US):
            if which == 0 and u + LAGS[stage] < 8:
                at = BLOCK_US * (u + LAGS[stage] + 1)
                continue
            at = at + length
            spots = [k for k in sorted(SPOTS) if SPOTS[k] >= at - 0.3]
            if spots:
                plan.setdefault(spots[0], []).append((at, which, stage, u))
                at = max(at, SPOTS[spots[0]])
            else:
                tail.append((at, which, stage, u))
    tail += [(SPOTS[21] + 2.0 + 5.5 * stage, 3, stage, 0) for stage in range(4)]
    return {k: [e[1:] for e in sorted(v)] for k, v in plan.items()}, [e[1:] for e in sorted(tail)]


def sums_scratch(units, lanes):
    vmem = pltpu.VMEM
    return [
        vmem((units * 256, lanes), F32), vmem((units * 256, lanes), BF16), vmem((units * 256, lanes), BF16),
        vmem((units, 3, 64, lanes), BF16), vmem((units, 64, lanes), F32), vmem((units, 3, 16, lanes), F32),
        vmem((units, 4, 16, lanes), F32), vmem((units, 16, lanes), BF16),
        pltpu.SemaphoreType.DMA((units, 4, 3)), pltpu.SemaphoreType.DMA((units, 5)),
    ]


def block(*args):
    vm = pl.BlockSpec(memory_space=pltpu.VMEM)
    hbm = pl.BlockSpec(memory_space=pl.ANY)
    shape = jax.ShapeDtypeStruct
    dma = pltpu.SemaphoreType.DMA
    vmem = pltpu.VMEM
    field = vmem((TOK, D), BF16)
    field_t = vmem((D, TOK), BF16)
    wide = vmem((TOK, D), F32)
    rim = vmem((4 * PIECE, D), BF16)
    lat_rim = vmem((2 * BLOCK, D), BF16)
    return pl.pallas_call(
        block_kernel,
        out_shape=(
            shape((2 * FF, D), BF16),
            shape((4 * D, 384), BF16),
            shape((D, D), BF16),
            shape((8, D), F32),
            shape((TOK, D), BF16),
            shape((TOK, D), BF16),
            shape((8 * PIECE, D), BF16),
            shape((4 * BLOCK, D), BF16),
        ),
        in_specs=[hbm, hbm] + [vm] * 5 + [hbm] * 4 + [vm],
        out_specs=(hbm,) * 3 + (vm,) * 5,
        scratch_shapes=[
            vmem((D, 3 * D), BF16), vmem((D, D), BF16), vmem((D, FF), BF16), vmem((FF, D), BF16),
            lat_rim, lat_rim, rim, rim, rim, rim, vmem((TOK, 1), F32), vmem((64, WIN), F32),
            field, field, field, field, field, field_t, field_t, field,
            vmem((TOK, 3 * D), BF16), vmem((TOK, 3 * D), BF16), vmem((HALF + 2 * PIECE, D), BF16),
            wide, wide, wide,
            *sums_scratch(8, D), *sums_scratch(4, 384), *sums_scratch(1, D),
            vmem((8 * PIECE, D), BF16), vmem((4 * BLOCK, D), BF16), vmem((4, 4, 8, D), F32), vmem((8, D), F32),
            dma((17,)), dma((8,)), dma((8,)), dma((6,)), dma((6,)), dma((4, 3)), dma((4, 3)),
        ],
        compiler_params=pltpu.CompilerParams(collective_id=0, has_side_effects=True, vmem_limit_bytes=VMEM_BYTES),
        name="block",
    )(*args)


def finish_kernel(
    r1, r2, r3, gain_sums, out_win, gtok_win, lon_rims, lat_blocks, back,
    outputs, g_tok, g_qkv, g_out, g_up, g_down, g_gains,
    v1, v2, v3, w1, w2, rims, blocks, src, full, f_up, f_down, f_qkv, f_out, sem_in, sem_out,
):
    halves = [
        [(r1.at[pl.ds(core * FF + n * 1024, 1024)], v1.at[pl.ds(core * FF + n * 1024, 1024)]) for core in range(2)]
        for n in range(2)
    ]
    wanted = halves[0] + [(out_win, w1), (lon_rims, rims), (lat_blocks, blocks)] + halves[1]
    wanted += [(gtok_win, w2), (r2, v2), (r3, v3)]
    loads = [pltpu.make_async_copy(a, b, sem_in.at[k]) for k, (a, b) in enumerate(wanted)]
    for copy in loads:
        copy.start()
    stores = []

    def store(a, b):
        copy = pltpu.make_async_copy(a, b, sem_out.at[len(stores)])
        copy.start()
        stores.append(copy)

    def wide(n):
        for core in range(2):
            for k in range(2):
                lanes = slice(k * 256, (k + 1) * 256)
                at = core * FF + n * 256
                f_up[core * 256 + k * 128:core * 256 + (k + 1) * 128, n * 256:(n + 1) * 256] = (
                    v1[at:at + 128, lanes].astype(F32)
                )
                f_down[n * 256 + k * 128:n * 256 + (k + 1) * 128, core * 256:(core + 1) * 256] = (
                    v1[at + 128:at + 256, lanes].astype(F32)
                )
        if n % 2:
            cols = pl.ds((n - 1) * 256, 512)
            store(f_up.at[:, cols], g_up.at[:, cols])
            store(f_down.at[cols], g_down.at[cols])

    def field(k, win, out):
        for wr in range(2):
            at = (k * 2 + wr) * 2 * PIECE
            src[:HALF, :] = win[wr * HALF:(wr + 1) * HALF, :]
            src[HALF:, :] = rims[at:at + 2 * PIECE, :]
            for lev in range(2):
                if wr == 0:
                    pick, length = slice(lev * 288, (lev + 1) * 288), 288
                    to = lev * HALF + 144
                else:
                    pick, length = slice(lev * 288, lev * 288 + 144), 144
                    to = lev * HALF + 432
                full[k, to:to + length, :] = mm(back[pick, :], src[...]).astype(BF16)
        for lev in range(2):
            edge = mm(back[lev * 288 + BLOCK:(lev + 1) * 288, HALF:], src[HALF:, :])
            inner = blocks[(k * 2 + lev) * BLOCK:(k * 2 + lev + 1) * BLOCK, :].astype(F32)
            full[k, lev * HALF:lev * HALF + BLOCK, :] = (inner + edge).astype(BF16)
        store(full.at[k], out)

    g_gains[...] = gain_sums[0:2, :]
    for copy in loads[0:2]:
        copy.wait()
    for n in range(4):
        wide(n)
    for copy in loads[2:5]:
        copy.wait()
    field(0, w1, outputs)
    for copy in loads[5:7]:
        copy.wait()
    for n in range(4, 8):
        wide(n)
    loads[7].wait()
    field(1, w2, g_tok)
    loads[8].wait()
    for part in range(3):
        for pair in range(4):
            for core in range(2):
                f_qkv[core * 256:(core + 1) * 256, part * D + pair * 128:part * D + (pair + 1) * 128] = (
                    v2[core * 1024 + pair * 256:core * 1024 + (pair + 1) * 256, part * 128:(part + 1) * 128].astype(F32)
                )
        cols = pl.ds(part * D, D)
        store(f_qkv.at[:, cols], g_qkv.at[:, cols])
    loads[9].wait()
    f_out[...] = v3[...].astype(F32)
    store(f_out, g_out)
    for copy in stores:
        copy.wait()


def finish_all(*args):
    vm = pl.BlockSpec(memory_space=pltpu.VMEM)
    hbm = pl.BlockSpec(memory_space=pl.ANY)
    shape = jax.ShapeDtypeStruct
    vmem = pltpu.VMEM
    return pl.pallas_call(
        finish_kernel,
        out_shape=(
            shape((TOK, D), BF16),
            shape((TOK, D), BF16),
            shape((D, 3 * D), F32),
            shape((D, D), F32),
            shape((D, FF), F32),
            shape((FF, D), F32),
            shape((2, D), F32),
        ),
        in_specs=[hbm] * 3 + [vm] + [hbm] * 4 + [vm],
        out_specs=(hbm,) * 6 + (vm,),
        scratch_shapes=[
            vmem((2 * FF, D), BF16), vmem((4 * D, 384), BF16), vmem((D, D), BF16), vmem((TOK, D), BF16),
            vmem((TOK, D), BF16), vmem((8 * PIECE, D), BF16), vmem((4 * BLOCK, D), BF16),
            vmem((HALF + 2 * PIECE, D), BF16), vmem((2, TOK, D), BF16),
            vmem((D, FF), F32), vmem((FF, D), F32), vmem((D, 3 * D), F32), vmem((D, D), F32),
            pltpu.SemaphoreType.DMA((10,)), pltpu.SemaphoreType.DMA((14,)),
        ],
        compiler_params=pltpu.CompilerParams(vmem_limit_bytes=VMEM_BYTES),
        name="finish",
    )(*args)


def on_device(tokens, cotangent, valid, w_qkv, w_out, w_up, w_down, gains):
    into, back, rim_in, rim_back = gather_maps()
    tok = tokens.reshape(TOK, D)
    cot = cotangent.reshape(TOK, D)
    back_last = jnp.concatenate([back[BLOCK:2 * BLOCK, :HALF], back[3 * BLOCK:, :HALF]], 0)
    *sums, out_win, gtok_win, lon_rims, lat_blocks = block(
        tok, cot, rim_in, into, rim_back, back_last, valid, w_qkv, w_out, w_up, w_down, gains
    )
    outputs, g_tok, g_qkv, g_out, g_up, g_down, g_gains = finish_all(
        *sums, out_win, gtok_win, lon_rims, lat_blocks, back
    )
    return (
        outputs.reshape(tokens.shape),
        g_tok.reshape(tokens.shape),
        g_qkv,
        g_out,
        g_up,
        g_down,
        g_gains,
    )


def solution(mesh):
    field = P(None, "lat", "lon", None)
    in_specs = (field, field, P("lat", "lon"), P(), P(), P(), P(), P())
    out_specs = (field, field, P(), P(), P(), P(), P())
    return jax.shard_map(on_device, mesh=mesh, in_specs=in_specs, out_specs=out_specs, check_vma=False)
```
